256 devices in a mesh: ctx: 32 (over y, z_hi, core), tp: 8 (over x, z_lo).
Axes of the slice: x: 4, y: 4, z: 8 (z_hi: 4, z_lo: 2; z = z_hi * 2 + z_lo), core: 2. Of those that a mesh axis runs over, the one named last changes fastest.
Arguments:
- projections: bfloat16 [32768, 3, 1024], P('ctx', None, 'tp'), may hold values from -71 to 71
- short_filter: float32 [3, 3, 1024], P(None, None, 'tp'), may hold values from -3.5 to 3.5
- residues: float32 [16, 1024], P(None, 'tp'), may hold values from -1.5 to 1.5
- decays: float32 [16, 1024], P(None, 'tp'), may hold values from 1.5258789e-05 to 0.05
- skip: float32 [1024], P('tp'), may hold values from -3 to 3
- gain: float32 [1024], P('tp'), may hold values from 0.5 to 1.5
Outputs:
- mixed: bfloat16 [32768, 1024], P('ctx', 'tp')
The draws below stay inside these ranges and needn't reach their ends.
All inputs are finite; a program needn't handle non-finite values.
Results may differ from the reference program's by a relative error of at most 0.009.
Values may be sent and summed in bfloat16 or wider, within the bound.
No kernel may reach another device: no remote copies, remote signals or barrier semaphores. Data moves between devices by JAX's collectives and lax.ppermute only.
A program may use at most 64 MiB of HBM per device.

```python
import math
import jax
import jax.numpy as jnp
from jax import lax

TAPS = 3
MODES = 16
TOKENS = 32768
SLAB = 1024


def draw_projections(key, part):
    key = jax.random.fold_in(key, 11)
    first_key, second_key, third_key = jax.random.split(key, 3)
    values = jnp.clip(jax.random.normal(first_key, (TOKENS, 3, SLAB), jnp.float32), -5.0, 5.0)
    spread = 5.0
    rough = jax.random.uniform(second_key, (SLAB,), jnp.float32, 0.7, 1.4)
    ramp = jnp.exp(jnp.log(spread) * jnp.arange(SLAB, dtype=jnp.float32) / (SLAB - 1)) * rough
    token_scale = jnp.exp(jax.random.uniform(third_key, (TOKENS,), jnp.float32, -0.69, 0.69))
    stream = jnp.arange(3)[None, :, None]
    lift = jnp.where(stream == 0, token_scale[:, None, None] * ramp[None, None, :], 1.0)
    return (values * lift).astype(jnp.bfloat16)


def block_scale(key, shape, shards, smallest, top_value):
    loudness, own = 1.0, jax.random.fold_in(key, 6)
    for position, parts in shards:
        draws = jnp.exp(jax.random.uniform(jax.random.fold_in(own, position), (parts,), jnp.float32, smallest / len(shards), top_value / len(shards)))
        loudness = loudness * jnp.repeat(draws, shape[position] // parts).reshape([-1 if axis == position else 1 for axis in range(len(shape))])
    return loudness


def scatter_about(own_key, extent, width, reach, cuts=(), kind=jnp.bfloat16):
    entries = width * jax.random.normal(own_key, extent, jnp.float32)
    if cuts:
        entries = entries * block_scale(own_key, extent, cuts, -0.22, 0.18)
    return jnp.clip(entries, -reach, reach).astype(kind)


def setup_inputs(seed: int = 0) -> dict:
    key_of = jax.random.split(jax.random.key(seed), 7)
    return {
        "projections": draw_projections(jax.random.fold_in(key_of[6], 71), 0),
        "short_filter": scatter_about(key_of[1], (3, TAPS, SLAB), TAPS ** -0.5, 3.5, ((2, 8),), jnp.float32),
        "residues": scatter_about(key_of[2], (MODES, SLAB), 0.25, 1.5, ((1, 8),), jnp.float32),
        "decays": jnp.clip(jnp.exp(math.log(0.05) - 8.094623 * jax.random.uniform(key_of[3], (MODES, SLAB), jnp.float32) ** block_scale(key_of[3], (MODES, SLAB), ((1, 8),), -0.2, 0.2)), 1.52587890625e-05, 0.05),
        "skip": scatter_about(key_of[4], (SLAB,), 1.0, 3.0, ((0, 8),), jnp.float32),
        "gain": jnp.clip(1.0 + 0.1 * jax.random.normal(key_of[5], (SLAB,), jnp.float32), 0.5, 1.5),
    }


def reference(projections, short_filter, residues, decays, skip, gain):
    values = projections.astype(jnp.float32)
    tap_count = short_filter.shape[1]
    padded = jnp.pad(values, ((tap_count - 1, 0), (0, 0), (0, 0)))
    filtered = jnp.zeros_like(values)
    for offset in range(tap_count):
        column_start = tap_count - 1 - offset
        filtered = filtered + short_filter[:, offset, :][None] * padded[column_start:column_start + TOKENS]
    product = filtered[:, 1, :] * filtered[:, 2, :]
    positions = jnp.arange(TOKENS, dtype=jnp.float32)[:, None]
    response = jnp.zeros((TOKENS, SLAB), jnp.float32)
    for mode_index in range(MODES):
        decay_rate = decays[mode_index][None, :]
        response = response + residues[mode_index][None, :] * jnp.sqrt(2.0 * decay_rate) * jnp.exp(-decay_rate * positions)
    pieces = []
    for column_start in range(0, SLAB, 128):
        column_end = min(column_start + 128, SLAB)
        spectrum = jnp.fft.rfft(product[:, column_start:column_end], 2 * TOKENS, axis=0)
        spectrum = spectrum * jnp.fft.rfft(response[:, column_start:column_end], 2 * TOKENS, axis=0)
        pieces.append(jnp.fft.irfft(spectrum, 2 * TOKENS, axis=0)[:TOKENS])
    convolved = jnp.concatenate(pieces, 1)
    gated_out = filtered[:, 0, :] * (convolved + skip[None, :] * product)
    mean_square = lax.optimization_barrier(jnp.mean(gated_out * gated_out, axis=1, keepdims=True))
    return (gain[None, :] * gated_out * lax.rsqrt(mean_square + 1e-05)).astype(jnp.bfloat16)
```

```python
import functools

import jax
import jax.numpy as jnp
from jax import lax
from jax.experimental import pallas as pl
from jax.experimental.pallas import tpu as pltpu
from jax.sharding import PartitionSpec as P

F32 = jnp.float32
BF16 = jnp.bfloat16
CHUNKS = 8
LANES = 128
VMEM_LIMIT = 32 * 1024 * 1024
VMEM = pl.BlockSpec(memory_space=pltpu.VMEM)

LAST = 0
FIRST = 6
EXTRA = 16


def over_sublanes(row):
    return jnp.broadcast_to(row, (CHUNKS, LANES))


def sublane_index():
    return lax.broadcasted_iota(jnp.int32, (CHUNKS, LANES), 0)


def next_chunk(block, distance=1):
    rolled = pltpu.roll(block, distance, 0)
    return jnp.where(sublane_index() >= distance, rolled, 0.0)


def strided(ref, step, run):
    return ref[pl.ds(step, CHUNKS, stride=run), :]


def added(terms):
    while len(terms) > 1:
        pairs = [terms[i] + terms[i + 1] for i in range(0, len(terms) - 1, 2)]
        terms = pairs + terms[2 * len(pairs) :]
    return terms[0]


def states_kernel(modes, x_ref, taps_ref, decays_ref, sent_ref, product_ref, state_ref, k_ref, v_ref, rows_ref):
    positions = x_ref.shape[1]
    run = positions // CHUNKS
    k_ref[...] = x_ref[1].astype(F32)
    v_ref[...] = x_ref[2].astype(F32)
    k_taps = [over_sublanes(taps_ref[1, i : i + 1, :]) for i in range(3)]
    v_taps = [over_sublanes(taps_ref[2, i : i + 1, :]) for i in range(3)]
    factors = [over_sublanes(jnp.exp(-decays_ref[m : m + 1, :])) for m in range(modes)]

    def step(j, carry):
        k1, k2, v1, v2, states = carry
        k0 = strided(k_ref, j, run)
        v0 = strided(v_ref, j, run)
        k = k_taps[0] * k0 + k_taps[1] * k1 + k_taps[2] * k2
        v = v_taps[0] * v0 + v_taps[1] * v1 + v_taps[2] * v2
        product = k * v
        product_ref[j] = product
        states = tuple(a * h + product for a, h in zip(factors, states))
        return k0, k1, v0, v1, states

    start = (
        next_chunk(strided(k_ref, run - 1, run)),
        next_chunk(strided(k_ref, run - 2, run)),
        next_chunk(strided(v_ref, run - 1, run)),
        next_chunk(strided(v_ref, run - 2, run)),
        tuple(jnp.zeros((CHUNKS, LANES), F32) for _ in range(modes)),
    )
    states = lax.fori_loop(0, run, step, start, unroll=8)[4]
    for m in range(modes):
        total = states[m]
        distance = 1
        while distance < CHUNKS:
            factor = over_sublanes(jnp.exp(-float(run * distance) * decays_ref[m : m + 1, :]))
            total = total + factor * next_chunk(total, distance)
            distance *= 2
        state_ref[m] = next_chunk(total)
        rows_ref[m : m + 1, :] = total[CHUNKS - 1 : CHUNKS, :]
    rows_ref[modes : modes + 2, :] = k_ref[positions - 2 : positions, :]
    rows_ref[modes + 2 : modes + 4, :] = v_ref[positions - 2 : positions, :]
    rows_ref[modes + 4 : modes + 6, :] = x_ref[0, positions - 16 : positions, :].astype(F32)[14:16]
    rows_ref[modes + 6 : modes + 8, :] = k_ref[0:2, :]
    rows_ref[modes + 8 : modes + 10, :] = v_ref[0:2, :]
    rows_ref[modes + 10 :, :] = jnp.zeros((EXTRA - 10, LANES), F32)
    rows = rows_ref[...].astype(BF16)
    sent_ref[...] = jnp.broadcast_to(rows[None], sent_ref.shape)


def local_kernel(modes, x_ref, product_ref, taps_ref, decays_ref, residues_ref, skip_ref, gate_ref, base_ref, q_ref):
    positions = x_ref.shape[1]
    run = positions // CHUNKS
    q_ref[...] = x_ref[0].astype(F32)
    taps = [over_sublanes(taps_ref[0, i : i + 1, :]) for i in range(3)]
    skip = over_sublanes(skip_ref[...])
    rates = decays_ref[...]
    weights = residues_ref[...] * jnp.sqrt(2.0 * rates)
    factors = [over_sublanes(jnp.exp(-rates[m : m + 1, :])) for m in range(modes)]
    weights = [over_sublanes(weights[m : m + 1, :]) for m in range(modes)]

    def step(j, carry):
        q1, q2, states = carry
        q0 = strided(q_ref, j, run)
        gate_ref[j] = taps[0] * q0 + taps[1] * q1 + taps[2] * q2
        product = product_ref[j]
        states = tuple(a * h + product for a, h in zip(factors, states))
        base_ref[j] = added([skip * product] + [w * h for w, h in zip(weights, states)])
        return q0, q1, states

    start = (
        next_chunk(strided(q_ref, run - 1, run)),
        next_chunk(strided(q_ref, run - 2, run)),
        tuple(jnp.zeros((CHUNKS, LANES), F32) for _ in range(modes)),
    )
    lax.fori_loop(0, run, step, start, unroll=4)


def carry_kernel(
    modes, axis, count, received_ref, gate_ref, base_ref, state_ref, taps_ref, decays_ref, residues_ref, skip_ref,
    power_ref, gated_ref, rows_ref, first_ref, second_ref,
):
    run = gate_ref.shape[0]
    positions = run * CHUNKS
    device = lax.axis_index(axis)
    pitch = modes + EXTRA
    rows_ref[0:pitch, :] = jnp.zeros((pitch, LANES), F32)
    for e in range(count):
        rows_ref[pitch * (e + 1) : pitch * (e + 2), :] = received_ref[e].astype(F32)

    def of_all(row, shift):
        return rows_ref[pl.ds(pitch * (1 - shift) + modes + row, count, stride=pitch), :]

    products = []
    for j in (1, 2):
        tap = [taps_ref[j, i : i + 1, :] for i in range(3)]
        far = of_all(LAST + 2 * (j - 1), 1)
        near = of_all(LAST + 2 * (j - 1) + 1, 1)
        zero = of_all(FIRST + 2 * (j - 1), 0)
        one = of_all(FIRST + 2 * (j - 1) + 1, 0)
        own = (tap[0] * zero, tap[0] * one + tap[1] * zero)
        whole = (own[0] + tap[1] * near + tap[2] * far, own[1] + tap[2] * near)
        products.append((own, whole))
    (k_own, k_whole), (v_own, v_whole) = products
    first_ref[...] = k_whole[0] * v_whole[0] - k_own[0] * v_own[0]
    second_ref[...] = k_whole[1] * v_whole[1] - k_own[1] * v_own[1]

    rates = decays_ref[...]
    across = jnp.exp(-float(positions) * rates)
    state = jnp.zeros((modes, LANES), F32)
    late_first = jnp.exp(-float(positions - 1) * rates)
    late_second = jnp.exp(-float(positions - 2) * rates)
    for e in range(count - 1):
        arrived = rows_ref[pitch * (e + 1) : pitch * (e + 1) + modes, :]
        arrived = arrived + late_first * first_ref[e : e + 1, :] + late_second * second_ref[e : e + 1, :]
        state = jnp.where(e < device, across * state + arrived, state)
    first = first_ref[pl.ds(device, 1), :]
    second = second_ref[pl.ds(device, 1), :]
    weights = residues_ref[...] * jnp.sqrt(2.0 * rates)
    state = state + jnp.exp(rates) * first + jnp.exp(2.0 * rates) * second
    early = jnp.sum(weights * jnp.exp(rates), 0, keepdims=True) * second

    chunk = sublane_index()
    top = chunk == 0
    behind = chunk.astype(F32) * float(run)
    factors = []
    carried = []
    for m in range(modes):
        rate = over_sublanes(rates[m : m + 1, :])
        factors.append(jnp.exp(-rate))
        begin = state_ref[m] + jnp.exp(-rate * behind) * over_sublanes(state[m : m + 1, :])
        carried.append(over_sublanes(weights[m : m + 1, :]) * begin)

    edge = [rows_ref[pl.ds(device * pitch + modes + LAST + 4 + i, 1), :] for i in range(2)]
    gate_edge = (
        taps_ref[0, 1:2, :] * edge[1] + taps_ref[0, 2:3, :] * edge[0],
        taps_ref[0, 2:3, :] * edge[1],
    )
    skip = skip_ref[...]
    base_edge = (skip * first - early, skip * second)
    lane = lax.broadcasted_iota(jnp.int32, (CHUNKS, LANES), 1)

    def step(j, held, gate_extra=None, base_extra=None):
        carried, power = held
        carried = tuple(a * g for a, g in zip(factors, carried))
        gate, base = gate_ref[j], base_ref[j]
        if gate_extra is not None:
            gate = gate + jnp.where(top, over_sublanes(gate_extra), 0.0)
            base = base + jnp.where(top, over_sublanes(base_extra), 0.0)
        gated = gate * added([base] + list(carried))
        gated_ref[pl.ds(j, CHUNKS, stride=run), :] = gated
        square = jnp.sum(gated * gated, 1, keepdims=True)
        return carried, jnp.where(lane == j, square, power)

    held = (tuple(carried), jnp.zeros((CHUNKS, LANES), F32))
    for j in range(2):
        held = step(j, held, gate_edge[j], base_edge[j])
    power = lax.fori_loop(2, run, step, held, unroll=6)[1]
    power_ref[...] = jnp.broadcast_to(power[None], power_ref.shape)


def finish_kernel(channels, power_ref, gated_ref, gain_ref, mixed_ref):
    positions = gated_ref.shape[0]
    run = positions // CHUNKS
    inverse = lax.rsqrt(jnp.sum(power_ref[...], 0) / channels + 1e-05)
    turned = inverse.T
    gain = gain_ref[...]
    for s in range(CHUNKS):
        block = gated_ref[s * run : (s + 1) * run, :] * gain * turned[:, s : s + 1]
        mixed_ref[s * run : (s + 1) * run, :] = block.astype(BF16)


def per_device(projections, short_filter, residues, decays, skip, gain):
    positions, _, width = projections.shape
    modes = decays.shape[0]
    ctx_count = lax.axis_size("ctx")
    tp_count = lax.axis_size("tp")
    run = positions // CHUNKS
    x = jnp.swapaxes(projections, 0, 1)
    skip = skip[None, :]
    gain = gain[None, :]
    params = pltpu.CompilerParams(vmem_limit_bytes=VMEM_LIMIT)
    block = jax.ShapeDtypeStruct((run, CHUNKS, width), F32)

    sent, product, state = pl.pallas_call(
        functools.partial(states_kernel, modes),
        out_shape=(
            jax.ShapeDtypeStruct((ctx_count, modes + EXTRA, width), BF16),
            block,
            jax.ShapeDtypeStruct((modes, CHUNKS, width), F32),
        ),
        in_specs=[VMEM] * 3,
        out_specs=(VMEM,) * 3,
        scratch_shapes=[
            pltpu.VMEM((positions, width), F32),
            pltpu.VMEM((positions, width), F32),
            pltpu.VMEM((modes + EXTRA, width), F32),
        ],
        compiler_params=params,
        name="states",
    )(x, short_filter, decays)
    received = lax.all_to_all(sent, "ctx", split_axis=0, concat_axis=0, tiled=True)

    gate, base = pl.pallas_call(
        functools.partial(local_kernel, modes),
        out_shape=(block, block),
        in_specs=[VMEM] * 6,
        out_specs=(VMEM,) * 2,
        scratch_shapes=[pltpu.VMEM((positions, width), F32)],
        compiler_params=params,
        name="local",
    )(x, product, short_filter, decays, residues, skip)

    power, gated = pl.pallas_call(
        functools.partial(carry_kernel, modes, "ctx", ctx_count),
        out_shape=(
            jax.ShapeDtypeStruct((tp_count, CHUNKS, run), F32),
            jax.ShapeDtypeStruct((positions, width), F32),
        ),
        in_specs=[VMEM] * 8,
        out_specs=(VMEM,) * 2,
        scratch_shapes=[
            pltpu.VMEM(((ctx_count + 1) * (modes + EXTRA), width), F32),
            pltpu.VMEM((ctx_count, width), F32),
            pltpu.VMEM((ctx_count, width), F32),
        ],
        compiler_params=params,
        name="carry",
    )(received, gate, base, state, short_filter, decays, residues, skip)
    powers = lax.all_to_all(power, "tp", split_axis=0, concat_axis=0, tiled=True)

    return pl.pallas_call(
        functools.partial(finish_kernel, width * tp_count),
        out_shape=jax.ShapeDtypeStruct((positions, width), BF16),
        in_specs=[VMEM] * 3,
        out_specs=VMEM,
        compiler_params=params,
        name="finish",
    )(powers, gated, gain)


def solution(mesh):
    in_specs = (
        P("ctx", None, "tp"),
        P(None, None, "tp"),
        P(None, "tp"),
        P(None, "tp"),
        P("tp"),
        P("tp"),
    )
    return jax.shard_map(per_device, mesh=mesh, in_specs=in_specs, out_specs=P("ctx", "tp"), check_vma=False)
```

```python
import functools

import jax
import jax.numpy as jnp
from jax import lax
from jax.experimental import pallas as pl
from jax.experimental.pallas import tpu as pltpu
from jax.sharding import PartitionSpec as P

F32 = jnp.float32
BF16 = jnp.bfloat16
CHUNKS = 8
LANES = 128
PAIR = 2
VMEM_LIMIT = 40 * 1024 * 1024
VMEM = pl.BlockSpec(memory_space=pltpu.VMEM)
ANY = pl.BlockSpec(memory_space=pl.ANY)

K_LAST, V_LAST, Q_LAST, K_FIRST, V_FIRST = 0, 2, 4, 6, 8
EXTRA = 16


def over_sublanes(row):
    return jnp.broadcast_to(row, (CHUNKS, LANES))


def sublane_index():
    return lax.broadcasted_iota(jnp.int32, (CHUNKS, LANES), 0)


def next_chunk(block, distance=1):
    rolled = pltpu.roll(block, distance, 0)
    return jnp.where(sublane_index() >= distance, rolled, 0.0)


def strided(ref, step, run):
    return ref[pl.ds(step, CHUNKS, stride=run), :]


def added(terms):
    while len(terms) > 1:
        pairs = [terms[i] + terms[i + 1] for i in range(0, len(terms) - 1, 2)]
        terms = pairs + terms[2 * len(pairs) :]
    return terms[0]


def boundary(taps_ref, last, first):
    products = []
    for j in (1, 2):
        tap = [taps_ref[j, i : i + 1, :] for i in range(3)]
        (far, near), (zero, one) = last[j - 1], first[j - 1]
        own = (tap[0] * zero, tap[0] * one + tap[1] * zero)
        gained = (tap[1] * near + tap[2] * far, tap[2] * near)
        products.append((own, gained))
    (k_own, k_gained), (v_own, v_gained) = products
    return [k_own[i] * v_gained[i] + k_gained[i] * (v_own[i] + v_gained[i]) for i in range(2)]


def two_rows(ref, row):
    return ref[row : row + 1, :], ref[row + 1 : row + 2, :]


def pair_boundary(modes, taps_ref, lower_ref, upper_ref):
    last = [two_rows(lower_ref, modes + row) for row in (K_LAST, V_LAST)]
    first = [two_rows(upper_ref, modes + row) for row in (K_FIRST, V_FIRST)]
    return boundary(taps_ref, last, first)


def gate_gain(taps_ref, far, near):
    return taps_ref[0, 1:2, :] * near + taps_ref[0, 2:3, :] * far, taps_ref[0, 2:3, :] * near


def states_kernel(modes, *refs):
    sources, refs = refs[:6], refs[6:]
    x_hbm = sources[0]
    (rows_ref, product_ref, state_ref, q_ref), refs = refs[:4], refs[4:]
    params, refs = refs[:5], refs[5:]
    taps_ref, decays_ref = params[0], params[1]
    k_half, v_half, k_ref, v_ref, semaphores = refs
    copies = [pltpu.make_async_copy(s, d, semaphores.at[i]) for i, (s, d) in enumerate(zip(sources[1:], params))]
    streams = [
        pltpu.make_async_copy(x_hbm.at[j], d, semaphores.at[5 + j]) for j, d in enumerate((q_ref, k_half, v_half))
    ]
    for copy in (streams[1], streams[2], copies[1], copies[0], streams[0], copies[2], copies[3], copies[4]):
        copy.start()
    positions = k_ref.shape[0]
    run = positions // CHUNKS
    copies[1].wait()
    copies[0].wait()
    k_taps = [over_sublanes(taps_ref[1, i : i + 1, :]) for i in range(3)]
    v_taps = [over_sublanes(taps_ref[2, i : i + 1, :]) for i in range(3)]
    factors = [over_sublanes(jnp.exp(-decays_ref[m : m + 1, :])) for m in range(modes)]
    streams[1].wait()
    k_ref[...] = k_half[...].astype(F32)
    streams[2].wait()
    v_ref[...] = v_half[...].astype(F32)

    def step(j, carry):
        k1, k2, v1, v2, states = carry
        k0 = strided(k_ref, j, run)
        v0 = strided(v_ref, j, run)
        k = k_taps[0] * k0 + k_taps[1] * k1 + k_taps[2] * k2
        v = v_taps[0] * v0 + v_taps[1] * v1 + v_taps[2] * v2
        product = k * v
        product_ref[j] = product
        states = tuple(a * h + product for a, h in zip(factors, states))
        return k0, k1, v0, v1, states

    start = (
        next_chunk(strided(k_ref, run - 1, run)),
        next_chunk(strided(k_ref, run - 2, run)),
        next_chunk(strided(v_ref, run - 1, run)),
        next_chunk(strided(v_ref, run - 2, run)),
        tuple(jnp.zeros((CHUNKS, LANES), F32) for _ in range(modes)),
    )
    states = lax.fori_loop(0, run, step, start, unroll=8)[4]
    for m in range(modes):
        total = states[m]
        distance = 1
        while distance < CHUNKS:
            factor = over_sublanes(jnp.exp(-float(run * distance) * decays_ref[m : m + 1, :]))
            total = total + factor * next_chunk(total, distance)
            distance *= 2
        state_ref[m] = next_chunk(total)
        rows_ref[m : m + 1, :] = total[CHUNKS - 1 : CHUNKS, :]
    streams[0].wait()
    rows_ref[modes + K_LAST : modes + K_LAST + 2, :] = k_ref[positions - 2 : positions, :]
    rows_ref[modes + V_LAST : modes + V_LAST + 2, :] = v_ref[positions - 2 : positions, :]
    rows_ref[modes + Q_LAST : modes + Q_LAST + 2, :] = q_ref[positions - 16 : positions, :].astype(F32)[14:16]
    rows_ref[modes + K_FIRST : modes + K_FIRST + 2, :] = k_ref[0:2, :]
    rows_ref[modes + V_FIRST : modes + V_FIRST + 2, :] = v_ref[0:2, :]
    rows_ref[modes + V_FIRST + 2 :, :] = jnp.zeros((EXTRA - V_FIRST - 2, LANES), F32)
    for i in (2, 3, 4):
        copies[i].wait()


def join_kernel(modes, positions, axis, own_ref, other_ref, taps_ref, decays_ref, sent_ref, pair_ref):
    upper = lax.rem(lax.axis_index(axis), PAIR) == 1
    own = own_ref[...]
    other = other_ref[...]
    below = jnp.where(upper, other, own)
    above = jnp.where(upper, own, other)
    pair_ref[0] = below
    pair_ref[1] = above
    first, second = pair_boundary(modes, taps_ref, pair_ref.at[0], pair_ref.at[1])
    rates = decays_ref[...]
    state = jnp.exp(-float(positions) * rates) * below[:modes] + above[:modes]
    state = state + jnp.exp(-float(positions - 1) * rates) * first + jnp.exp(-float(positions - 2) * rates) * second
    row = lax.broadcasted_iota(jnp.int32, (EXTRA, LANES), 0)
    beside = jnp.where(row < K_FIRST, above[modes:], below[modes:])
    rows = jnp.concatenate([state, beside], 0).astype(BF16)
    sent_ref[...] = jnp.broadcast_to(rows[None], sent_ref.shape)


def local_kernel(
    modes, axis, pairs, q_half, product_ref, state_ref, pair_ref, taps_ref, decays_ref, residues_ref, skip_ref,
    gate_ref, base_ref, begin_ref, reach_ref, factor_ref, weight_ref, late_ref, q_ref,
):
    positions = q_ref.shape[0]
    run = positions // CHUNKS
    device = lax.axis_index(axis)
    pair = device // PAIR
    upper = lax.rem(device, PAIR)
    inside = upper.astype(F32)
    q_ref[...] = q_half[...].astype(F32)
    taps = [over_sublanes(taps_ref[0, i : i + 1, :]) for i in range(3)]
    skip = over_sublanes(skip_ref[...])
    rates = decays_ref[...]
    weights = residues_ref[...] * jnp.sqrt(2.0 * rates)
    factors = [over_sublanes(jnp.exp(-rates[m : m + 1, :])) for m in range(modes)]
    spread = [over_sublanes(weights[m : m + 1, :]) for m in range(modes)]

    first, second = pair_boundary(modes, taps_ref, pair_ref.at[0], pair_ref.at[1])
    first, second = first * inside, second * inside
    arrived = inside * pair_ref[0, :modes, :] + jnp.exp(rates) * first + jnp.exp(2.0 * rates) * second
    early = jnp.sum(weights * jnp.exp(rates), 0, keepdims=True) * second
    gain = gate_gain(taps_ref, *two_rows(pair_ref.at[0], modes + Q_LAST))

    def step(j, carry):
        q1, q2, states = carry
        q0 = strided(q_ref, j, run)
        gate_ref[j] = taps[0] * q0 + taps[1] * q1 + taps[2] * q2
        product = product_ref[j]
        states = tuple(a * h + product for a, h in zip(factors, states))
        base_ref[j] = added([skip * product] + [w * h for w, h in zip(spread, states)])
        return q0, q1, states

    start = (
        next_chunk(strided(q_ref, run - 1, run)),
        next_chunk(strided(q_ref, run - 2, run)),
        tuple(jnp.zeros((CHUNKS, LANES), F32) for _ in range(modes)),
    )
    lax.fori_loop(0, run, step, start, unroll=4)
    top = sublane_index() == 0
    base_gain = (skip_ref[...] * first - early, skip_ref[...] * second)
    for j in range(2):
        gate_ref[j] = gate_ref[j] + jnp.where(top, over_sublanes(gain[j] * inside), 0.0)
        base_ref[j] = base_ref[j] + jnp.where(top, over_sublanes(base_gain[j]), 0.0)

    behind = sublane_index().astype(F32) * float(run)
    for m in range(modes):
        rate = over_sublanes(rates[m : m + 1, :])
        fade = jnp.exp(-rate * behind)
        begin_ref[m] = spread[m] * (state_ref[m] + fade * over_sublanes(arrived[m : m + 1, :]))
        reach_ref[m] = spread[m] * fade * jnp.exp(-rate * (inside * float(positions)))
        factor_ref[m] = factors[m]
    length = PAIR * positions
    for e in range(pairs):
        distance = (jnp.maximum(pair - 1 - e, 0) * length).astype(F32)
        weight_ref[e] = jnp.where(e < pair, jnp.exp(-rates * distance), 0.0)
        distance = (jnp.maximum(pair - e, 0) * length - 1).astype(F32)
        late_ref[e] = jnp.where(e <= pair, jnp.exp(-rates * distance), 0.0)


def carry_kernel(
    modes, axis, received_ref, gate_ref, base_ref, begin_ref, reach_ref, factor_ref, weight_ref, late_ref,
    taps_ref, decays_ref, residues_ref, skip_ref, power_ref, gated_ref, rows_ref, first_ref, second_ref,
):
    run = gate_ref.shape[0]
    pairs = received_ref.shape[0]
    device = lax.axis_index(axis)
    pair = device // PAIR
    lower = 1.0 - lax.rem(device, PAIR).astype(F32)
    pitch = modes + EXTRA
    rows_ref[0:pitch, :] = jnp.zeros((pitch, LANES), F32)
    for e in range(pairs):
        rows_ref[pitch * (e + 1) : pitch * (e + 2), :] = received_ref[e].astype(F32)

    def of_all(row, block):
        return tuple(rows_ref[pl.ds(pitch * block + modes + row + i, pairs, stride=pitch), :] for i in range(2))

    last = [of_all(row, 0) for row in (K_LAST, V_LAST)]
    begun = [of_all(row, 1) for row in (K_FIRST, V_FIRST)]
    first_ref[...], second_ref[...] = boundary(taps_ref, last, begun)

    rates = decays_ref[...]
    states, firsts, seconds = [], [], []
    for e in range(pairs):
        states.append(weight_ref[e] * rows_ref[pitch * (e + 1) : pitch * (e + 1) + modes, :])
        firsts.append(late_ref[e] * first_ref[e : e + 1, :])
        seconds.append(late_ref[e] * second_ref[e : e + 1, :])
    state = added(states) + added(firsts) + jnp.exp(rates) * added(seconds)

    first = first_ref[pl.ds(pair, 1), :] * lower
    second = second_ref[pl.ds(pair, 1), :] * lower
    weights = residues_ref[...] * jnp.sqrt(2.0 * rates)
    early = jnp.sum(weights * jnp.exp(rates), 0, keepdims=True) * second
    edge = [rows_ref[pl.ds(pair * pitch + modes + Q_LAST + i, 1), :] * lower for i in range(2)]
    gate_extra = gate_gain(taps_ref, *edge)
    skip = skip_ref[...]
    base_extra = (skip * first - early, skip * second)
    top = sublane_index() == 0
    factors = [factor_ref[m] for m in range(modes)]
    carried = [begin_ref[m] + reach_ref[m] * over_sublanes(state[m : m + 1, :]) for m in range(modes)]

    def step(j, carried, gate_more=None, base_more=None):
        carried = tuple(a * g for a, g in zip(factors, carried))
        gate, base = gate_ref[j], base_ref[j]
        if gate_more is not None:
            gate = gate + jnp.where(top, over_sublanes(gate_more), 0.0)
            base = base + jnp.where(top, over_sublanes(base_more), 0.0)
        gated_ref[pl.ds(j, CHUNKS, stride=run), :] = gate * added([base] + list(carried))
        return carried

    carried = tuple(carried)
    for j in range(2):
        carried = step(j, carried, gate_extra[j], base_extra[j])
    lax.fori_loop(2, run, step, carried, unroll=6)

    gated = gated_ref[...]
    square = gated * gated
    high = square.astype(BF16)
    low = (square - high.astype(F32)).astype(BF16)
    ones = jnp.ones((LANES, LANES), BF16)
    sums = jnp.dot(high, ones, preferred_element_type=F32) + jnp.dot(low, ones, preferred_element_type=F32)
    lane = lax.broadcasted_iota(jnp.int32, (CHUNKS, LANES), 1)
    power = jnp.zeros((CHUNKS, LANES), F32)
    for i in range(run):
        power = jnp.where(lane == i, sums[i * CHUNKS : (i + 1) * CHUNKS, :], power)
    power_ref[...] = jnp.broadcast_to(power[None], power_ref.shape)


def finish_kernel(channels, power_ref, gated_ref, gain_ref, mixed_ref):
    run = gated_ref.shape[0] // CHUNKS
    inverse = lax.rsqrt(jnp.sum(power_ref[...], 0) / channels + 1e-05)
    gain = over_sublanes(gain_ref[...])
    for i in range(0, run, 2):
        halves = [
            gated_ref[(i + h) * CHUNKS : (i + h + 1) * CHUNKS, :] * gain * inverse[:, i + h : i + h + 1] for h in range(2)
        ]
        mixed_ref[i * CHUNKS : (i + 2) * CHUNKS, :] = jnp.concatenate(halves, 0).astype(BF16)


def per_device(projections, short_filter, residues, decays, skip, gain):
    positions, _, width = projections.shape
    modes = decays.shape[0]
    ctx_count = lax.axis_size("ctx")
    tp_count = lax.axis_size("tp")
    pairs = ctx_count // PAIR
    run = positions // CHUNKS
    x = jnp.swapaxes(projections, 0, 1)

    def shape(*extent, kind=F32):
        return jax.ShapeDtypeStruct(extent, kind)

    def call(kernel, name, out_shape, in_specs, scratch, *operands):
        return pl.pallas_call(
            kernel,
            out_shape=out_shape,
            in_specs=in_specs,
            out_specs=jax.tree.map(lambda _: VMEM, out_shape),
            scratch_shapes=scratch,
            compiler_params=pltpu.CompilerParams(vmem_limit_bytes=VMEM_LIMIT),
            name=name,
        )(*operands)

    block = shape(run, CHUNKS, width)
    table = shape(modes, CHUNKS, width)
    sources = (x, short_filter, decays, residues, skip[None, :], gain[None, :])
    rows, product, state, q, short_filter, decays, residues, skip, gain = call(
        functools.partial(states_kernel, modes),
        "states",
        (shape(modes + EXTRA, width), block, table, shape(positions, width, kind=BF16))
        + tuple(shape(*s.shape) for s in sources[1:]),
        [ANY] * 6,
        [
            pltpu.VMEM((positions, width), BF16),
            pltpu.VMEM((positions, width), BF16),
            pltpu.VMEM((positions, width), F32),
            pltpu.VMEM((positions, width), F32),
            pltpu.SemaphoreType.DMA((8,)),
        ],
        *sources,
    )
    other = lax.ppermute(rows, "ctx", [(i, i + 1 - 2 * (i % PAIR)) for i in range(ctx_count)])
    sent, joined = call(
        functools.partial(join_kernel, modes, positions, "ctx"),
        "join",
        (shape(pairs, modes + EXTRA, width, kind=BF16), shape(PAIR, modes + EXTRA, width)),
        [VMEM] * 4,
        [],
        rows,
        other,
        short_filter,
        decays,
    )
    groups = [[PAIR * i + h for i in range(pairs)] for h in range(PAIR)]
    received = lax.all_to_all(sent, "ctx", split_axis=0, concat_axis=0, tiled=True, axis_index_groups=groups)

    gate, base, begin, reach, factor, weight, late = call(
        functools.partial(local_kernel, modes, "ctx", pairs),
        "local",
        (block, block, table, table, table, shape(pairs, modes, width), shape(pairs, modes, width)),
        [VMEM] * 8,
        [pltpu.VMEM((positions, width), F32)],
        q,
        product,
        state,
        joined,
        short_filter,
        decays,
        residues,
        skip,
    )
    power, gated = call(
        functools.partial(carry_kernel, modes, "ctx"),
        "carry",
        (shape(tp_count, CHUNKS, run), shape(positions, width)),
        [VMEM] * 12,
        [
            pltpu.VMEM(((pairs + 1) * (modes + EXTRA), width), F32),
            pltpu.VMEM((pairs, width), F32),
            pltpu.VMEM((pairs, width), F32),
        ],
        received,
        gate,
        base,
        begin,
        reach,
        factor,
        weight,
        late,
        short_filter,
        decays,
        residues,
        skip,
    )
    powers = lax.all_to_all(power, "tp", split_axis=0, concat_axis=0, tiled=True)
    return call(
        functools.partial(finish_kernel, width * tp_count),
        "finish",
        shape(positions, width, kind=BF16),
        [VMEM] * 3,
        [],
        powers,
        gated,
        gain,
    )


def solution(mesh):
    in_specs = (
        P("ctx", None, "tp"),
        P(None, None, "tp"),
        P(None, "tp"),
        P(None, "tp"),
        P("tp"),
        P("tp"),
    )
    return jax.shard_map(per_device, mesh=mesh, in_specs=in_specs, out_specs=P("ctx", "tp"), check_vma=False)
```

```python
import functools

import jax
import jax.numpy as jnp
from jax import lax
from jax.experimental import pallas as pl
from jax.experimental.pallas import tpu as pltpu
from jax.sharding import PartitionSpec as P

F32 = jnp.float32
BF16 = jnp.bfloat16
CHUNKS = 8
LANES = 128
PAIR = 2
VMEM_LIMIT = 40 * 1024 * 1024
VMEM = pl.BlockSpec(memory_space=pltpu.VMEM)
ANY = pl.BlockSpec(memory_space=pl.ANY)

K_LAST, V_LAST, Q_LAST, K_FIRST, V_FIRST = 0, 2, 4, 6, 8
EXTRA = 16


def over_sublanes(row):
    return jnp.broadcast_to(row, (CHUNKS, LANES))


def sublane_index():
    return lax.broadcasted_iota(jnp.int32, (CHUNKS, LANES), 0)


def next_chunk(block, distance=1):
    rolled = pltpu.roll(block, distance, 0)
    return jnp.where(sublane_index() >= distance, rolled, 0.0)


def strided(ref, step, run):
    return ref[pl.ds(step, CHUNKS, stride=run), :]


def added(terms):
    while len(terms) > 1:
        pairs = [terms[i] + terms[i + 1] for i in range(0, len(terms) - 1, 2)]
        terms = pairs + terms[2 * len(pairs) :]
    return terms[0]


def boundary(taps_ref, last, first):
    products = []
    for j in (1, 2):
        tap = [taps_ref[j, i : i + 1, :] for i in range(3)]
        (far, near), (zero, one) = last[j - 1], first[j - 1]
        own = (tap[0] * zero, tap[0] * one + tap[1] * zero)
        gained = (tap[1] * near + tap[2] * far, tap[2] * near)
        products.append((own, gained))
    (k_own, k_gained), (v_own, v_gained) = products
    return [k_own[i] * v_gained[i] + k_gained[i] * (v_own[i] + v_gained[i]) for i in range(2)]


def two_rows(ref, row):
    return ref[row : row + 1, :], ref[row + 1 : row + 2, :]


def pair_boundary(modes, taps_ref, lower_ref, upper_ref):
    last = [two_rows(lower_ref, modes + row) for row in (K_LAST, V_LAST)]
    first = [two_rows(upper_ref, modes + row) for row in (K_FIRST, V_FIRST)]
    return boundary(taps_ref, last, first)


def gate_gain(taps_ref, far, near):
    return taps_ref[0, 1:2, :] * near + taps_ref[0, 2:3, :] * far, taps_ref[0, 2:3, :] * near


def states_kernel(modes, *refs):
    sources, refs = refs[:6], refs[6:]
    x_hbm = sources[0]
    (rows_ref, product_ref, state_ref, q_ref), refs = refs[:4], refs[4:]
    params, refs = refs[:5], refs[5:]
    taps_ref, decays_ref = params[0], params[1]
    k_half, v_half, k_ref, v_ref, semaphores = refs
    copies = [pltpu.make_async_copy(s, d, semaphores.at[i]) for i, (s, d) in enumerate(zip(sources[1:], params))]
    streams = [
        pltpu.make_async_copy(x_hbm.at[j], d, semaphores.at[5 + j]) for j, d in enumerate((q_ref, k_half, v_half))
    ]
    for copy in (streams[1], streams[2], copies[1], copies[0], streams[0], copies[2], copies[3], copies[4]):
        copy.start()
    positions = k_ref.shape[0]
    run = positions // CHUNKS
    copies[1].wait()
    copies[0].wait()
    k_taps = [over_sublanes(taps_ref[1, i : i + 1, :]) for i in range(3)]
    v_taps = [over_sublanes(taps_ref[2, i : i + 1, :]) for i in range(3)]
    factors = [over_sublanes(jnp.exp(-decays_ref[m : m + 1, :])) for m in range(modes)]
    streams[1].wait()
    k_ref[...] = k_half[...].astype(F32)
    streams[2].wait()
    v_ref[...] = v_half[...].astype(F32)

    def step(j, carry):
        k1, k2, v1, v2, states = carry
        k0 = strided(k_ref, j, run)
        v0 = strided(v_ref, j, run)
        k = k_taps[0] * k0 + k_taps[1] * k1 + k_taps[2] * k2
        v = v_taps[0] * v0 + v_taps[1] * v1 + v_taps[2] * v2
        product = k * v
        product_ref[j] = product
        states = tuple(a * h + product for a, h in zip(factors, states))
        return k0, k1, v0, v1, states

    start = (
        next_chunk(strided(k_ref, run - 1, run)),
        next_chunk(strided(k_ref, run - 2, run)),
        next_chunk(strided(v_ref, run - 1, run)),
        next_chunk(strided(v_ref, run - 2, run)),
        tuple(jnp.zeros((CHUNKS, LANES), F32) for _ in range(modes)),
    )
    states = lax.fori_loop(0, run, step, start, unroll=8)[4]
    for m in range(modes):
        total = states[m]
        distance = 1
        while distance < CHUNKS:
            factor = over_sublanes(jnp.exp(-float(run * distance) * decays_ref[m : m + 1, :]))
            total = total + factor * next_chunk(total, distance)
            distance *= 2
        state_ref[m] = next_chunk(total)
        rows_ref[m : m + 1, :] = total[CHUNKS - 1 : CHUNKS, :]
    streams[0].wait()
    rows_ref[modes + K_LAST : modes + K_LAST + 2, :] = k_ref[positions - 2 : positions, :]
    rows_ref[modes + V_LAST : modes + V_LAST + 2, :] = v_ref[positions - 2 : positions, :]
    rows_ref[modes + Q_LAST : modes + Q_LAST + 2, :] = q_ref[positions - 16 : positions, :].astype(F32)[14:16]
    rows_ref[modes + K_FIRST : modes + K_FIRST + 2, :] = k_ref[0:2, :]
    rows_ref[modes + V_FIRST : modes + V_FIRST + 2, :] = v_ref[0:2, :]
    rows_ref[modes + V_FIRST + 2 :, :] = jnp.zeros((EXTRA - V_FIRST - 2, LANES), F32)
    for i in (2, 3, 4):
        copies[i].wait()


def join_kernel(modes, positions, axis, own_ref, other_ref, taps_ref, decays_ref, sent_ref, pair_ref):
    upper = lax.rem(lax.axis_index(axis), PAIR) == 1
    own = own_ref[...]
    other = other_ref[...]
    below = jnp.where(upper, other, own)
    above = jnp.where(upper, own, other)
    pair_ref[0] = below
    pair_ref[1] = above
    first, second = pair_boundary(modes, taps_ref, pair_ref.at[0], pair_ref.at[1])
    rates = decays_ref[...]
    state = jnp.exp(-float(positions) * rates) * below[:modes] + above[:modes]
    state = state + jnp.exp(-float(positions - 1) * rates) * first + jnp.exp(-float(positions - 2) * rates) * second
    row = lax.broadcasted_iota(jnp.int32, (EXTRA, LANES), 0)
    beside = jnp.where(row < K_FIRST, above[modes:], below[modes:])
    rows = jnp.concatenate([state, beside], 0).astype(BF16)
    sent_ref[...] = jnp.broadcast_to(rows[None], sent_ref.shape)


def local_kernel(
    modes, axis, pairs, q_half, product_ref, state_ref, pair_ref, taps_ref, decays_ref, residues_ref, skip_ref,
    gate_ref, base_ref, begin_ref, reach_ref, factor_ref, weight_ref, late_ref, q_ref,
):
    positions = q_ref.shape[0]
    run = positions // CHUNKS
    device = lax.axis_index(axis)
    pair = device // PAIR
    upper = lax.rem(device, PAIR)
    inside = upper.astype(F32)
    q_ref[...] = q_half[...].astype(F32)
    taps = [over_sublanes(taps_ref[0, i : i + 1, :]) for i in range(3)]
    skip = over_sublanes(skip_ref[...])
    rates = decays_ref[...]
    weights = residues_ref[...] * jnp.sqrt(2.0 * rates)
    factors = [over_sublanes(jnp.exp(-rates[m : m + 1, :])) for m in range(modes)]
    spread = [over_sublanes(weights[m : m + 1, :]) for m in range(modes)]

    first, second = pair_boundary(modes, taps_ref, pair_ref.at[0], pair_ref.at[1])
    first, second = first * inside, second * inside
    arrived = inside * pair_ref[0, :modes, :] + jnp.exp(rates) * first + jnp.exp(2.0 * rates) * second
    early = jnp.sum(weights * jnp.exp(rates), 0, keepdims=True) * second
    gain = gate_gain(taps_ref, *two_rows(pair_ref.at[0], modes + Q_LAST))

    def step(j, carry):
        q1, q2, states = carry
        q0 = strided(q_ref, j, run)
        gate_ref[j] = taps[0] * q0 + taps[1] * q1 + taps[2] * q2
        product = product_ref[j]
        states = tuple(a * h + product for a, h in zip(factors, states))
        base_ref[j] = added([skip * product] + [w * h for w, h in zip(spread, states)])
        return q0, q1, states

    start = (
        next_chunk(strided(q_ref, run - 1, run)),
        next_chunk(strided(q_ref, run - 2, run)),
        tuple(jnp.zeros((CHUNKS, LANES), F32) for _ in range(modes)),
    )
    lax.fori_loop(0, run, step, start, unroll=4)
    top = sublane_index() == 0
    base_gain = (skip_ref[...] * first - early, skip_ref[...] * second)
    for j in range(2):
        gate_ref[j] = gate_ref[j] + jnp.where(top, over_sublanes(gain[j] * inside), 0.0)
        base_ref[j] = base_ref[j] + jnp.where(top, over_sublanes(base_gain[j]), 0.0)

    behind = sublane_index().astype(F32) * float(run)
    for m in range(modes):
        rate = over_sublanes(rates[m : m + 1, :])
        fade = jnp.exp(-rate * behind)
        begin_ref[m] = spread[m] * (state_ref[m] + fade * over_sublanes(arrived[m : m + 1, :]))
        reach_ref[m] = spread[m] * fade * jnp.exp(-rate * (inside * float(positions)))
        factor_ref[m] = factors[m]
    length = PAIR * positions
    for e in range(pairs):
        distance = (jnp.maximum(pair - 1 - e, 0) * length).astype(F32)
        weight_ref[e] = jnp.where(e < pair, jnp.exp(-rates * distance), 0.0)
        distance = (jnp.maximum(pair - e, 0) * length - 1).astype(F32)
        late_ref[e] = jnp.where(e <= pair, jnp.exp(-rates * distance), 0.0)


def carry_kernel(
    modes, axis, received_ref, gate_ref, base_ref, begin_ref, reach_ref, factor_ref, weight_ref, late_ref,
    taps_ref, decays_ref, residues_ref, skip_ref, power_ref, gated_ref, rows_ref, first_ref, second_ref,
):
    run = gate_ref.shape[0]
    pairs = received_ref.shape[0]
    device = lax.axis_index(axis)
    pair = device // PAIR
    lower = 1.0 - lax.rem(device, PAIR).astype(F32)
    pitch = modes + EXTRA
    rows_ref[0:pitch, :] = jnp.zeros((pitch, LANES), F32)
    for e in range(pairs):
        rows_ref[pitch * (e + 1) : pitch * (e + 2), :] = received_ref[e].astype(F32)

    def of_all(row, block):
        return tuple(rows_ref[pl.ds(pitch * block + modes + row + i, pairs, stride=pitch), :] for i in range(2))

    last = [of_all(row, 0) for row in (K_LAST, V_LAST)]
    begun = [of_all(row, 1) for row in (K_FIRST, V_FIRST)]
    first_ref[...], second_ref[...] = boundary(taps_ref, last, begun)

    rates = decays_ref[...]
    states, firsts, seconds = [], [], []
    for e in range(pairs):
        states.append(weight_ref[e] * rows_ref[pitch * (e + 1) : pitch * (e + 1) + modes, :])
        firsts.append(late_ref[e] * first_ref[e : e + 1, :])
        seconds.append(late_ref[e] * second_ref[e : e + 1, :])
    state = added(states) + added(firsts) + jnp.exp(rates) * added(seconds)

    first = first_ref[pl.ds(pair, 1), :] * lower
    second = second_ref[pl.ds(pair, 1), :] * lower
    weights = residues_ref[...] * jnp.sqrt(2.0 * rates)
    early = jnp.sum(weights * jnp.exp(rates), 0, keepdims=True) * second
    edge = [rows_ref[pl.ds(pair * pitch + modes + Q_LAST + i, 1), :] * lower for i in range(2)]
    gate_extra = gate_gain(taps_ref, *edge)
    skip = skip_ref[...]
    base_extra = (skip * first - early, skip * second)
    top = sublane_index() == 0
    factors = [factor_ref[m] for m in range(modes)]
    carried = [begin_ref[m] + reach_ref[m] * over_sublanes(state[m : m + 1, :]) for m in range(modes)]

    def step(j, carried, gate_more=None, base_more=None):
        carried = tuple(a * g for a, g in zip(factors, carried))
        gate, base = gate_ref[j], base_ref[j]
        if gate_more is not None:
            gate = gate + jnp.where(top, over_sublanes(gate_more), 0.0)
            base = base + jnp.where(top, over_sublanes(base_more), 0.0)
        gated_ref[pl.ds(j, CHUNKS, stride=run), :] = gate * added([base] + list(carried))
        return carried

    carried = tuple(carried)
    for j in range(2):
        carried = step(j, carried, gate_extra[j], base_extra[j])
    lax.fori_loop(2, run, step, carried, unroll=6)

    gated = gated_ref[...]
    square = gated * gated
    high = square.astype(BF16)
    low = (square - high.astype(F32)).astype(BF16)
    ones = jnp.ones((LANES, LANES), BF16)
    sums = jnp.dot(high, ones, preferred_element_type=F32) + jnp.dot(low, ones, preferred_element_type=F32)
    lane = lax.broadcasted_iota(jnp.int32, (CHUNKS, LANES), 1)
    power = jnp.zeros((CHUNKS, LANES), F32)
    for i in range(run):
        power = jnp.where(lane == i, sums[i * CHUNKS : (i + 1) * CHUNKS, :], power)
    power_ref[...] = jnp.broadcast_to(power[None], power_ref.shape)


def finish_kernel(channels, power_ref, gated_ref, gain_ref, mixed_ref):
    run = gated_ref.shape[0] // CHUNKS
    inverse = lax.rsqrt(jnp.sum(power_ref[...], 0) / channels + 1e-05)
    gain = over_sublanes(gain_ref[...])
    for i in range(0, run, 2):
        halves = [
            gated_ref[(i + h) * CHUNKS : (i + h + 1) * CHUNKS, :] * gain * inverse[:, i + h : i + h + 1] for h in range(2)
        ]
        mixed_ref[i * CHUNKS : (i + 2) * CHUNKS, :] = jnp.concatenate(halves, 0).astype(BF16)


def per_device(projections, short_filter, residues, decays, skip, gain):
    positions, _, width = projections.shape
    modes = decays.shape[0]
    ctx_count = lax.axis_size("ctx")
    tp_count = lax.axis_size("tp")
    pairs = ctx_count // PAIR
    run = positions // CHUNKS
    x = jnp.swapaxes(projections, 0, 1)

    def shape(*extent, kind=F32):
        return jax.ShapeDtypeStruct(extent, kind)

    def call(kernel, name, out_shape, in_specs, scratch, *operands):
        return pl.pallas_call(
            kernel,
            out_shape=out_shape,
            in_specs=in_specs,
            out_specs=jax.tree.map(lambda _: VMEM, out_shape),
            scratch_shapes=scratch,
            compiler_params=pltpu.CompilerParams(vmem_limit_bytes=VMEM_LIMIT),
            name=name,
        )(*operands)

    block = shape(run, CHUNKS, width)
    table = shape(modes, CHUNKS, width)
    sources = (x, short_filter, decays, residues, skip[None, :], gain[None, :])
    rows, product, state, q, short_filter, decays, residues, skip, gain = call(
        functools.partial(states_kernel, modes),
        "states",
        (shape(modes + EXTRA, width), block, table, shape(positions, width, kind=BF16))
        + tuple(shape(*s.shape) for s in sources[1:]),
        [ANY] * 6,
        [
            pltpu.VMEM((positions, width), BF16),
            pltpu.VMEM((positions, width), BF16),
            pltpu.VMEM((positions, width), F32),
            pltpu.VMEM((positions, width), F32),
            pltpu.SemaphoreType.DMA((8,)),
        ],
        *[pltpu.with_memory_space_constraint(s, pltpu.HBM) for s in sources],
    )
    other = lax.ppermute(rows, "ctx", [(i, i + 1 - 2 * (i % PAIR)) for i in range(ctx_count)])
    sent, joined = call(
        functools.partial(join_kernel, modes, positions, "ctx"),
        "join",
        (shape(pairs, modes + EXTRA, width, kind=BF16), shape(PAIR, modes + EXTRA, width)),
        [VMEM] * 4,
        [],
        rows,
        other,
        short_filter,
        decays,
    )
    groups = [[PAIR * i + h for i in range(pairs)] for h in range(PAIR)]
    received = lax.all_to_all(sent, "ctx", split_axis=0, concat_axis=0, tiled=True, axis_index_groups=groups)

    gate, base, begin, reach, factor, weight, late = call(
        functools.partial(local_kernel, modes, "ctx", pairs),
        "local",
        (block, block, table, table, table, shape(pairs, modes, width), shape(pairs, modes, width)),
        [VMEM] * 8,
        [pltpu.VMEM((positions, width), F32)],
        q,
        product,
        state,
        joined,
        short_filter,
        decays,
        residues,
        skip,
    )
    power, gated = call(
        functools.partial(carry_kernel, modes, "ctx"),
        "carry",
        (shape(tp_count, CHUNKS, run), shape(positions, width)),
        [VMEM] * 12,
        [
            pltpu.VMEM(((pairs + 1) * (modes + EXTRA), width), F32),
            pltpu.VMEM((pairs, width), F32),
            pltpu.VMEM((pairs, width), F32),
        ],
        received,
        gate,
        base,
        begin,
        reach,
        factor,
        weight,
        late,
        short_filter,
        decays,
        residues,
        skip,
    )
    powers = lax.all_to_all(power, "tp", split_axis=0, concat_axis=0, tiled=True)
    return call(
        functools.partial(finish_kernel, width * tp_count),
        "finish",
        shape(positions, width, kind=BF16),
        [VMEM] * 3,
        [],
        powers,
        gated,
        gain,
    )


def solution(mesh):
    in_specs = (
        P("ctx", None, "tp"),
        P(None, None, "tp"),
        P(None, "tp"),
        P(None, "tp"),
        P("tp"),
        P("tp"),
    )
    return jax.shard_map(per_device, mesh=mesh, in_specs=in_specs, out_specs=P("ctx", "tp"), check_vma=False)
```

```python
import functools

import jax
import jax.numpy as jnp
from jax import lax
from jax.experimental import pallas as pl
from jax.experimental.pallas import tpu as pltpu
from jax.sharding import PartitionSpec as P

F32 = jnp.float32
BF16 = jnp.bfloat16
CHUNKS = 8
LANES = 128
PAIR = 2
VMEM_LIMIT = 40 * 1024 * 1024
VMEM = pl.BlockSpec(memory_space=pltpu.VMEM)
ANY = pl.BlockSpec(memory_space=pl.ANY)

FIRST_PAIR = 10
FIRST_SLICE = 5
GRID = 4

K_LAST, V_LAST, Q_LAST, K_FIRST, V_FIRST = 0, 2, 4, 6, 8
EXTRA = 16


def first_then(first, members, distance):
    return [first] + sorted((i for i in range(members) if i != first), key=lambda i: -distance(i, first))


def around(a, b, size):
    return min((a - b) % size, (b - a) % size)


def pair_order(pairs):
    def distance(a, b):
        return around(a // GRID, b // GRID, max(pairs // GRID, 1)) + 2 * around(a % GRID, b % GRID, GRID)

    return first_then(FIRST_PAIR % pairs, pairs, distance)


def slice_order(slices):
    return first_then(FIRST_SLICE % slices, slices, lambda a, b: 0)


def over_sublanes(row):
    return jnp.broadcast_to(row, (CHUNKS, LANES))


def sublane_index():
    return lax.broadcasted_iota(jnp.int32, (CHUNKS, LANES), 0)


def next_chunk(block, distance=1):
    rolled = pltpu.roll(block, distance, 0)
    return jnp.where(sublane_index() >= distance, rolled, 0.0)


def strided(ref, step, run):
    return ref[pl.ds(step, CHUNKS, stride=run), :]


def added(terms):
    while len(terms) > 1:
        pairs = [terms[i] + terms[i + 1] for i in range(0, len(terms) - 1, 2)]
        terms = pairs + terms[2 * len(pairs) :]
    return terms[0]


def boundary(taps_ref, last, first):
    products = []
    for j in (1, 2):
        tap = [taps_ref[j, i : i + 1, :] for i in range(3)]
        (far, near), (zero, one) = last[j - 1], first[j - 1]
        own = (tap[0] * zero, tap[0] * one + tap[1] * zero)
        gained = (tap[1] * near + tap[2] * far, tap[2] * near)
        products.append((own, gained))
    (k_own, k_gained), (v_own, v_gained) = products
    return [k_own[i] * v_gained[i] + k_gained[i] * (v_own[i] + v_gained[i]) for i in range(2)]


def two_rows(ref, row):
    return ref[row : row + 1, :], ref[row + 1 : row + 2, :]


def pair_boundary(modes, taps_ref, lower_ref, upper_ref):
    last = [two_rows(lower_ref, modes + row) for row in (K_LAST, V_LAST)]
    first = [two_rows(upper_ref, modes + row) for row in (K_FIRST, V_FIRST)]
    return boundary(taps_ref, last, first)


def gate_gain(taps_ref, far, near):
    return taps_ref[0, 1:2, :] * near + taps_ref[0, 2:3, :] * far, taps_ref[0, 2:3, :] * near


def states_kernel(modes, *refs):
    sources, refs = refs[:6], refs[6:]
    x_hbm = sources[0]
    (rows_ref, product_ref, state_ref, q_ref), refs = refs[:4], refs[4:]
    params, refs = refs[:5], refs[5:]
    taps_ref, decays_ref = params[0], params[1]
    k_half, v_half, k_ref, v_ref, semaphores = refs
    copies = [pltpu.make_async_copy(s, d, semaphores.at[i]) for i, (s, d) in enumerate(zip(sources[1:], params))]
    streams = [
        pltpu.make_async_copy(x_hbm.at[j], d, semaphores.at[5 + j]) for j, d in enumerate((q_ref, k_half, v_half))
    ]
    for copy in (streams[1], streams[2], copies[1], copies[0], streams[0], copies[2], copies[3], copies[4]):
        copy.start()
    positions = k_ref.shape[0]
    run = positions // CHUNKS
    copies[1].wait()
    copies[0].wait()
    k_taps = [over_sublanes(taps_ref[1, i : i + 1, :]) for i in range(3)]
    v_taps = [over_sublanes(taps_ref[2, i : i + 1, :]) for i in range(3)]
    factors = [over_sublanes(jnp.exp(-decays_ref[m : m + 1, :])) for m in range(modes)]
    streams[1].wait()
    k_ref[...] = k_half[...].astype(F32)
    streams[2].wait()
    v_ref[...] = v_half[...].astype(F32)

    def step(j, carry):
        k1, k2, v1, v2, states = carry
        k0 = strided(k_ref, j, run)
        v0 = strided(v_ref, j, run)
        k = k_taps[0] * k0 + k_taps[1] * k1 + k_taps[2] * k2
        v = v_taps[0] * v0 + v_taps[1] * v1 + v_taps[2] * v2
        product = k * v
        product_ref[j] = product
        states = tuple(a * h + product for a, h in zip(factors, states))
        return k0, k1, v0, v1, states

    start = (
        next_chunk(strided(k_ref, run - 1, run)),
        next_chunk(strided(k_ref, run - 2, run)),
        next_chunk(strided(v_ref, run - 1, run)),
        next_chunk(strided(v_ref, run - 2, run)),
        tuple(jnp.zeros((CHUNKS, LANES), F32) for _ in range(modes)),
    )
    states = lax.fori_loop(0, run, step, start, unroll=8)[4]
    for m in range(modes):
        total = states[m]
        distance = 1
        while distance < CHUNKS:
            factor = over_sublanes(jnp.exp(-float(run * distance) * decays_ref[m : m + 1, :]))
            total = total + factor * next_chunk(total, distance)
            distance *= 2
        state_ref[m] = next_chunk(total)
        rows_ref[m : m + 1, :] = total[CHUNKS - 1 : CHUNKS, :]
    streams[0].wait()
    rows_ref[modes + K_LAST : modes + K_LAST + 2, :] = k_ref[positions - 2 : positions, :]
    rows_ref[modes + V_LAST : modes + V_LAST + 2, :] = v_ref[positions - 2 : positions, :]
    rows_ref[modes + Q_LAST : modes + Q_LAST + 2, :] = q_ref[positions - 16 : positions, :].astype(F32)[14:16]
    rows_ref[modes + K_FIRST : modes + K_FIRST + 2, :] = k_ref[0:2, :]
    rows_ref[modes + V_FIRST : modes + V_FIRST + 2, :] = v_ref[0:2, :]
    rows_ref[modes + V_FIRST + 2 :, :] = jnp.zeros((EXTRA - V_FIRST - 2, LANES), F32)
    for i in (2, 3, 4):
        copies[i].wait()


def join_kernel(modes, positions, axis, own_ref, other_ref, taps_ref, decays_ref, sent_ref, pair_ref):
    upper = lax.rem(lax.axis_index(axis), PAIR) == 1
    own = own_ref[...]
    other = other_ref[...]
    below = jnp.where(upper, other, own)
    above = jnp.where(upper, own, other)
    pair_ref[0] = below
    pair_ref[1] = above
    first, second = pair_boundary(modes, taps_ref, pair_ref.at[0], pair_ref.at[1])
    rates = decays_ref[...]
    state = jnp.exp(-float(positions) * rates) * below[:modes] + above[:modes]
    state = state + jnp.exp(-float(positions - 1) * rates) * first + jnp.exp(-float(positions - 2) * rates) * second
    row = lax.broadcasted_iota(jnp.int32, (EXTRA, LANES), 0)
    beside = jnp.where(row < K_FIRST, above[modes:], below[modes:])
    rows = jnp.concatenate([state, beside], 0).astype(BF16)
    sent_ref[...] = jnp.broadcast_to(rows[None], sent_ref.shape)


def local_kernel(
    modes, axis, pairs, q_half, product_ref, state_ref, pair_ref, taps_ref, decays_ref, residues_ref, skip_ref,
    gate_ref, base_ref, begin_ref, reach_ref, factor_ref, weight_ref, late_ref, q_ref,
):
    positions = q_ref.shape[0]
    run = positions // CHUNKS
    device = lax.axis_index(axis)
    pair = device // PAIR
    upper = lax.rem(device, PAIR)
    inside = upper.astype(F32)
    q_ref[...] = q_half[...].astype(F32)
    taps = [over_sublanes(taps_ref[0, i : i + 1, :]) for i in range(3)]
    skip = over_sublanes(skip_ref[...])
    rates = decays_ref[...]
    weights = residues_ref[...] * jnp.sqrt(2.0 * rates)
    factors = [over_sublanes(jnp.exp(-rates[m : m + 1, :])) for m in range(modes)]
    spread = [over_sublanes(weights[m : m + 1, :]) for m in range(modes)]

    first, second = pair_boundary(modes, taps_ref, pair_ref.at[0], pair_ref.at[1])
    first, second = first * inside, second * inside
    arrived = inside * pair_ref[0, :modes, :] + jnp.exp(rates) * first + jnp.exp(2.0 * rates) * second
    early = jnp.sum(weights * jnp.exp(rates), 0, keepdims=True) * second
    gain = gate_gain(taps_ref, *two_rows(pair_ref.at[0], modes + Q_LAST))

    def step(j, carry):
        q1, q2, states = carry
        q0 = strided(q_ref, j, run)
        gate_ref[j] = taps[0] * q0 + taps[1] * q1 + taps[2] * q2
        product = product_ref[j]
        states = tuple(a * h + product for a, h in zip(factors, states))
        base_ref[j] = added([skip * product] + [w * h for w, h in zip(spread, states)])
        return q0, q1, states

    start = (
        next_chunk(strided(q_ref, run - 1, run)),
        next_chunk(strided(q_ref, run - 2, run)),
        tuple(jnp.zeros((CHUNKS, LANES), F32) for _ in range(modes)),
    )
    lax.fori_loop(0, run, step, start, unroll=4)
    top = sublane_index() == 0
    base_gain = (skip_ref[...] * first - early, skip_ref[...] * second)
    for j in range(2):
        gate_ref[j] = gate_ref[j] + jnp.where(top, over_sublanes(gain[j] * inside), 0.0)
        base_ref[j] = base_ref[j] + jnp.where(top, over_sublanes(base_gain[j]), 0.0)

    behind = sublane_index().astype(F32) * float(run)
    for m in range(modes):
        rate = over_sublanes(rates[m : m + 1, :])
        fade = jnp.exp(-rate * behind)
        begin_ref[m] = spread[m] * (state_ref[m] + fade * over_sublanes(arrived[m : m + 1, :]))
        reach_ref[m] = spread[m] * fade * jnp.exp(-rate * (inside * float(positions)))
        factor_ref[m] = factors[m]
    length = PAIR * positions
    for e in range(pairs):
        distance = (jnp.maximum(pair - 1 - e, 0) * length).astype(F32)
        weight_ref[e] = jnp.where(e < pair, jnp.exp(-rates * distance), 0.0)
        distance = (jnp.maximum(pair - e, 0) * length - 1).astype(F32)
        late_ref[e] = jnp.where(e <= pair, jnp.exp(-rates * distance), 0.0)


def carry_kernel(
    modes, axis, received_ref, gate_ref, base_ref, begin_ref, reach_ref, factor_ref, weight_ref, late_ref,
    taps_ref, decays_ref, residues_ref, skip_ref, power_ref, gated_ref, rows_ref, first_ref, second_ref,
):
    run = gate_ref.shape[0]
    pairs = received_ref.shape[0]
    device = lax.axis_index(axis)
    pair = device // PAIR
    lower = 1.0 - lax.rem(device, PAIR).astype(F32)
    pitch = modes + EXTRA
    rows_ref[0:pitch, :] = jnp.zeros((pitch, LANES), F32)
    for slot, e in enumerate(pair_order(pairs)):
        rows_ref[pitch * (e + 1) : pitch * (e + 2), :] = received_ref[slot].astype(F32)

    def of_all(row, block):
        return tuple(rows_ref[pl.ds(pitch * block + modes + row + i, pairs, stride=pitch), :] for i in range(2))

    last = [of_all(row, 0) for row in (K_LAST, V_LAST)]
    begun = [of_all(row, 1) for row in (K_FIRST, V_FIRST)]
    first_ref[...], second_ref[...] = boundary(taps_ref, last, begun)

    rates = decays_ref[...]
    states, firsts, seconds = [], [], []
    for e in range(pairs):
        states.append(weight_ref[e] * rows_ref[pitch * (e + 1) : pitch * (e + 1) + modes, :])
        firsts.append(late_ref[e] * first_ref[e : e + 1, :])
        seconds.append(late_ref[e] * second_ref[e : e + 1, :])
    state = added(states) + added(firsts) + jnp.exp(rates) * added(seconds)

    first = first_ref[pl.ds(pair, 1), :] * lower
    second = second_ref[pl.ds(pair, 1), :] * lower
    weights = residues_ref[...] * jnp.sqrt(2.0 * rates)
    early = jnp.sum(weights * jnp.exp(rates), 0, keepdims=True) * second
    edge = [rows_ref[pl.ds(pair * pitch + modes + Q_LAST + i, 1), :] * lower for i in range(2)]
    gate_extra = gate_gain(taps_ref, *edge)
    skip = skip_ref[...]
    base_extra = (skip * first - early, skip * second)
    top = sublane_index() == 0
    factors = [factor_ref[m] for m in range(modes)]
    carried = [begin_ref[m] + reach_ref[m] * over_sublanes(state[m : m + 1, :]) for m in range(modes)]

    def step(j, carried, gate_more=None, base_more=None):
        carried = tuple(a * g for a, g in zip(factors, carried))
        gate, base = gate_ref[j], base_ref[j]
        if gate_more is not None:
            gate = gate + jnp.where(top, over_sublanes(gate_more), 0.0)
            base = base + jnp.where(top, over_sublanes(base_more), 0.0)
        gated_ref[pl.ds(j, CHUNKS, stride=run), :] = gate * added([base] + list(carried))
        return carried

    carried = tuple(carried)
    for j in range(2):
        carried = step(j, carried, gate_extra[j], base_extra[j])
    lax.fori_loop(2, run, step, carried, unroll=6)

    gated = gated_ref[...]
    square = gated * gated
    high = square.astype(BF16)
    low = (square - high.astype(F32)).astype(BF16)
    ones = jnp.ones((LANES, LANES), BF16)
    sums = jnp.dot(high, ones, preferred_element_type=F32) + jnp.dot(low, ones, preferred_element_type=F32)
    lane = lax.broadcasted_iota(jnp.int32, (CHUNKS, LANES), 1)
    power = jnp.zeros((CHUNKS, LANES), F32)
    for i in range(run):
        power = jnp.where(lane == i, sums[i * CHUNKS : (i + 1) * CHUNKS, :], power)
    power_ref[...] = jnp.broadcast_to(power[None], power_ref.shape)


def finish_kernel(channels, power_ref, gated_ref, gain_ref, mixed_ref):
    run = gated_ref.shape[0] // CHUNKS
    inverse = lax.rsqrt(jnp.sum(power_ref[...], 0) / channels + 1e-05)
    gain = over_sublanes(gain_ref[...])
    for i in range(0, run, 2):
        halves = [
            gated_ref[(i + h) * CHUNKS : (i + h + 1) * CHUNKS, :] * gain * inverse[:, i + h : i + h + 1] for h in range(2)
        ]
        mixed_ref[i * CHUNKS : (i + 2) * CHUNKS, :] = jnp.concatenate(halves, 0).astype(BF16)


def per_device(projections, short_filter, residues, decays, skip, gain):
    positions, _, width = projections.shape
    modes = decays.shape[0]
    ctx_count = lax.axis_size("ctx")
    tp_count = lax.axis_size("tp")
    pairs = ctx_count // PAIR
    run = positions // CHUNKS
    x = jnp.swapaxes(projections, 0, 1)

    def shape(*extent, kind=F32):
        return jax.ShapeDtypeStruct(extent, kind)

    def call(kernel, name, out_shape, in_specs, scratch, *operands):
        return pl.pallas_call(
            kernel,
            out_shape=out_shape,
            in_specs=in_specs,
            out_specs=jax.tree.map(lambda _: VMEM, out_shape),
            scratch_shapes=scratch,
            compiler_params=pltpu.CompilerParams(vmem_limit_bytes=VMEM_LIMIT),
            name=name,
        )(*operands)

    block = shape(run, CHUNKS, width)
    table = shape(modes, CHUNKS, width)
    sources = (x, short_filter, decays, residues, skip[None, :], gain[None, :])
    rows, product, state, q, short_filter, decays, residues, skip, gain = call(
        functools.partial(states_kernel, modes),
        "states",
        (shape(modes + EXTRA, width), block, table, shape(positions, width, kind=BF16))
        + tuple(shape(*s.shape) for s in sources[1:]),
        [ANY] * 6,
        [
            pltpu.VMEM((positions, width), BF16),
            pltpu.VMEM((positions, width), BF16),
            pltpu.VMEM((positions, width), F32),
            pltpu.VMEM((positions, width), F32),
            pltpu.SemaphoreType.DMA((8,)),
        ],
        *[pltpu.with_memory_space_constraint(s, pltpu.HBM) for s in sources],
    )
    other = lax.ppermute(rows, "ctx", [(i, i + 1 - 2 * (i % PAIR)) for i in range(ctx_count)])
    sent, joined = call(
        functools.partial(join_kernel, modes, positions, "ctx"),
        "join",
        (shape(pairs, modes + EXTRA, width, kind=BF16), shape(PAIR, modes + EXTRA, width)),
        [VMEM] * 4,
        [],
        rows,
        other,
        short_filter,
        decays,
    )
    groups = [[PAIR * i + h for i in pair_order(pairs)] for h in range(PAIR)]
    received = lax.all_to_all(sent, "ctx", split_axis=0, concat_axis=0, tiled=True, axis_index_groups=groups)

    gate, base, begin, reach, factor, weight, late = call(
        functools.partial(local_kernel, modes, "ctx", pairs),
        "local",
        (block, block, table, table, table, shape(pairs, modes, width), shape(pairs, modes, width)),
        [VMEM] * 8,
        [pltpu.VMEM((positions, width), F32)],
        q,
        product,
        state,
        joined,
        short_filter,
        decays,
        residues,
        skip,
    )
    power, gated = call(
        functools.partial(carry_kernel, modes, "ctx"),
        "carry",
        (shape(tp_count, CHUNKS, run), shape(positions, width)),
        [VMEM] * 12,
        [
            pltpu.VMEM(((pairs + 1) * (modes + EXTRA), width), F32),
            pltpu.VMEM((pairs, width), F32),
            pltpu.VMEM((pairs, width), F32),
        ],
        received,
        gate,
        base,
        begin,
        reach,
        factor,
        weight,
        late,
        short_filter,
        decays,
        residues,
        skip,
    )
    powers = lax.all_to_all(
        power, "tp", split_axis=0, concat_axis=0, tiled=True, axis_index_groups=[slice_order(tp_count)]
    )
    return call(
        functools.partial(finish_kernel, width * tp_count),
        "finish",
        shape(positions, width, kind=BF16),
        [VMEM] * 3,
        [],
        powers,
        gated,
        gain,
    )


def solution(mesh):
    in_specs = (
        P("ctx", None, "tp"),
        P(None, None, "tp"),
        P(None, "tp"),
        P(None, "tp"),
        P("tp"),
        P("tp"),
    )
    return jax.shard_map(per_device, mesh=mesh, in_specs=in_specs, out_specs=P("ctx", "tp"), check_vma=False)
```

```python
import functools

import jax
import jax.numpy as jnp
from jax import lax
from jax.experimental import pallas as pl
from jax.experimental.pallas import tpu as pltpu
from jax.sharding import PartitionSpec as P

F32 = jnp.float32
BF16 = jnp.bfloat16
CHUNKS = 8
LANES = 128
PAIR = 2
VMEM_LIMIT = 40 * 1024 * 1024
VMEM = pl.BlockSpec(memory_space=pltpu.VMEM)
ANY = pl.BlockSpec(memory_space=pl.ANY)

FIRST_PAIR = 10
FIRST_SLICE = 5
GRID = 4
PITCH = 137
SPAN = 136

K_LAST, V_LAST, Q_LAST, K_FIRST, V_FIRST = 0, 2, 4, 6, 8
EXTRA = 16


def first_then(first, members, distance):
    return [first] + sorted((i for i in range(members) if i != first), key=lambda i: -distance(i, first))


def around(a, b, size):
    return min((a - b) % size, (b - a) % size)


def pair_order(pairs):
    def distance(a, b):
        return around(a // GRID, b // GRID, max(pairs // GRID, 1)) + 2 * around(a % GRID, b % GRID, GRID)

    return first_then(FIRST_PAIR % pairs, pairs, distance)


def slice_order(slices):
    return first_then(FIRST_SLICE % slices, slices, lambda a, b: 0)


def over_sublanes(row):
    return jnp.broadcast_to(row, (CHUNKS, LANES))


def sublane_index():
    return lax.broadcasted_iota(jnp.int32, (CHUNKS, LANES), 0)


def next_chunk(block, distance=1):
    rolled = pltpu.roll(block, distance, 0)
    return jnp.where(sublane_index() >= distance, rolled, 0.0)


def strided(ref, step, run):
    return ref[pl.ds(step, CHUNKS, stride=run), :]


def added(terms):
    while len(terms) > 1:
        pairs = [terms[i] + terms[i + 1] for i in range(0, len(terms) - 1, 2)]
        terms = pairs + terms[2 * len(pairs) :]
    return terms[0]


def boundary(taps_ref, last, first):
    products = []
    for j in (1, 2):
        tap = [taps_ref[j, i : i + 1, :] for i in range(3)]
        (far, near), (zero, one) = last[j - 1], first[j - 1]
        own = (tap[0] * zero, tap[0] * one + tap[1] * zero)
        gained = (tap[1] * near + tap[2] * far, tap[2] * near)
        products.append((own, gained))
    (k_own, k_gained), (v_own, v_gained) = products
    return [k_own[i] * v_gained[i] + k_gained[i] * (v_own[i] + v_gained[i]) for i in range(2)]


def two_rows(ref, row):
    return ref[row : row + 1, :], ref[row + 1 : row + 2, :]


def pair_boundary(modes, taps_ref, lower_ref, upper_ref):
    last = [two_rows(lower_ref, modes + row) for row in (K_LAST, V_LAST)]
    first = [two_rows(upper_ref, modes + row) for row in (K_FIRST, V_FIRST)]
    return boundary(taps_ref, last, first)


def states_kernel(modes, *refs):
    sources, refs = refs[:6], refs[6:]
    x_hbm = sources[0]
    (rows_ref, product_ref, state_ref, q_ref), refs = refs[:4], refs[4:]
    params, refs = refs[:5], refs[5:]
    taps_ref, decays_ref = params[0], params[1]
    k_half, v_half, k_ref, v_ref, jump_ref, semaphores = refs
    copies = [pltpu.make_async_copy(s, d, semaphores.at[i]) for i, (s, d) in enumerate(zip(sources[1:], params))]
    streams = [
        pltpu.make_async_copy(x_hbm.at[j], d, semaphores.at[5 + j]) for j, d in enumerate((q_ref, k_half, v_half))
    ]
    for copy in (streams[1], streams[2], copies[1], copies[0], streams[0], copies[2], copies[3], copies[4]):
        copy.start()
    positions = q_ref.shape[0]
    run = positions // CHUNKS
    copies[1].wait()
    copies[0].wait()
    k_taps = [over_sublanes(taps_ref[1, i : i + 1, :]) for i in range(3)]
    v_taps = [over_sublanes(taps_ref[2, i : i + 1, :]) for i in range(3)]
    rates = decays_ref[...]
    factor = jnp.exp(-rates)
    factors = [over_sublanes(factor[m : m + 1, :]) for m in range(modes)]
    for i in range(3):
        jump_ref[i] = jnp.exp(-float(run << i) * rates)
    streams[1].wait()
    for s in range(CHUNKS):
        k_ref[s * PITCH : s * PITCH + run, :] = k_half[s * run : (s + 1) * run, :].astype(F32)
    streams[2].wait()
    for s in range(CHUNKS):
        v_ref[s * PITCH : s * PITCH + run, :] = v_half[s * run : (s + 1) * run, :].astype(F32)

    def step(j, carry):
        k1, k2, v1, v2, states = carry
        k0 = strided(k_ref, j, PITCH)
        v0 = strided(v_ref, j, PITCH)
        k = k_taps[0] * k0 + k_taps[1] * k1 + k_taps[2] * k2
        v = v_taps[0] * v0 + v_taps[1] * v1 + v_taps[2] * v2
        product = k * v
        product_ref[j] = product
        states = tuple(a * h + product for a, h in zip(factors, states))
        return k0, k1, v0, v1, states

    start = (
        next_chunk(strided(k_ref, run - 1, PITCH)),
        next_chunk(strided(k_ref, run - 2, PITCH)),
        next_chunk(strided(v_ref, run - 1, PITCH)),
        next_chunk(strided(v_ref, run - 2, PITCH)),
        tuple(jnp.zeros((CHUNKS, LANES), F32) for _ in range(modes)),
    )
    states = lax.fori_loop(0, run, step, start, unroll=16)[4]
    for m in range(modes):
        total = states[m]
        for i in range(3):
            total = total + over_sublanes(jump_ref[i, m : m + 1, :]) * next_chunk(total, 1 << i)
        state_ref[m] = next_chunk(total)
        rows_ref[m : m + 1, :] = total[CHUNKS - 1 : CHUNKS, :]
    streams[0].wait()
    rows_ref[modes + K_LAST : modes + K_LAST + 2, :] = k_ref[7 * PITCH + run - 2 : 7 * PITCH + run, :]
    rows_ref[modes + V_LAST : modes + V_LAST + 2, :] = v_ref[7 * PITCH + run - 2 : 7 * PITCH + run, :]
    rows_ref[modes + Q_LAST : modes + Q_LAST + 2, :] = q_ref[positions - 16 : positions, :].astype(F32)[14:16]
    rows_ref[modes + K_FIRST : modes + K_FIRST + 2, :] = k_ref[0:2, :]
    rows_ref[modes + V_FIRST : modes + V_FIRST + 2, :] = v_ref[0:2, :]
    rows_ref[modes + V_FIRST + 2 :, :] = jnp.zeros((EXTRA - V_FIRST - 2, LANES), F32)
    for i in (2, 3, 4):
        copies[i].wait()


def starts_early(axis):
    pair = lax.axis_index(axis) // PAIR
    y, z = pair // GRID, lax.rem(pair, GRID)
    return jnp.logical_or(z < 1, jnp.logical_and(z < 2, y < 2))


def mode_weights(decays_ref, residues_ref):
    return residues_ref[...] * jnp.sqrt(2.0 * decays_ref[...])


def edge_gains(taps_ref, skip_ref, rates, weights, first, second, far, near):
    early = jnp.sum(weights * jnp.exp(rates), 0, keepdims=True) * second
    skip = skip_ref[...]
    gate = (taps_ref[0, 1:2, :] * near + taps_ref[0, 2:3, :] * far, taps_ref[0, 2:3, :] * near)
    return gate, (skip * first - early, skip * second)


def from_lower(modes, axis, pair_ref, taps_ref, decays_ref, residues_ref, skip_ref):
    inside = lax.rem(lax.axis_index(axis), PAIR).astype(F32)
    rates = decays_ref[...]
    first, second = (inside * p for p in pair_boundary(modes, taps_ref, pair_ref.at[0], pair_ref.at[1]))
    state = inside * pair_ref[0, :modes, :] + jnp.exp(rates) * first + jnp.exp(2.0 * rates) * second
    far, near = (inside * row for row in two_rows(pair_ref.at[0], modes + Q_LAST))
    weights = mode_weights(decays_ref, residues_ref)
    return state, *edge_gains(taps_ref, skip_ref, rates, weights, first, second, far, near)


def at_top(block, row):
    return block + jnp.where(sublane_index() == 0, over_sublanes(row), 0.0)


def fades(decays_ref, run, m):
    return jnp.exp(over_sublanes(decays_ref[m : m + 1, :]) * (sublane_index().astype(F32) * -float(run)))


def load_gate(q_ref, q_half, taps_ref):
    run = q_half.shape[0] // CHUNKS
    for s in range(CHUNKS):
        q_ref[s * PITCH : s * PITCH + run, :] = q_half[s * run : (s + 1) * run, :].astype(F32)
    taps = [over_sublanes(taps_ref[0, i : i + 1, :]) for i in range(3)]
    return taps, [next_chunk(strided(q_ref, run - 1 - i, PITCH)) for i in range(2)]


def split(table):
    return [over_sublanes(table[m : m + 1, :]) for m in range(table.shape[0])]


def local_work(
    modes, axis, q_half, product_ref, state_ref, pair_ref, taps_ref, decays_ref, residues_ref, skip_ref,
    gate_ref, base_ref, begin_ref, reach_ref, q_ref,
):
    run = product_ref.shape[0]
    positions = run * CHUNKS
    inside = lax.rem(lax.axis_index(axis), PAIR).astype(F32)
    rates = decays_ref[...]
    spread = split(mode_weights(decays_ref, residues_ref))
    factors = split(jnp.exp(-rates))
    skip = over_sublanes(skip_ref[...])
    taps, before = load_gate(q_ref, q_half, taps_ref)

    def step(j, carry):
        q1, q2, states = carry
        q0 = strided(q_ref, j, PITCH)
        gate_ref[j] = taps[0] * q0 + taps[1] * q1 + taps[2] * q2
        product = product_ref[j]
        states = tuple(a * h + product for a, h in zip(factors, states))
        base_ref[j] = added([skip * product] + [w * h for w, h in zip(spread, states)])
        return q0, q1, states

    start = (*before, tuple(jnp.zeros((CHUNKS, LANES), F32) for _ in range(modes)))
    lax.fori_loop(0, run, step, start, unroll=4)

    arrived, gate_gain, base_gain = from_lower(modes, axis, pair_ref, taps_ref, decays_ref, residues_ref, skip_ref)
    for j in range(2):
        gate_ref[j] = at_top(gate_ref[j], gate_gain[j])
        base_ref[j] = at_top(base_ref[j], base_gain[j])
    across = jnp.exp(-rates * (inside * float(positions)))
    for m in range(modes):
        fade = fades(decays_ref, run, m)
        begin_ref[m] = spread[m] * (state_ref[m] + fade * over_sublanes(arrived[m : m + 1, :]))
        reach_ref[m] = spread[m] * fade * over_sublanes(across[m : m + 1, :])


def join_kernel(
    modes, axis, own_ref, other_ref, q_half, product_ref, state_ref, taps_ref, decays_ref, residues_ref, skip_ref,
    sent_ref, pair_ref, *refs,
):
    positions = q_half.shape[0]
    upper = lax.rem(lax.axis_index(axis), PAIR) == 1
    own = own_ref[...]
    other = other_ref[...]
    below = jnp.where(upper, other, own)
    above = jnp.where(upper, own, other)
    pair_ref[0] = below
    pair_ref[1] = above
    first, second = pair_boundary(modes, taps_ref, pair_ref.at[0], pair_ref.at[1])
    rates = decays_ref[...]
    state = jnp.exp(-float(positions) * rates) * below[:modes] + above[:modes]
    state = state + jnp.exp(-float(positions - 1) * rates) * first + jnp.exp(-float(positions - 2) * rates) * second
    row = lax.broadcasted_iota(jnp.int32, (EXTRA, LANES), 0)
    beside = jnp.where(row < K_FIRST, above[modes:], below[modes:])
    rows = jnp.concatenate([state, beside], 0).astype(BF16)
    sent_ref[...] = jnp.broadcast_to(rows[None], sent_ref.shape)

    @pl.when(starts_early(axis))
    def _():
        params = (taps_ref, decays_ref, residues_ref, skip_ref)
        local_work(modes, axis, q_half, product_ref, state_ref, pair_ref, *params, *refs)


def carry_kernel(
    modes, axis, received_ref, gate_ref, base_ref, begin_ref, reach_ref, q_half, product_ref, state_ref, pair_ref,
    taps_ref, decays_ref, residues_ref, skip_ref, power_ref, gated_ref, rows_ref, first_ref, second_ref, q_ref,
):
    run = product_ref.shape[0]
    positions = run * CHUNKS
    pairs = received_ref.shape[0]
    device = lax.axis_index(axis)
    pair = device // PAIR
    inside = lax.rem(device, PAIR).astype(F32)
    pitch = modes + EXTRA
    rows_ref[0:pitch, :] = jnp.zeros((pitch, LANES), F32)
    for slot, e in enumerate(pair_order(pairs)):
        rows_ref[pitch * (e + 1) : pitch * (e + 2), :] = received_ref[slot].astype(F32)

    def of_all(row, block):
        return tuple(rows_ref[pl.ds(pitch * block + modes + row + i, pairs, stride=pitch), :] for i in range(2))

    last = [of_all(row, 0) for row in (K_LAST, V_LAST)]
    begun = [of_all(row, 1) for row in (K_FIRST, V_FIRST)]
    first_ref[...], second_ref[...] = boundary(taps_ref, last, begun)

    rates = decays_ref[...]
    length = PAIR * positions
    across = jnp.exp(-float(length) * rates)
    late_first = jnp.exp(-float(length - 1) * rates)
    late_second = jnp.exp(-float(length - 2) * rates)
    state = jnp.zeros((modes, LANES), F32)
    for e in range(pairs - 1):
        sent = rows_ref[pitch * (e + 1) : pitch * (e + 1) + modes, :]
        sent = sent + late_first * first_ref[e : e + 1, :] + late_second * second_ref[e : e + 1, :]
        state = jnp.where(e < pair, across * state + sent, state)
    first, second = first_ref[pl.ds(pair, 1), :], second_ref[pl.ds(pair, 1), :]
    state = state + jnp.exp(rates) * first + jnp.exp(2.0 * rates) * second

    weights = mode_weights(decays_ref, residues_ref)
    lower = 1.0 - inside
    far, near = (lower * rows_ref[pl.ds(pair * pitch + modes + Q_LAST + i, 1), :] for i in range(2))
    gate_more, base_more = edge_gains(taps_ref, skip_ref, rates, weights, lower * first, lower * second, far, near)
    factors = split(jnp.exp(-rates))

    def put(j, gate, base, terms, more):
        if more is not None:
            gate, base = at_top(gate, more[0]), at_top(base, more[1])
        gated_ref[pl.ds(j, CHUNKS, stride=SPAN), :] = gate * added([base] + terms)

    def over_steps(step, held, gains, unroll):
        for j in range(2):
            held = step(j, held, (gains[0][j], gains[1][j]))
        lax.fori_loop(2, run, lambda j, held: step(j, held, None), held, unroll=unroll)

    @pl.when(starts_early(axis))
    def _():
        def step(j, carried, more):
            carried = tuple(a * g for a, g in zip(factors, carried))
            put(j, gate_ref[j], base_ref[j], list(carried), more)
            return carried

        carried = tuple(begin_ref[m] + reach_ref[m] * over_sublanes(state[m : m + 1, :]) for m in range(modes))
        over_steps(step, carried, (gate_more, base_more), 14)

    @pl.when(jnp.logical_not(starts_early(axis)))
    def _():
        taps, before = load_gate(q_ref, q_half, taps_ref)
        skip = over_sublanes(skip_ref[...])
        spread = split(weights)
        arrived, gate_gain, base_gain = from_lower(modes, axis, pair_ref, taps_ref, decays_ref, residues_ref, skip_ref)
        arrived = arrived + jnp.exp(-rates * (inside * float(positions))) * state
        states = tuple(
            state_ref[m] + fades(decays_ref, run, m) * over_sublanes(arrived[m : m + 1, :]) for m in range(modes)
        )

        def step(j, held, more):
            q1, q2, states = held
            q0 = strided(q_ref, j, PITCH)
            product = product_ref[j]
            states = tuple(a * h + product for a, h in zip(factors, states))
            gate = taps[0] * q0 + taps[1] * q1 + taps[2] * q2
            put(j, gate, skip * product, [w * h for w, h in zip(spread, states)], more)
            return q0, q1, states

        gains = tuple([a + b for a, b in zip(*both)] for both in ((gate_gain, gate_more), (base_gain, base_more)))
        over_steps(step, (*before, states), gains, 6)

    ones = jnp.ones((LANES, LANES), BF16)
    lane = lax.broadcasted_iota(jnp.int32, (CHUNKS, LANES), 1)
    power = jnp.zeros((CHUNKS, LANES), F32)
    tiles = run // CHUNKS
    for s in range(CHUNKS):
        gated = gated_ref[s * SPAN : s * SPAN + run, :]
        square = gated * gated
        high = square.astype(BF16)
        low = (square - high.astype(F32)).astype(BF16)
        sums = jnp.dot(high, ones, preferred_element_type=F32) + jnp.dot(low, ones, preferred_element_type=F32)
        for i in range(tiles):
            power = jnp.where(lane == s * tiles + i, sums[i * CHUNKS : (i + 1) * CHUNKS, :], power)
    power_ref[...] = jnp.broadcast_to(power[None], power_ref.shape)


def finish_kernel(channels, power_ref, gated_ref, gain_ref, mixed_ref):
    run = mixed_ref.shape[0] // CHUNKS
    tiles = run // CHUNKS
    inverse = lax.rsqrt(jnp.sum(power_ref[...], 0) / channels + 1e-05)
    gain = over_sublanes(gain_ref[...])
    for s in range(CHUNKS):
        for i in range(0, tiles, 2):
            halves = []
            for h in (i, i + 1):
                gated = gated_ref[s * SPAN + h * CHUNKS : s * SPAN + (h + 1) * CHUNKS, :]
                halves.append(gated * gain * inverse[:, s * tiles + h : s * tiles + h + 1])
            mixed_ref[s * run + i * CHUNKS : s * run + (i + 2) * CHUNKS, :] = jnp.concatenate(halves, 0).astype(BF16)


def per_device(projections, short_filter, residues, decays, skip, gain):
    positions, _, width = projections.shape
    modes = decays.shape[0]
    ctx_count = lax.axis_size("ctx")
    tp_count = lax.axis_size("tp")
    pairs = ctx_count // PAIR
    run = positions // CHUNKS
    x = jnp.swapaxes(projections, 0, 1)

    def shape(*extent, kind=F32):
        return jax.ShapeDtypeStruct(extent, kind)

    def call(kernel, name, out_shape, in_specs, scratch, *operands):
        return pl.pallas_call(
            kernel,
            out_shape=out_shape,
            in_specs=in_specs,
            out_specs=jax.tree.map(lambda _: VMEM, out_shape),
            scratch_shapes=scratch,
            compiler_params=pltpu.CompilerParams(vmem_limit_bytes=VMEM_LIMIT),
            name=name,
        )(*operands)

    block = shape(run, CHUNKS, width)
    table = shape(modes, CHUNKS, width)
    sources = (x, short_filter, decays, residues, skip[None, :], gain[None, :])
    rows, product, state, q, short_filter, decays, residues, skip, gain = call(
        functools.partial(states_kernel, modes),
        "states",
        (shape(modes + EXTRA, width), block, table, shape(positions, width, kind=BF16))
        + tuple(shape(*s.shape) for s in sources[1:]),
        [ANY] * 6,
        [
            pltpu.VMEM((positions, width), BF16),
            pltpu.VMEM((positions, width), BF16),
            pltpu.VMEM((PITCH * CHUNKS, width), F32),
            pltpu.VMEM((PITCH * CHUNKS, width), F32),
            pltpu.VMEM((3, modes, width), F32),
            pltpu.SemaphoreType.DMA((8,)),
        ],
        *[pltpu.with_memory_space_constraint(s, pltpu.HBM) for s in sources],
    )
    other = lax.ppermute(rows, "ctx", [(i, i + 1 - 2 * (i % PAIR)) for i in range(ctx_count)])
    params = (short_filter, decays, residues, skip)
    pitched = pltpu.VMEM((PITCH * CHUNKS, width), F32)
    sent, joined, gate, base, begin, reach = call(
        functools.partial(join_kernel, modes, "ctx"),
        "join",
        (shape(pairs, modes + EXTRA, width, kind=BF16), shape(PAIR, modes + EXTRA, width), block, block, table, table),
        [VMEM] * 9,
        [pitched],
        rows,
        other,
        q,
        product,
        state,
        *params,
    )
    groups = [[PAIR * i + h for i in pair_order(pairs)] for h in range(PAIR)]
    received = lax.all_to_all(sent, "ctx", split_axis=0, concat_axis=0, tiled=True, axis_index_groups=groups)

    power, gated = call(
        functools.partial(carry_kernel, modes, "ctx"),
        "carry",
        (shape(tp_count, CHUNKS, run), shape(SPAN * CHUNKS, width)),
        [VMEM] * 13,
        [
            pltpu.VMEM(((pairs + 1) * (modes + EXTRA), width), F32),
            pltpu.VMEM((pairs, width), F32),
            pltpu.VMEM((pairs, width), F32),
            pitched,
        ],
        received,
        gate,
        base,
        begin,
        reach,
        q,
        product,
        state,
        joined,
        *params,
    )
    powers = lax.all_to_all(
        power, "tp", split_axis=0, concat_axis=0, tiled=True, axis_index_groups=[slice_order(tp_count)]
    )
    return call(
        functools.partial(finish_kernel, width * tp_count),
        "finish",
        shape(positions, width, kind=BF16),
        [VMEM] * 3,
        [],
        powers,
        gated,
        gain,
    )


def solution(mesh):
    in_specs = (
        P("ctx", None, "tp"),
        P(None, None, "tp"),
        P(None, "tp"),
        P(None, "tp"),
        P("tp"),
        P("tp"),
    )
    return jax.shard_map(per_device, mesh=mesh, in_specs=in_specs, out_specs=P("ctx", "tp"), check_vma=False)
```

```python
import functools

import jax
import jax.numpy as jnp
from jax import lax
from jax.experimental import pallas as pl
from jax.experimental.pallas import tpu as pltpu
from jax.sharding import PartitionSpec as P

F32 = jnp.float32
BF16 = jnp.bfloat16
CHUNKS = 8
LANES = 128
PAIR = 2
VMEM_LIMIT = 40 * 1024 * 1024
VMEM = pl.BlockSpec(memory_space=pltpu.VMEM)
ANY = pl.BlockSpec(memory_space=pl.ANY)

FIRST_PAIR = 10
FIRST_SLICE = 5
GRID = 4
PITCH = 137
SPAN = 136

K_LAST, V_LAST, Q_LAST, K_FIRST, V_FIRST = 0, 2, 4, 6, 8
EXTRA = 16
EDGE = 8


def first_then(first, members, distance):
    return [first] + sorted((i for i in range(members) if i != first), key=lambda i: -distance(i, first))


def around(a, b, size):
    return min((a - b) % size, (b - a) % size)


def pair_order(pairs):
    def distance(a, b):
        return around(a // GRID, b // GRID, max(pairs // GRID, 1)) + 2 * around(a % GRID, b % GRID, GRID)

    return first_then(FIRST_PAIR % pairs, pairs, distance)


def ctx_groups(pairs, slices):
    def index(pair, half, piece):
        return (pair * PAIR + half) * slices + piece

    groups = [[index(p, PAIR - 1, piece) for p in pair_order(pairs)] for piece in range(slices)]
    rest = [(p % GRID, p // GRID // 2, -index(p, 0, piece)) for p in range(pairs) for piece in range(slices)]
    rest = [-i for *_, i in sorted(rest)]
    return groups + [rest[i : i + pairs] for i in range(0, len(rest), pairs)]


def slice_order(slices):
    return first_then(FIRST_SLICE % slices, slices, lambda a, b: 0)


def over_sublanes(row):
    return jnp.broadcast_to(row, (CHUNKS, LANES))


def sublane_index():
    return lax.broadcasted_iota(jnp.int32, (CHUNKS, LANES), 0)


def next_chunk(block, distance=1):
    rolled = pltpu.roll(block, distance, 0)
    return jnp.where(sublane_index() >= distance, rolled, 0.0)


def strided(ref, step, run):
    return ref[pl.ds(step, CHUNKS, stride=run), :]


def added(terms):
    while len(terms) > 1:
        pairs = [terms[i] + terms[i + 1] for i in range(0, len(terms) - 1, 2)]
        terms = pairs + terms[2 * len(pairs) :]
    return terms[0]


def boundary(taps_ref, last, first):
    products = []
    for j in (1, 2):
        tap = [taps_ref[j, i : i + 1, :] for i in range(3)]
        (far, near), (zero, one) = last[j - 1], first[j - 1]
        own = (tap[0] * zero, tap[0] * one + tap[1] * zero)
        gained = (tap[1] * near + tap[2] * far, tap[2] * near)
        products.append((own, gained))
    (k_own, k_gained), (v_own, v_gained) = products
    return [k_own[i] * v_gained[i] + k_gained[i] * (v_own[i] + v_gained[i]) for i in range(2)]


def two_rows(ref, row):
    return ref[row : row + 1, :], ref[row + 1 : row + 2, :]


def pair_boundary(modes, taps_ref, lower_ref, upper_ref):
    last = [two_rows(lower_ref, modes + row) for row in (K_LAST, V_LAST)]
    first = [two_rows(upper_ref, modes + row) for row in (K_FIRST, V_FIRST)]
    return boundary(taps_ref, last, first)


def states_kernel(modes, *refs):
    sources, refs = refs[:6], refs[6:]
    x_hbm = sources[0]
    (rows_ref, product_ref, state_ref, q_ref), refs = refs[:4], refs[4:]
    params, refs = refs[:5], refs[5:]
    taps_ref, decays_ref = params[0], params[1]
    k_half, v_half, k_ref, v_ref, jump_ref, semaphores = refs
    copies = [pltpu.make_async_copy(s, d, semaphores.at[i]) for i, (s, d) in enumerate(zip(sources[1:], params))]
    streams = [
        pltpu.make_async_copy(x_hbm.at[j], d, semaphores.at[5 + j]) for j, d in enumerate((q_ref, k_half, v_half))
    ]
    for copy in (streams[1], streams[2], copies[1], copies[0], streams[0], copies[2], copies[3], copies[4]):
        copy.start()
    positions = q_ref.shape[0]
    run = positions // CHUNKS
    copies[1].wait()
    copies[0].wait()
    k_taps = [over_sublanes(taps_ref[1, i : i + 1, :]) for i in range(3)]
    v_taps = [over_sublanes(taps_ref[2, i : i + 1, :]) for i in range(3)]
    rates = decays_ref[...]
    factor = jnp.exp(-rates)
    factors = [over_sublanes(factor[m : m + 1, :]) for m in range(modes)]
    for i in range(3):
        jump_ref[i] = jnp.exp(-float(run << i) * rates)
    streams[1].wait()
    for s in range(CHUNKS):
        k_ref[s * PITCH : s * PITCH + run, :] = k_half[s * run : (s + 1) * run, :].astype(F32)
    streams[2].wait()
    for s in range(CHUNKS):
        v_ref[s * PITCH : s * PITCH + run, :] = v_half[s * run : (s + 1) * run, :].astype(F32)

    def step(j, carry):
        k1, k2, v1, v2, states = carry
        k0 = strided(k_ref, j, PITCH)
        v0 = strided(v_ref, j, PITCH)
        k = k_taps[0] * k0 + k_taps[1] * k1 + k_taps[2] * k2
        v = v_taps[0] * v0 + v_taps[1] * v1 + v_taps[2] * v2
        product = k * v
        product_ref[j] = product
        states = tuple(a * h + product for a, h in zip(factors, states))
        return k0, k1, v0, v1, states

    start = (
        next_chunk(strided(k_ref, run - 1, PITCH)),
        next_chunk(strided(k_ref, run - 2, PITCH)),
        next_chunk(strided(v_ref, run - 1, PITCH)),
        next_chunk(strided(v_ref, run - 2, PITCH)),
        tuple(jnp.zeros((CHUNKS, LANES), F32) for _ in range(modes)),
    )
    states = lax.fori_loop(0, run, step, start, unroll=16)[4]
    for m in range(modes):
        total = states[m]
        for i in range(3):
            total = total + over_sublanes(jump_ref[i, m : m + 1, :]) * next_chunk(total, 1 << i)
        state_ref[m] = next_chunk(total)
        rows_ref[m : m + 1, :] = total[CHUNKS - 1 : CHUNKS, :]
    streams[0].wait()
    rows_ref[modes + K_LAST : modes + K_LAST + 2, :] = k_ref[7 * PITCH + run - 2 : 7 * PITCH + run, :]
    rows_ref[modes + V_LAST : modes + V_LAST + 2, :] = v_ref[7 * PITCH + run - 2 : 7 * PITCH + run, :]
    rows_ref[modes + Q_LAST : modes + Q_LAST + 2, :] = q_ref[positions - 16 : positions, :].astype(F32)[14:16]
    rows_ref[modes + K_FIRST : modes + K_FIRST + 2, :] = k_ref[0:2, :]
    rows_ref[modes + V_FIRST : modes + V_FIRST + 2, :] = v_ref[0:2, :]
    rows_ref[modes + V_FIRST + 2 :, :] = jnp.zeros((EXTRA - V_FIRST - 2, LANES), F32)
    for i in (2, 3, 4):
        copies[i].wait()


def starts_early(axis):
    pair = lax.axis_index(axis) // PAIR
    y, z = pair // GRID, lax.rem(pair, GRID)
    return jnp.logical_or(z < 1, jnp.logical_and(z < 2, y < 2))


def mode_weights(decays_ref, residues_ref):
    return residues_ref[...] * jnp.sqrt(2.0 * decays_ref[...])


def edge_gains(taps_ref, skip_ref, rates, weights, first, second, far, near):
    early = jnp.sum(weights * jnp.exp(rates), 0, keepdims=True) * second
    skip = skip_ref[...]
    gate = (taps_ref[0, 1:2, :] * near + taps_ref[0, 2:3, :] * far, taps_ref[0, 2:3, :] * near)
    return gate, (skip * first - early, skip * second)


def from_lower(modes, axis, pair_ref, taps_ref, decays_ref, residues_ref, skip_ref):
    inside = lax.rem(lax.axis_index(axis), PAIR).astype(F32)
    rates = decays_ref[...]
    first, second = (inside * p for p in pair_boundary(modes, taps_ref, pair_ref.at[0], pair_ref.at[1]))
    state = inside * pair_ref[0, :modes, :] + jnp.exp(rates) * first + jnp.exp(2.0 * rates) * second
    far, near = (inside * row for row in two_rows(pair_ref.at[0], modes + Q_LAST))
    weights = mode_weights(decays_ref, residues_ref)
    return state, *edge_gains(taps_ref, skip_ref, rates, weights, first, second, far, near)


def at_top(block, row):
    return block + jnp.where(sublane_index() == 0, over_sublanes(row), 0.0)


def fades(decays_ref, run, m):
    return jnp.exp(over_sublanes(decays_ref[m : m + 1, :]) * (sublane_index().astype(F32) * -float(run)))


def load_gate(q_ref, q_half, taps_ref):
    run = q_half.shape[0] // CHUNKS
    for s in range(CHUNKS):
        q_ref[s * PITCH : s * PITCH + run, :] = q_half[s * run : (s + 1) * run, :].astype(F32)
    taps = [over_sublanes(taps_ref[0, i : i + 1, :]) for i in range(3)]
    return taps, [next_chunk(strided(q_ref, run - 1 - i, PITCH)) for i in range(2)]


def split(table):
    return [over_sublanes(table[m : m + 1, :]) for m in range(table.shape[0])]


def local_work(
    modes, axis, q_half, product_ref, state_ref, pair_ref, taps_ref, decays_ref, residues_ref, skip_ref,
    gate_ref, base_ref, begin_ref, reach_ref, q_ref,
):
    run = product_ref.shape[0]
    positions = run * CHUNKS
    inside = lax.rem(lax.axis_index(axis), PAIR).astype(F32)
    rates = decays_ref[...]
    spread = split(mode_weights(decays_ref, residues_ref))
    factors = split(jnp.exp(-rates))
    skip = over_sublanes(skip_ref[...])
    taps, before = load_gate(q_ref, q_half, taps_ref)

    def step(j, carry):
        q1, q2, states = carry
        q0 = strided(q_ref, j, PITCH)
        gate_ref[j] = taps[0] * q0 + taps[1] * q1 + taps[2] * q2
        product = product_ref[j]
        states = tuple(a * h + product for a, h in zip(factors, states))
        base_ref[j] = added([skip * product] + [w * h for w, h in zip(spread, states)])
        return q0, q1, states

    start = (*before, tuple(jnp.zeros((CHUNKS, LANES), F32) for _ in range(modes)))
    lax.fori_loop(0, run, step, start, unroll=4)

    arrived, gate_gain, base_gain = from_lower(modes, axis, pair_ref, taps_ref, decays_ref, residues_ref, skip_ref)
    for j in range(2):
        gate_ref[j] = at_top(gate_ref[j], gate_gain[j])
        base_ref[j] = at_top(base_ref[j], base_gain[j])
    across = jnp.exp(-rates * (inside * float(positions)))
    for m in range(modes):
        fade = fades(decays_ref, run, m)
        begin_ref[m] = spread[m] * (state_ref[m] + fade * over_sublanes(arrived[m : m + 1, :]))
        reach_ref[m] = spread[m] * fade * over_sublanes(across[m : m + 1, :])


def join_kernel(
    modes, axis, own_ref, other_ref, q_half, product_ref, state_ref, taps_ref, decays_ref, residues_ref, skip_ref,
    sent_ref, pair_ref, *refs,
):
    positions = q_half.shape[0]
    below, above = other_ref[...], own_ref[...]
    pair_ref[0] = below
    pair_ref[1] = above
    first, second = pair_boundary(modes, taps_ref, pair_ref.at[0], pair_ref.at[1])
    rates = decays_ref[...]
    state = jnp.exp(-float(positions) * rates) * below[:modes] + above[:modes]
    state = state + jnp.exp(-float(positions - 1) * rates) * first + jnp.exp(-float(positions - 2) * rates) * second
    row = lax.broadcasted_iota(jnp.int32, (EXTRA, LANES), 0)
    beside = jnp.where(row < K_FIRST, above[modes:], below[modes:])
    rows = jnp.concatenate([state, beside], 0).astype(BF16)
    sent_ref[...] = jnp.broadcast_to(rows[None], sent_ref.shape)

    @pl.when(starts_early(axis))
    def _():
        params = (taps_ref, decays_ref, residues_ref, skip_ref)
        local_work(modes, axis, q_half, product_ref, state_ref, pair_ref, *params, *refs)


def enter_kernel(
    modes, axis, received_ref, q_half, product_ref, state_ref, pair_ref, taps_ref, decays_ref, residues_ref, skip_ref, *refs
):
    enter_ref, local_refs, (rows_ref, first_ref, second_ref, q_ref) = refs[0], refs[1:5], refs[5:]
    positions = q_half.shape[0]
    device = lax.axis_index(axis)
    pair = device // PAIR
    upper = lax.rem(device, PAIR) == 1

    @pl.when(jnp.logical_not(jnp.logical_or(upper, starts_early(axis))))
    def _():
        params = (taps_ref, decays_ref, residues_ref, skip_ref)
        local_work(modes, axis, q_half, product_ref, state_ref, pair_ref, *params, *local_refs, q_ref)

    enter_ref[...] = jnp.zeros_like(enter_ref)

    @pl.when(upper)
    def _():
        pairs = received_ref.shape[0]
        pitch = modes + EXTRA
        rows_ref[0:pitch, :] = jnp.zeros((pitch, LANES), F32)
        for slot, e in enumerate(pair_order(pairs)):
            rows_ref[pitch * (e + 1) : pitch * (e + 2), :] = received_ref[slot].astype(F32)

        def of_all(row, block):
            return tuple(rows_ref[pl.ds(pitch * block + modes + row + i, pairs, stride=pitch), :] for i in range(2))

        last = [of_all(row, 0) for row in (K_LAST, V_LAST)]
        begun = [of_all(row, 1) for row in (K_FIRST, V_FIRST)]
        first_ref[...], second_ref[...] = boundary(taps_ref, last, begun)

        rates = decays_ref[...]
        length = PAIR * positions
        across = jnp.exp(-float(length) * rates)
        late_first = jnp.exp(-float(length - 1) * rates)
        late_second = jnp.exp(-float(length - 2) * rates)
        state = jnp.zeros((modes, LANES), F32)
        for e in range(pairs - 1):
            sent = rows_ref[pitch * (e + 1) : pitch * (e + 1) + modes, :]
            sent = sent + late_first * first_ref[e : e + 1, :] + late_second * second_ref[e : e + 1, :]
            state = jnp.where(e < pair, across * state + sent, state)
        first, second = first_ref[pl.ds(pair, 1), :], second_ref[pl.ds(pair, 1), :]
        enter_ref[:modes, :] = state + jnp.exp(rates) * first + jnp.exp(2.0 * rates) * second
        enter_ref[modes : modes + 1, :] = first
        enter_ref[modes + 1 : modes + 2, :] = second
        for i in range(2):
            enter_ref[modes + 2 + i : modes + 3 + i, :] = rows_ref[pl.ds(pair * pitch + modes + Q_LAST + i, 1), :]
        enter_ref[modes + 4 :, :] = jnp.zeros((EDGE - 4, LANES), F32)


def carry_kernel(
    modes, axis, own_ref, other_ref, *refs
):
    early_locals, locals_, refs = refs[:4], refs[4:8], refs[8:]
    q_half, product_ref, state_ref, pair_ref, taps_ref, decays_ref, residues_ref, skip_ref, *refs = refs
    power_ref, gated_ref, enter_ref, q_ref = refs
    run = product_ref.shape[0]
    positions = run * CHUNKS
    upper = lax.rem(lax.axis_index(axis), PAIR) == 1
    inside = lax.rem(lax.axis_index(axis), PAIR).astype(F32)
    enter_ref[...] = jnp.where(upper, own_ref[...], other_ref[...])
    rates = decays_ref[...]
    state = enter_ref[:modes, :]
    first, second, far, near = (enter_ref[modes + i : modes + i + 1, :] for i in range(4))
    weights = mode_weights(decays_ref, residues_ref)
    lower = 1.0 - inside
    edge = (lower * row for row in (first, second, far, near))
    gate_more, base_more = edge_gains(taps_ref, skip_ref, rates, weights, *edge)
    factors = split(jnp.exp(-rates))

    def put(j, gate, base, terms, more):
        if more is not None:
            gate, base = at_top(gate, more[0]), at_top(base, more[1])
        gated_ref[pl.ds(j, CHUNKS, stride=SPAN), :] = gate * added([base] + terms)

    def over_steps(step, held, gains, unroll):
        for j in range(2):
            held = step(j, held, (gains[0][j], gains[1][j]))
        lax.fori_loop(2, run, lambda j, held: step(j, held, None), held, unroll=unroll)

    early = starts_early(axis)

    def from_local(gate_ref, base_ref, begin_ref, reach_ref):
        def step(j, carried, more):
            carried = tuple(a * g for a, g in zip(factors, carried))
            put(j, gate_ref[j], base_ref[j], list(carried), more)
            return carried

        carried = tuple(begin_ref[m] + reach_ref[m] * over_sublanes(state[m : m + 1, :]) for m in range(modes))
        over_steps(step, carried, (gate_more, base_more), 14)

    @pl.when(early)
    def _():
        from_local(*early_locals)

    @pl.when(jnp.logical_not(jnp.logical_or(early, upper)))
    def _():
        from_local(*locals_)

    @pl.when(jnp.logical_and(upper, jnp.logical_not(early)))
    def _():
        taps, before = load_gate(q_ref, q_half, taps_ref)
        skip = over_sublanes(skip_ref[...])
        spread = split(weights)
        arrived, gate_gain, base_gain = from_lower(modes, axis, pair_ref, taps_ref, decays_ref, residues_ref, skip_ref)
        arrived = arrived + jnp.exp(-rates * (inside * float(positions))) * state
        states = tuple(
            state_ref[m] + fades(decays_ref, run, m) * over_sublanes(arrived[m : m + 1, :]) for m in range(modes)
        )

        def step(j, held, more):
            q1, q2, states = held
            q0 = strided(q_ref, j, PITCH)
            product = product_ref[j]
            states = tuple(a * h + product for a, h in zip(factors, states))
            gate = taps[0] * q0 + taps[1] * q1 + taps[2] * q2
            put(j, gate, skip * product, [w * h for w, h in zip(spread, states)], more)
            return q0, q1, states

        gains = tuple([a + b for a, b in zip(*both)] for both in ((gate_gain, gate_more), (base_gain, base_more)))
        over_steps(step, (*before, states), gains, 6)

    ones = jnp.ones((LANES, LANES), BF16)
    lane = lax.broadcasted_iota(jnp.int32, (CHUNKS, LANES), 1)
    power = jnp.zeros((CHUNKS, LANES), F32)
    tiles = run // CHUNKS
    for s in range(CHUNKS):
        gated = gated_ref[s * SPAN : s * SPAN + run, :]
        square = gated * gated
        high = square.astype(BF16)
        low = (square - high.astype(F32)).astype(BF16)
        sums = jnp.dot(high, ones, preferred_element_type=F32) + jnp.dot(low, ones, preferred_element_type=F32)
        for i in range(tiles):
            power = jnp.where(lane == s * tiles + i, sums[i * CHUNKS : (i + 1) * CHUNKS, :], power)
    power_ref[...] = jnp.broadcast_to(power[None], power_ref.shape)


def finish_kernel(channels, power_ref, gated_ref, gain_ref, mixed_ref):
    run = mixed_ref.shape[0] // CHUNKS
    tiles = run // CHUNKS
    inverse = lax.rsqrt(jnp.sum(power_ref[...], 0) / channels + 1e-05)
    gain = over_sublanes(gain_ref[...])
    for s in range(CHUNKS):
        for i in range(0, tiles, 2):
            halves = []
            for h in (i, i + 1):
                gated = gated_ref[s * SPAN + h * CHUNKS : s * SPAN + (h + 1) * CHUNKS, :]
                halves.append(gated * gain * inverse[:, s * tiles + h : s * tiles + h + 1])
            mixed_ref[s * run + i * CHUNKS : s * run + (i + 2) * CHUNKS, :] = jnp.concatenate(halves, 0).astype(BF16)


def per_device(projections, short_filter, residues, decays, skip, gain):
    positions, _, width = projections.shape
    modes = decays.shape[0]
    ctx_count = lax.axis_size("ctx")
    tp_count = lax.axis_size("tp")
    pairs = ctx_count // PAIR
    run = positions // CHUNKS
    x = jnp.swapaxes(projections, 0, 1)

    def shape(*extent, kind=F32):
        return jax.ShapeDtypeStruct(extent, kind)

    def call(kernel, name, out_shape, in_specs, scratch, *operands):
        return pl.pallas_call(
            kernel,
            out_shape=out_shape,
            in_specs=in_specs,
            out_specs=jax.tree.map(lambda _: VMEM, out_shape),
            scratch_shapes=scratch,
            compiler_params=pltpu.CompilerParams(vmem_limit_bytes=VMEM_LIMIT),
            name=name,
        )(*operands)

    block = shape(run, CHUNKS, width)
    table = shape(modes, CHUNKS, width)
    sources = (x, short_filter, decays, residues, skip[None, :], gain[None, :])
    rows, product, state, q, short_filter, decays, residues, skip, gain = call(
        functools.partial(states_kernel, modes),
        "states",
        (shape(modes + EXTRA, width), block, table, shape(positions, width, kind=BF16))
        + tuple(shape(*s.shape) for s in sources[1:]),
        [ANY] * 6,
        [
            pltpu.VMEM((positions, width), BF16),
            pltpu.VMEM((positions, width), BF16),
            pltpu.VMEM((PITCH * CHUNKS, width), F32),
            pltpu.VMEM((PITCH * CHUNKS, width), F32),
            pltpu.VMEM((3, modes, width), F32),
            pltpu.SemaphoreType.DMA((8,)),
        ],
        *[pltpu.with_memory_space_constraint(s, pltpu.HBM) for s in sources],
    )
    partners = [(i, i + 1 - 2 * (i % PAIR)) for i in range(ctx_count)]
    other = lax.ppermute(rows, "ctx", partners)
    params = (short_filter, decays, residues, skip)
    pitched = pltpu.VMEM((PITCH * CHUNKS, width), F32)
    sent, joined, *early_locals = call(
        functools.partial(join_kernel, modes, "ctx"),
        "join",
        (shape(pairs, modes + EXTRA, width, kind=BF16), shape(PAIR, modes + EXTRA, width), block, block, table, table),
        [VMEM] * 9,
        [pitched],
        rows,
        other,
        q,
        product,
        state,
        *params,
    )
    received = lax.all_to_all(
        sent, ("ctx", "tp"), split_axis=0, concat_axis=0, tiled=True, axis_index_groups=ctx_groups(pairs, tp_count)
    )
    enter_shape = shape(modes + EDGE, width)
    local_shapes = (block, block, table, table)
    enter, *locals_ = call(
        functools.partial(enter_kernel, modes, "ctx"),
        "enter",
        (enter_shape, *local_shapes),
        [VMEM] * 9,
        [
            pltpu.VMEM(((pairs + 1) * (modes + EXTRA), width), F32),
            pltpu.VMEM((pairs, width), F32),
            pltpu.VMEM((pairs, width), F32),
            pitched,
        ],
        received,
        q,
        product,
        state,
        joined,
        *params,
    )
    entered = lax.ppermute(enter, "ctx", partners)
    power, gated = call(
        functools.partial(carry_kernel, modes, "ctx"),
        "carry",
        (shape(tp_count, CHUNKS, run), shape(SPAN * CHUNKS, width)),
        [VMEM] * 18,
        [pltpu.VMEM((modes + EDGE, width), F32), pitched],
        enter,
        entered,
        *early_locals,
        *locals_,
        q,
        product,
        state,
        joined,
        *params,
    )
    powers = lax.all_to_all(
        power, "tp", split_axis=0, concat_axis=0, tiled=True, axis_index_groups=[slice_order(tp_count)]
    )
    return call(
        functools.partial(finish_kernel, width * tp_count),
        "finish",
        shape(positions, width, kind=BF16),
        [VMEM] * 3,
        [],
        powers,
        gated,
        gain,
    )


def solution(mesh):
    in_specs = (
        P("ctx", None, "tp"),
        P(None, None, "tp"),
        P(None, "tp"),
        P(None, "tp"),
        P("tp"),
        P("tp"),
    )
    return jax.shard_map(per_device, mesh=mesh, in_specs=in_specs, out_specs=P("ctx", "tp"), check_vma=False)
```

```python
import functools

import jax
import jax.numpy as jnp
from jax import lax
from jax.experimental import pallas as pl
from jax.experimental.pallas import tpu as pltpu
from jax.sharding import PartitionSpec as P

F32 = jnp.float32
BF16 = jnp.bfloat16
CHUNKS = 8
LANES = 128
PAIR = 2
VMEM_LIMIT = 40 * 1024 * 1024
VMEM = pl.BlockSpec(memory_space=pltpu.VMEM)
ANY = pl.BlockSpec(memory_space=pl.ANY)

FIRST_PAIR = 10
FIRST_SLICE = 5
GRID = 4
PITCH = 137
SPAN = 136

K_LAST, V_LAST, Q_LAST, K_FIRST, V_FIRST = 0, 2, 4, 6, 8
EXTRA = 16
EDGE = 8


def first_then(first, members, distance):
    return [first] + sorted((i for i in range(members) if i != first), key=lambda i: -distance(i, first))


def around(a, b, size):
    return min((a - b) % size, (b - a) % size)


def pair_order(pairs):
    def distance(a, b):
        return around(a // GRID, b // GRID, max(pairs // GRID, 1)) + 2 * around(a % GRID, b % GRID, GRID)

    return first_then(FIRST_PAIR % pairs, pairs, distance)


def ctx_groups(pairs, slices):
    def index(pair, half, piece):
        return (pair * PAIR + half) * slices + piece

    groups = [[index(p, PAIR - 1, piece) for p in pair_order(pairs)] for piece in range(slices)]
    rest = [(p % GRID, p // GRID // 2, -index(p, 0, piece)) for p in range(pairs) for piece in range(slices)]
    rest = [-i for *_, i in sorted(rest)]
    return groups + [rest[i : i + pairs] for i in range(0, len(rest), pairs)]


def slice_order(slices):
    return first_then(FIRST_SLICE % slices, slices, lambda a, b: 0)


def over_sublanes(row):
    return jnp.broadcast_to(row, (CHUNKS, LANES))


def sublane_index():
    return lax.broadcasted_iota(jnp.int32, (CHUNKS, LANES), 0)


def next_chunk(block, distance=1):
    rolled = pltpu.roll(block, distance, 0)
    return jnp.where(sublane_index() >= distance, rolled, 0.0)


def strided(ref, step, run):
    return ref[pl.ds(step, CHUNKS, stride=run), :]


def added(terms):
    while len(terms) > 1:
        pairs = [terms[i] + terms[i + 1] for i in range(0, len(terms) - 1, 2)]
        terms = pairs + terms[2 * len(pairs) :]
    return terms[0]


def boundary(taps_ref, last, first):
    products = []
    for j in (1, 2):
        tap = [taps_ref[j, i : i + 1, :] for i in range(3)]
        (far, near), (zero, one) = last[j - 1], first[j - 1]
        own = (tap[0] * zero, tap[0] * one + tap[1] * zero)
        gained = (tap[1] * near + tap[2] * far, tap[2] * near)
        products.append((own, gained))
    (k_own, k_gained), (v_own, v_gained) = products
    return [k_own[i] * v_gained[i] + k_gained[i] * (v_own[i] + v_gained[i]) for i in range(2)]


def two_rows(ref, row):
    return ref[row : row + 1, :], ref[row + 1 : row + 2, :]


def pair_boundary(modes, taps_ref, lower_ref, upper_ref):
    last = [two_rows(lower_ref, modes + row) for row in (K_LAST, V_LAST)]
    first = [two_rows(upper_ref, modes + row) for row in (K_FIRST, V_FIRST)]
    return boundary(taps_ref, last, first)


def states_kernel(modes, *refs):
    sources, refs = refs[:6], refs[6:]
    x_hbm = sources[0]
    (rows_ref, product_ref, state_ref, q_ref), refs = refs[:4], refs[4:]
    params, refs = refs[:5], refs[5:]
    taps_ref, decays_ref = params[0], params[1]
    k_half, v_half, k_ref, v_ref, jump_ref, semaphores = refs
    copies = [pltpu.make_async_copy(s, d, semaphores.at[i]) for i, (s, d) in enumerate(zip(sources[1:], params))]
    streams = [
        pltpu.make_async_copy(x_hbm.at[j], d, semaphores.at[5 + j]) for j, d in enumerate((q_ref, k_half, v_half))
    ]
    for copy in (streams[1], streams[2], copies[1], copies[0], streams[0], copies[2], copies[3], copies[4]):
        copy.start()
    positions = q_ref.shape[0]
    run = positions // CHUNKS
    copies[1].wait()
    copies[0].wait()
    k_taps = [over_sublanes(taps_ref[1, i : i + 1, :]) for i in range(3)]
    v_taps = [over_sublanes(taps_ref[2, i : i + 1, :]) for i in range(3)]
    rates = decays_ref[...]
    factor = jnp.exp(-rates)
    factors = [over_sublanes(factor[m : m + 1, :]) for m in range(modes)]
    for i in range(3):
        jump_ref[i] = jnp.exp(-float(run << i) * rates)
    streams[1].wait()
    for s in range(CHUNKS):
        k_ref[s * PITCH : s * PITCH + run, :] = k_half[s * run : (s + 1) * run, :].astype(F32)
    streams[2].wait()
    for s in range(CHUNKS):
        v_ref[s * PITCH : s * PITCH + run, :] = v_half[s * run : (s + 1) * run, :].astype(F32)

    def step(j, carry):
        k1, k2, v1, v2, states = carry
        k0 = strided(k_ref, j, PITCH)
        v0 = strided(v_ref, j, PITCH)
        k = k_taps[0] * k0 + k_taps[1] * k1 + k_taps[2] * k2
        v = v_taps[0] * v0 + v_taps[1] * v1 + v_taps[2] * v2
        product = k * v
        product_ref[j] = product
        states = tuple(a * h + product for a, h in zip(factors, states))
        return k0, k1, v0, v1, states

    start = (
        next_chunk(strided(k_ref, run - 1, PITCH)),
        next_chunk(strided(k_ref, run - 2, PITCH)),
        next_chunk(strided(v_ref, run - 1, PITCH)),
        next_chunk(strided(v_ref, run - 2, PITCH)),
        tuple(jnp.zeros((CHUNKS, LANES), F32) for _ in range(modes)),
    )
    states = lax.fori_loop(0, run, step, start, unroll=16)[4]
    for m in range(modes):
        total = states[m]
        for i in range(3):
            total = total + over_sublanes(jump_ref[i, m : m + 1, :]) * next_chunk(total, 1 << i)
        state_ref[m] = next_chunk(total)
        rows_ref[m : m + 1, :] = total[CHUNKS - 1 : CHUNKS, :]
    streams[0].wait()
    rows_ref[modes + K_LAST : modes + K_LAST + 2, :] = k_ref[7 * PITCH + run - 2 : 7 * PITCH + run, :]
    rows_ref[modes + V_LAST : modes + V_LAST + 2, :] = v_ref[7 * PITCH + run - 2 : 7 * PITCH + run, :]
    rows_ref[modes + Q_LAST : modes + Q_LAST + 2, :] = q_ref[positions - 16 : positions, :].astype(F32)[14:16]
    rows_ref[modes + K_FIRST : modes + K_FIRST + 2, :] = k_ref[0:2, :]
    rows_ref[modes + V_FIRST : modes + V_FIRST + 2, :] = v_ref[0:2, :]
    rows_ref[modes + V_FIRST + 2 :, :] = jnp.zeros((EXTRA - V_FIRST - 2, LANES), F32)
    for i in (2, 3, 4):
        copies[i].wait()


def starts_early(axis):
    pair = lax.axis_index(axis) // PAIR
    y, z = pair // GRID, lax.rem(pair, GRID)
    return jnp.logical_or(z < 1, jnp.logical_and(z < 2, y < 2))


def mode_weights(decays_ref, residues_ref):
    return residues_ref[...] * jnp.sqrt(2.0 * decays_ref[...])


def edge_gains(taps_ref, skip_ref, rates, weights, first, second, far, near):
    early = jnp.sum(weights * jnp.exp(rates), 0, keepdims=True) * second
    skip = skip_ref[...]
    gate = (taps_ref[0, 1:2, :] * near + taps_ref[0, 2:3, :] * far, taps_ref[0, 2:3, :] * near)
    return gate, (skip * first - early, skip * second)


def from_lower(modes, axis, pair_ref, taps_ref, decays_ref, residues_ref, skip_ref):
    inside = lax.rem(lax.axis_index(axis), PAIR).astype(F32)
    rates = decays_ref[...]
    first, second = (inside * p for p in pair_boundary(modes, taps_ref, pair_ref.at[0], pair_ref.at[1]))
    state = inside * pair_ref[0, :modes, :] + jnp.exp(rates) * first + jnp.exp(2.0 * rates) * second
    far, near = (inside * row for row in two_rows(pair_ref.at[0], modes + Q_LAST))
    weights = mode_weights(decays_ref, residues_ref)
    return state, *edge_gains(taps_ref, skip_ref, rates, weights, first, second, far, near)


def at_top(block, row):
    return block + jnp.where(sublane_index() == 0, over_sublanes(row), 0.0)


def fades(decays_ref, run, m):
    return jnp.exp(over_sublanes(decays_ref[m : m + 1, :]) * (sublane_index().astype(F32) * -float(run)))


def load_gate(q_ref, q_half, taps_ref):
    run = q_half.shape[0] // CHUNKS
    for s in range(CHUNKS):
        q_ref[s * PITCH : s * PITCH + run, :] = q_half[s * run : (s + 1) * run, :].astype(F32)
    taps = [over_sublanes(taps_ref[0, i : i + 1, :]) for i in range(3)]
    return taps, [next_chunk(strided(q_ref, run - 1 - i, PITCH)) for i in range(2)]


def split(table):
    return [over_sublanes(table[m : m + 1, :]) for m in range(table.shape[0])]


def local_work(
    modes, axis, q_half, product_ref, state_ref, pair_ref, taps_ref, decays_ref, residues_ref, skip_ref,
    gate_ref, base_ref, begin_ref, reach_ref, q_ref,
):
    run = product_ref.shape[0]
    positions = run * CHUNKS
    inside = lax.rem(lax.axis_index(axis), PAIR).astype(F32)
    rates = decays_ref[...]
    spread = split(mode_weights(decays_ref, residues_ref))
    factors = split(jnp.exp(-rates))
    skip = over_sublanes(skip_ref[...])
    taps, before = load_gate(q_ref, q_half, taps_ref)

    def step(j, carry):
        q1, q2, states = carry
        q0 = strided(q_ref, j, PITCH)
        gate_ref[j] = taps[0] * q0 + taps[1] * q1 + taps[2] * q2
        product = product_ref[j]
        states = tuple(a * h + product for a, h in zip(factors, states))
        base_ref[j] = added([skip * product] + [w * h for w, h in zip(spread, states)])
        return q0, q1, states

    start = (*before, tuple(jnp.zeros((CHUNKS, LANES), F32) for _ in range(modes)))
    lax.fori_loop(0, run, step, start, unroll=4)

    arrived, gate_gain, base_gain = from_lower(modes, axis, pair_ref, taps_ref, decays_ref, residues_ref, skip_ref)
    for j in range(2):
        gate_ref[j] = at_top(gate_ref[j], gate_gain[j])
        base_ref[j] = at_top(base_ref[j], base_gain[j])
    across = jnp.exp(-rates * (inside * float(positions)))
    for m in range(modes):
        fade = fades(decays_ref, run, m)
        begin_ref[m] = spread[m] * (state_ref[m] + fade * over_sublanes(arrived[m : m + 1, :]))
        reach_ref[m] = spread[m] * fade * over_sublanes(across[m : m + 1, :])


def join_kernel(
    modes, axis, own_ref, other_ref, q_half, product_ref, state_ref, taps_ref, decays_ref, residues_ref, skip_ref,
    sent_ref, pair_ref, *refs,
):
    positions = q_half.shape[0]
    below, above = other_ref[...], own_ref[...]
    pair_ref[0] = below
    pair_ref[1] = above
    first, second = pair_boundary(modes, taps_ref, pair_ref.at[0], pair_ref.at[1])
    rates = decays_ref[...]
    state = jnp.exp(-float(positions) * rates) * below[:modes] + above[:modes]
    state = state + jnp.exp(-float(positions - 1) * rates) * first + jnp.exp(-float(positions - 2) * rates) * second
    row = lax.broadcasted_iota(jnp.int32, (EXTRA, LANES), 0)
    beside = jnp.where(row < K_FIRST, above[modes:], below[modes:])
    rows = jnp.concatenate([state, beside], 0).astype(BF16)
    sent_ref[...] = jnp.broadcast_to(rows[None], sent_ref.shape)

    @pl.when(starts_early(axis))
    def _():
        params = (taps_ref, decays_ref, residues_ref, skip_ref)
        local_work(modes, axis, q_half, product_ref, state_ref, pair_ref, *params, *refs)


def enter_kernel(
    modes, axis, received_ref, q_half, product_ref, state_ref, pair_ref, taps_ref, decays_ref, residues_ref, skip_ref, *refs
):
    enter_ref, local_refs, (rows_ref, first_ref, second_ref, q_ref) = refs[0], refs[1:5], refs[5:]
    positions = q_half.shape[0]
    device = lax.axis_index(axis)
    pair = device // PAIR
    upper = lax.rem(device, PAIR) == 1

    @pl.when(jnp.logical_not(jnp.logical_or(upper, starts_early(axis))))
    def _():
        params = (taps_ref, decays_ref, residues_ref, skip_ref)
        local_work(modes, axis, q_half, product_ref, state_ref, pair_ref, *params, *local_refs, q_ref)

    enter_ref[...] = jnp.zeros_like(enter_ref)

    @pl.when(upper)
    def _():
        pairs = received_ref.shape[0]
        pitch = modes + EXTRA
        rows_ref[0:pitch, :] = jnp.zeros((pitch, LANES), F32)
        for slot, e in enumerate(pair_order(pairs)):
            rows_ref[pitch * (e + 1) : pitch * (e + 2), :] = received_ref[slot].astype(F32)

        def of_all(row, block):
            return tuple(rows_ref[pl.ds(pitch * block + modes + row + i, pairs, stride=pitch), :] for i in range(2))

        last = [of_all(row, 0) for row in (K_LAST, V_LAST)]
        begun = [of_all(row, 1) for row in (K_FIRST, V_FIRST)]
        first_ref[...], second_ref[...] = boundary(taps_ref, last, begun)

        rates = decays_ref[...]
        length = PAIR * positions
        across = jnp.exp(-float(length) * rates)
        late_first = jnp.exp(-float(length - 1) * rates)
        late_second = jnp.exp(-float(length - 2) * rates)
        state = jnp.zeros((modes, LANES), F32)
        for e in range(pairs - 1):
            sent = rows_ref[pitch * (e + 1) : pitch * (e + 1) + modes, :]
            sent = sent + late_first * first_ref[e : e + 1, :] + late_second * second_ref[e : e + 1, :]
            state = jnp.where(e < pair, across * state + sent, state)
        first, second = first_ref[pl.ds(pair, 1), :], second_ref[pl.ds(pair, 1), :]
        enter_ref[:modes, :] = state + jnp.exp(rates) * first + jnp.exp(2.0 * rates) * second
        enter_ref[modes : modes + 1, :] = first
        enter_ref[modes + 1 : modes + 2, :] = second
        for i in range(2):
            enter_ref[modes + 2 + i : modes + 3 + i, :] = rows_ref[pl.ds(pair * pitch + modes + Q_LAST + i, 1), :]
        enter_ref[modes + 4 :, :] = jnp.zeros((EDGE - 4, LANES), F32)


def carry_kernel(
    modes, axis, own_ref, other_ref, *refs
):
    early_locals, locals_, refs = refs[:4], refs[4:8], refs[8:]
    q_half, product_ref, state_ref, pair_ref, taps_ref, decays_ref, residues_ref, skip_ref, *refs = refs
    power_ref, gated_ref, enter_ref, q_ref = refs
    run = product_ref.shape[0]
    positions = run * CHUNKS
    upper = lax.rem(lax.axis_index(axis), PAIR) == 1
    inside = lax.rem(lax.axis_index(axis), PAIR).astype(F32)
    enter_ref[...] = jnp.where(upper, own_ref[...], other_ref[...])
    rates = decays_ref[...]
    state = enter_ref[:modes, :]
    first, second, far, near = (enter_ref[modes + i : modes + i + 1, :] for i in range(4))
    weights = mode_weights(decays_ref, residues_ref)
    lower = 1.0 - inside
    edge = (lower * row for row in (first, second, far, near))
    gate_more, base_more = edge_gains(taps_ref, skip_ref, rates, weights, *edge)
    factors = split(jnp.exp(-rates))

    def put(j, gate, base, terms, more):
        if more is not None:
            gate, base = at_top(gate, more[0]), at_top(base, more[1])
        gated_ref[pl.ds(j, CHUNKS, stride=SPAN), :] = gate * added([base] + terms)

    def over_steps(step, held, gains, unroll):
        for j in range(2):
            held = step(j, held, (gains[0][j], gains[1][j]))
        lax.fori_loop(2, run, lambda j, held: step(j, held, None), held, unroll=unroll)

    early = starts_early(axis)

    def from_local(gate_ref, base_ref, begin_ref, reach_ref):
        def step(j, carried, more):
            carried = tuple(a * g for a, g in zip(factors, carried))
            put(j, gate_ref[j], base_ref[j], list(carried), more)
            return carried

        carried = tuple(begin_ref[m] + reach_ref[m] * over_sublanes(state[m : m + 1, :]) for m in range(modes))
        over_steps(step, carried, (gate_more, base_more), 14)

    @pl.when(early)
    def _():
        from_local(*early_locals)

    @pl.when(jnp.logical_not(jnp.logical_or(early, upper)))
    def _():
        from_local(*locals_)

    @pl.when(jnp.logical_and(upper, jnp.logical_not(early)))
    def _():
        taps, before = load_gate(q_ref, q_half, taps_ref)
        skip = over_sublanes(skip_ref[...])
        spread = split(weights)
        arrived, gate_gain, base_gain = from_lower(modes, axis, pair_ref, taps_ref, decays_ref, residues_ref, skip_ref)
        arrived = arrived + jnp.exp(-rates * (inside * float(positions))) * state
        states = tuple(
            state_ref[m] + fades(decays_ref, run, m) * over_sublanes(arrived[m : m + 1, :]) for m in range(modes)
        )

        def step(j, held, more):
            q1, q2, states = held
            q0 = strided(q_ref, j, PITCH)
            product = product_ref[j]
            states = tuple(a * h + product for a, h in zip(factors, states))
            gate = taps[0] * q0 + taps[1] * q1 + taps[2] * q2
            put(j, gate, skip * product, [w * h for w, h in zip(spread, states)], more)
            return q0, q1, states

        gains = tuple([a + b for a, b in zip(*both)] for both in ((gate_gain, gate_more), (base_gain, base_more)))
        over_steps(step, (*before, states), gains, 6)

    ones = jnp.ones((LANES, LANES), BF16)
    lane = lax.broadcasted_iota(jnp.int32, (CHUNKS, LANES), 1)
    power = jnp.zeros((CHUNKS, LANES), F32)
    tiles = run // CHUNKS
    for s in range(CHUNKS):
        gated = gated_ref[s * SPAN : s * SPAN + run, :]
        square = gated * gated
        high = square.astype(BF16)
        low = (square - high.astype(F32)).astype(BF16)
        sums = jnp.dot(high, ones, preferred_element_type=F32) + jnp.dot(low, ones, preferred_element_type=F32)
        for i in range(tiles):
            power = jnp.where(lane == s * tiles + i, sums[i * CHUNKS : (i + 1) * CHUNKS, :], power)
    power_ref[...] = jnp.broadcast_to(power[None], power_ref.shape)


def finish_kernel(channels, power_ref, gated_ref, gain_ref, mixed_ref):
    run = mixed_ref.shape[0] // CHUNKS
    tiles = run // CHUNKS
    inverse = lax.rsqrt(jnp.sum(power_ref[...], 0) / channels + 1e-05)
    gain = over_sublanes(gain_ref[...])
    for s in range(CHUNKS):
        for i in range(0, tiles, 2):
            halves = []
            for h in (i, i + 1):
                gated = gated_ref[s * SPAN + h * CHUNKS : s * SPAN + (h + 1) * CHUNKS, :]
                halves.append(gated * gain * inverse[:, s * tiles + h : s * tiles + h + 1])
            mixed_ref[s * run + i * CHUNKS : s * run + (i + 2) * CHUNKS, :] = jnp.concatenate(halves, 0).astype(BF16)


def per_device(projections, short_filter, residues, decays, skip, gain):
    positions, _, width = projections.shape
    modes = decays.shape[0]
    ctx_count = lax.axis_size("ctx")
    tp_count = lax.axis_size("tp")
    pairs = ctx_count // PAIR
    run = positions // CHUNKS
    x = jnp.swapaxes(projections, 0, 1)

    def shape(*extent, kind=F32):
        return jax.ShapeDtypeStruct(extent, kind)

    def call(kernel, name, out_shape, in_specs, scratch, *operands):
        return pl.pallas_call(
            kernel,
            out_shape=out_shape,
            in_specs=in_specs,
            out_specs=jax.tree.map(lambda _: VMEM, out_shape),
            scratch_shapes=scratch,
            compiler_params=pltpu.CompilerParams(vmem_limit_bytes=VMEM_LIMIT),
            name=name,
        )(*operands)

    block = shape(run, CHUNKS, width)
    table = shape(modes, CHUNKS, width)
    sources = (x, short_filter, decays, residues, skip[None, :], gain[None, :])
    rows, product, state, q, short_filter, decays, residues, skip, gain = call(
        functools.partial(states_kernel, modes),
        "states",
        (shape(modes + EXTRA, width), block, table, shape(positions, width, kind=BF16))
        + tuple(shape(*s.shape) for s in sources[1:]),
        [ANY] * 6,
        [
            pltpu.VMEM((positions, width), BF16),
            pltpu.VMEM((positions, width), BF16),
            pltpu.VMEM((PITCH * (CHUNKS + 1), width), F32),
            pltpu.VMEM((PITCH * (CHUNKS + 1), width), F32),
            pltpu.VMEM((3, modes, width), F32),
            pltpu.SemaphoreType.DMA((8,)),
        ],
        *[pltpu.with_memory_space_constraint(s, pltpu.HBM) for s in sources],
    )
    partners = [(i, i + 1 - 2 * (i % PAIR)) for i in range(ctx_count)]
    other = lax.ppermute(rows, "ctx", partners)
    params = (short_filter, decays, residues, skip)
    pitched = pltpu.VMEM((PITCH * (CHUNKS + 1), width), F32)
    sent, joined, *early_locals = call(
        functools.partial(join_kernel, modes, "ctx"),
        "join",
        (shape(pairs, modes + EXTRA, width, kind=BF16), shape(PAIR, modes + EXTRA, width), block, block, table, table),
        [VMEM] * 9,
        [pitched],
        rows,
        other,
        q,
        product,
        state,
        *params,
    )
    received = lax.all_to_all(
        sent, ("ctx", "tp"), split_axis=0, concat_axis=0, tiled=True, axis_index_groups=ctx_groups(pairs, tp_count)
    )
    enter_shape = shape(modes + EDGE, width)
    local_shapes = (block, block, table, table)
    enter, *locals_ = call(
        functools.partial(enter_kernel, modes, "ctx"),
        "enter",
        (enter_shape, *local_shapes),
        [VMEM] * 9,
        [
            pltpu.VMEM(((pairs + 2) * (modes + EXTRA), width), F32),
            pltpu.VMEM((pairs, width), F32),
            pltpu.VMEM((pairs, width), F32),
            pitched,
        ],
        received,
        q,
        product,
        state,
        joined,
        *params,
    )
    entered = lax.ppermute(enter, "ctx", partners)
    power, gated = call(
        functools.partial(carry_kernel, modes, "ctx"),
        "carry",
        (shape(tp_count, CHUNKS, run), shape(SPAN * (CHUNKS + 1), width)),
        [VMEM] * 18,
        [pltpu.VMEM((modes + EDGE, width), F32), pitched],
        enter,
        entered,
        *early_locals,
        *locals_,
        q,
        product,
        state,
        joined,
        *params,
    )
    powers = lax.all_to_all(
        power, "tp", split_axis=0, concat_axis=0, tiled=True, axis_index_groups=[slice_order(tp_count)]
    )
    return call(
        functools.partial(finish_kernel, width * tp_count),
        "finish",
        shape(positions, width, kind=BF16),
        [VMEM] * 3,
        [],
        powers,
        gated,
        gain,
    )


def solution(mesh):
    in_specs = (
        P("ctx", None, "tp"),
        P(None, None, "tp"),
        P(None, "tp"),
        P(None, "tp"),
        P("tp"),
        P("tp"),
    )
    return jax.shard_map(per_device, mesh=mesh, in_specs=in_specs, out_specs=P("ctx", "tp"), check_vma=False)
```

```python
import functools

import jax
import jax.numpy as jnp
from jax import lax
from jax.experimental import pallas as pl
from jax.experimental.pallas import tpu as pltpu
from jax.sharding import PartitionSpec as P

F32 = jnp.float32
BF16 = jnp.bfloat16
CHUNKS = 8
LANES = 128
PAIR = 2
VMEM_LIMIT = 40 * 1024 * 1024
VMEM = pl.BlockSpec(memory_space=pltpu.VMEM)
ANY = pl.BlockSpec(memory_space=pl.ANY)

FIRST_PAIR = 10
FIRST_SLICE = 5
GRID = 4
PITCH = 137
SPAN = 136

K_LAST, V_LAST, Q_LAST, K_FIRST, V_FIRST = 0, 2, 4, 6, 8
EXTRA = 16
EDGE = 8


def first_then(first, members, distance):
    return [first] + sorted((i for i in range(members) if i != first), key=lambda i: -distance(i, first))


def around(a, b, size):
    return min((a - b) % size, (b - a) % size)


def pair_order(pairs):
    def distance(a, b):
        return around(a // GRID, b // GRID, max(pairs // GRID, 1)) + 2 * around(a % GRID, b % GRID, GRID)

    return first_then(FIRST_PAIR % pairs, pairs, distance)


def ctx_groups(pairs, slices):
    def index(pair, half, piece):
        return (pair * PAIR + half) * slices + piece

    groups = [[index(p, PAIR - 1, piece) for p in pair_order(pairs)] for piece in range(slices)]
    rest = [(p % GRID, p // GRID // 2, -index(p, 0, piece)) for p in range(pairs) for piece in range(slices)]
    rest = [-i for *_, i in sorted(rest)]
    return groups + [rest[i : i + pairs] for i in range(0, len(rest), pairs)]


def slice_order(slices):
    return first_then(FIRST_SLICE % slices, slices, lambda a, b: 0)


def over_sublanes(row):
    return jnp.broadcast_to(row, (CHUNKS, LANES))


def sublane_index():
    return lax.broadcasted_iota(jnp.int32, (CHUNKS, LANES), 0)


def next_chunk(block, distance=1):
    rolled = pltpu.roll(block, distance, 0)
    return jnp.where(sublane_index() >= distance, rolled, 0.0)


def strided(ref, step, run):
    return ref[pl.ds(step, CHUNKS, stride=run), :]


def added(terms):
    while len(terms) > 1:
        pairs = [terms[i] + terms[i + 1] for i in range(0, len(terms) - 1, 2)]
        terms = pairs + terms[2 * len(pairs) :]
    return terms[0]


def boundary(taps_ref, last, first):
    products = []
    for j in (1, 2):
        tap = [taps_ref[j, i : i + 1, :] for i in range(3)]
        (far, near), (zero, one) = last[j - 1], first[j - 1]
        own = (tap[0] * zero, tap[0] * one + tap[1] * zero)
        gained = (tap[1] * near + tap[2] * far, tap[2] * near)
        products.append((own, gained))
    (k_own, k_gained), (v_own, v_gained) = products
    return [k_own[i] * v_gained[i] + k_gained[i] * (v_own[i] + v_gained[i]) for i in range(2)]


def two_rows(ref, row):
    return ref[row : row + 1, :], ref[row + 1 : row + 2, :]


def pair_boundary(modes, taps_ref, lower_ref, upper_ref):
    last = [two_rows(lower_ref, modes + row) for row in (K_LAST, V_LAST)]
    first = [two_rows(upper_ref, modes + row) for row in (K_FIRST, V_FIRST)]
    return boundary(taps_ref, last, first)


def states_kernel(modes, *refs):
    sources, refs = refs[:6], refs[6:]
    x_hbm = sources[0]
    (rows_ref, product_ref, state_ref, q_ref), refs = refs[:4], refs[4:]
    params, refs = refs[:5], refs[5:]
    taps_ref, decays_ref = params[0], params[1]
    k_half, v_half, k_ref, v_ref, jump_ref, semaphores = refs
    copies = [pltpu.make_async_copy(s, d, semaphores.at[i]) for i, (s, d) in enumerate(zip(sources[1:], params))]
    streams = [
        pltpu.make_async_copy(x_hbm.at[j], d, semaphores.at[5 + j]) for j, d in enumerate((q_ref, k_half, v_half))
    ]
    for copy in (streams[1], streams[2], copies[1], copies[0], streams[0], copies[2], copies[3], copies[4]):
        copy.start()
    positions = q_ref.shape[0]
    run = positions // CHUNKS
    copies[1].wait()
    copies[0].wait()
    k_taps = [over_sublanes(taps_ref[1, i : i + 1, :]) for i in range(3)]
    v_taps = [over_sublanes(taps_ref[2, i : i + 1, :]) for i in range(3)]
    rates = decays_ref[...]
    factor = jnp.exp(-rates)
    factors = [over_sublanes(factor[m : m + 1, :]) for m in range(modes)]
    for i in range(3):
        jump_ref[i] = jnp.exp(-float(run << i) * rates)
    streams[1].wait()
    for s in range(CHUNKS):
        k_ref[s * PITCH : s * PITCH + run, :] = k_half[s * run : (s + 1) * run, :].astype(F32)
    streams[2].wait()
    for s in range(CHUNKS):
        v_ref[s * PITCH : s * PITCH + run, :] = v_half[s * run : (s + 1) * run, :].astype(F32)

    def step(j, carry):
        k1, k2, v1, v2, states = carry
        k0 = strided(k_ref, j, PITCH)
        v0 = strided(v_ref, j, PITCH)
        k = k_taps[0] * k0 + k_taps[1] * k1 + k_taps[2] * k2
        v = v_taps[0] * v0 + v_taps[1] * v1 + v_taps[2] * v2
        product = k * v
        product_ref[j] = product
        states = tuple(a * h + product for a, h in zip(factors, states))
        return k0, k1, v0, v1, states

    start = (
        next_chunk(strided(k_ref, run - 1, PITCH)),
        next_chunk(strided(k_ref, run - 2, PITCH)),
        next_chunk(strided(v_ref, run - 1, PITCH)),
        next_chunk(strided(v_ref, run - 2, PITCH)),
        tuple(jnp.zeros((CHUNKS, LANES), F32) for _ in range(modes)),
    )
    states = lax.fori_loop(0, run, step, start, unroll=16)[4]
    for m in range(modes):
        total = states[m]
        for i in range(3):
            total = total + over_sublanes(jump_ref[i, m : m + 1, :]) * next_chunk(total, 1 << i)
        state_ref[m] = next_chunk(total)
        rows_ref[m : m + 1, :] = total[CHUNKS - 1 : CHUNKS, :]
    streams[0].wait()
    rows_ref[modes + K_LAST : modes + K_LAST + 2, :] = k_ref[7 * PITCH + run - 2 : 7 * PITCH + run, :]
    rows_ref[modes + V_LAST : modes + V_LAST + 2, :] = v_ref[7 * PITCH + run - 2 : 7 * PITCH + run, :]
    rows_ref[modes + Q_LAST : modes + Q_LAST + 2, :] = q_ref[positions - 16 : positions, :].astype(F32)[14:16]
    rows_ref[modes + K_FIRST : modes + K_FIRST + 2, :] = k_ref[0:2, :]
    rows_ref[modes + V_FIRST : modes + V_FIRST + 2, :] = v_ref[0:2, :]
    rows_ref[modes + V_FIRST + 2 :, :] = jnp.zeros((EXTRA - V_FIRST - 2, LANES), F32)
    for i in (2, 3, 4):
        copies[i].wait()


def starts_early(axis):
    pair = lax.axis_index(axis) // PAIR
    y, z = pair // GRID, lax.rem(pair, GRID)
    return jnp.logical_or(z < 1, jnp.logical_and(z < 2, y < 2))


def mode_weights(decays_ref, residues_ref):
    return residues_ref[...] * jnp.sqrt(2.0 * decays_ref[...])


def edge_gains(taps_ref, skip_ref, rates, weights, first, second, far, near):
    early = jnp.sum(weights * jnp.exp(rates), 0, keepdims=True) * second
    skip = skip_ref[...]
    gate = (taps_ref[0, 1:2, :] * near + taps_ref[0, 2:3, :] * far, taps_ref[0, 2:3, :] * near)
    return gate, (skip * first - early, skip * second)


def from_lower(modes, axis, pair_ref, taps_ref, decays_ref, residues_ref, skip_ref):
    inside = lax.rem(lax.axis_index(axis), PAIR).astype(F32)
    rates = decays_ref[...]
    first, second = (inside * p for p in pair_boundary(modes, taps_ref, pair_ref.at[0], pair_ref.at[1]))
    state = inside * pair_ref[0, :modes, :] + jnp.exp(rates) * first + jnp.exp(2.0 * rates) * second
    far, near = (inside * row for row in two_rows(pair_ref.at[0], modes + Q_LAST))
    weights = mode_weights(decays_ref, residues_ref)
    return state, *edge_gains(taps_ref, skip_ref, rates, weights, first, second, far, near)


def at_top(block, row):
    return block + jnp.where(sublane_index() == 0, over_sublanes(row), 0.0)


def fades(decays_ref, run, m):
    return jnp.exp(over_sublanes(decays_ref[m : m + 1, :]) * (sublane_index().astype(F32) * -float(run)))


def load_gate(q_ref, q_half, taps_ref):
    run = q_half.shape[0] // CHUNKS
    for s in range(CHUNKS):
        q_ref[s * PITCH : s * PITCH + run, :] = q_half[s * run : (s + 1) * run, :].astype(F32)
    taps = [over_sublanes(taps_ref[0, i : i + 1, :]) for i in range(3)]
    return taps, [next_chunk(strided(q_ref, run - 1 - i, PITCH)) for i in range(2)]


def split(table):
    return [over_sublanes(table[m : m + 1, :]) for m in range(table.shape[0])]


def local_work(
    modes, axis, q_half, product_ref, state_ref, pair_ref, taps_ref, decays_ref, residues_ref, skip_ref,
    gate_ref, base_ref, begin_ref, reach_ref, q_ref,
):
    run = product_ref.shape[0]
    positions = run * CHUNKS
    inside = lax.rem(lax.axis_index(axis), PAIR).astype(F32)
    rates = decays_ref[...]
    spread = split(mode_weights(decays_ref, residues_ref))
    factors = split(jnp.exp(-rates))
    skip = over_sublanes(skip_ref[...])
    taps, before = load_gate(q_ref, q_half, taps_ref)

    def step(j, carry):
        q1, q2, states = carry
        q0 = strided(q_ref, j, PITCH)
        gate_ref[j] = taps[0] * q0 + taps[1] * q1 + taps[2] * q2
        product = product_ref[j]
        states = tuple(a * h + product for a, h in zip(factors, states))
        base_ref[j] = added([skip * product] + [w * h for w, h in zip(spread, states)])
        return q0, q1, states

    start = (*before, tuple(jnp.zeros((CHUNKS, LANES), F32) for _ in range(modes)))
    lax.fori_loop(0, run, step, start, unroll=4)

    arrived, gate_gain, base_gain = from_lower(modes, axis, pair_ref, taps_ref, decays_ref, residues_ref, skip_ref)
    for j in range(2):
        gate_ref[j] = at_top(gate_ref[j], gate_gain[j])
        base_ref[j] = at_top(base_ref[j], base_gain[j])
    across = jnp.exp(-rates * (inside * float(positions)))
    for m in range(modes):
        fade = fades(decays_ref, run, m)
        begin_ref[m] = spread[m] * (state_ref[m] + fade * over_sublanes(arrived[m : m + 1, :]))
        reach_ref[m] = spread[m] * fade * over_sublanes(across[m : m + 1, :])


def join_kernel(
    modes, axis, own_ref, other_ref, q_half, product_ref, state_ref, taps_ref, decays_ref, residues_ref, skip_ref,
    sent_ref, pair_ref, *refs,
):
    positions = q_half.shape[0]
    below, above = other_ref[...], own_ref[...]
    pair_ref[0] = below
    pair_ref[1] = above
    first, second = pair_boundary(modes, taps_ref, pair_ref.at[0], pair_ref.at[1])
    rates = decays_ref[...]
    state = jnp.exp(-float(positions) * rates) * below[:modes] + above[:modes]
    state = state + jnp.exp(-float(positions - 1) * rates) * first + jnp.exp(-float(positions - 2) * rates) * second
    row = lax.broadcasted_iota(jnp.int32, (EXTRA, LANES), 0)
    beside = jnp.where(row < K_FIRST, above[modes:], below[modes:])
    rows = jnp.concatenate([state, beside], 0).astype(BF16)
    sent_ref[...] = jnp.broadcast_to(rows[None], sent_ref.shape)

    @pl.when(starts_early(axis))
    def _():
        params = (taps_ref, decays_ref, residues_ref, skip_ref)
        local_work(modes, axis, q_half, product_ref, state_ref, pair_ref, *params, *refs)


def enter_kernel(
    modes, axis, received_ref, q_half, product_ref, state_ref, pair_ref, taps_ref, decays_ref, residues_ref, skip_ref, *refs
):
    enter_ref, local_refs, (rows_ref, first_ref, second_ref, q_ref) = refs[0], refs[1:5], refs[5:]
    positions = q_half.shape[0]
    device = lax.axis_index(axis)
    pair = device // PAIR
    upper = lax.rem(device, PAIR) == 1

    @pl.when(jnp.logical_not(jnp.logical_or(upper, starts_early(axis))))
    def _():
        params = (taps_ref, decays_ref, residues_ref, skip_ref)
        local_work(modes, axis, q_half, product_ref, state_ref, pair_ref, *params, *local_refs, q_ref)

    enter_ref[...] = jnp.zeros_like(enter_ref)

    @pl.when(upper)
    def _():
        pairs = received_ref.shape[0]
        pitch = modes + EXTRA
        rows_ref[0:pitch, :] = jnp.zeros((pitch, LANES), F32)
        for slot, e in enumerate(pair_order(pairs)):
            rows_ref[pitch * (e + 1) : pitch * (e + 2), :] = received_ref[slot].astype(F32)

        def of_all(row, block):
            return tuple(rows_ref[pl.ds(pitch * block + modes + row + i, pairs, stride=pitch), :] for i in range(2))

        last = [of_all(row, 0) for row in (K_LAST, V_LAST)]
        begun = [of_all(row, 1) for row in (K_FIRST, V_FIRST)]
        first_ref[...], second_ref[...] = boundary(taps_ref, last, begun)

        rates = decays_ref[...]
        length = PAIR * positions
        across = jnp.exp(-float(length) * rates)
        late_first = jnp.exp(-float(length - 1) * rates)
        late_second = jnp.exp(-float(length - 2) * rates)
        state = jnp.zeros((modes, LANES), F32)
        for e in range(pairs - 1):
            sent = rows_ref[pitch * (e + 1) : pitch * (e + 1) + modes, :]
            sent = sent + late_first * first_ref[e : e + 1, :] + late_second * second_ref[e : e + 1, :]
            state = jnp.where(e < pair, across * state + sent, state)
        first, second = first_ref[pl.ds(pair, 1), :], second_ref[pl.ds(pair, 1), :]
        enter_ref[:modes, :] = state + jnp.exp(rates) * first + jnp.exp(2.0 * rates) * second
        enter_ref[modes : modes + 1, :] = first
        enter_ref[modes + 1 : modes + 2, :] = second
        for i in range(2):
            enter_ref[modes + 2 + i : modes + 3 + i, :] = rows_ref[pl.ds(pair * pitch + modes + Q_LAST + i, 1), :]
        enter_ref[modes + 4 :, :] = jnp.zeros((EDGE - 4, LANES), F32)


def carry_kernel(modes, axis, half, *refs):
    mine = lax.rem(lax.axis_index(axis), PAIR) == half
    if half == 0:
        *refs, power_in_ref, power_ref, gated_ref = refs

        @pl.when(jnp.logical_not(mine))
        def _():
            power_ref[...] = power_in_ref[...]

        refs = (*refs, power_ref, gated_ref)

    @pl.when(mine)
    def _():
        carry_work(modes, axis, half, *refs)


def carry_work(modes, axis, half, enter_ref, *refs):
    early_locals, refs = refs[:4], refs[4:]
    if half:
        (q_half, product_ref, state_ref, pair_ref), refs = refs[:4], refs[4:]
        taps_ref, decays_ref, residues_ref, skip_ref, power_ref, gated_ref, q_ref = refs
    else:
        locals_, refs = refs[:4], refs[4:]
        taps_ref, decays_ref, residues_ref, skip_ref, power_ref, gated_ref = refs
    run = early_locals[0].shape[0]
    positions = run * CHUNKS
    rates = decays_ref[...]
    state = enter_ref[:modes, :]
    weights = mode_weights(decays_ref, residues_ref)
    if half:
        edges = from_lower(modes, axis, pair_ref, taps_ref, decays_ref, residues_ref, skip_ref)
    else:
        edge = (enter_ref[modes + i : modes + i + 1, :] for i in range(4))
        gains = edge_gains(taps_ref, skip_ref, rates, weights, *edge)
    factors = split(jnp.exp(-rates))

    def put(j, gate, base, terms, more):
        if more is not None:
            gate, base = at_top(gate, more[0]), at_top(base, more[1])
        gated_ref[pl.ds(j, CHUNKS, stride=SPAN), :] = gate * added([base] + terms)

    def over_steps(step, held, gains, unroll):
        for j in range(2):
            held = step(j, held, gains and (gains[0][j], gains[1][j]))
        lax.fori_loop(2, run, lambda j, held: step(j, held, None), held, unroll=unroll)

    early = starts_early(axis)

    def from_local(gate_ref, base_ref, begin_ref, reach_ref):
        def step(j, carried, more):
            carried = tuple(a * g for a, g in zip(factors, carried))
            put(j, gate_ref[j], base_ref[j], list(carried), more)
            return carried

        carried = tuple(begin_ref[m] + reach_ref[m] * over_sublanes(state[m : m + 1, :]) for m in range(modes))
        over_steps(step, carried, None if half else gains, 14)

    @pl.when(early)
    def _():
        from_local(*early_locals)

    @pl.when(jnp.logical_not(early))
    def _():
        if not half:
            from_local(*locals_)
            return
        taps, before = load_gate(q_ref, q_half, taps_ref)
        skip = over_sublanes(skip_ref[...])
        spread = split(weights)
        arrived, *more_gains = edges
        arrived = arrived + jnp.exp(-rates * float(positions)) * state
        states = tuple(
            state_ref[m] + fades(decays_ref, run, m) * over_sublanes(arrived[m : m + 1, :]) for m in range(modes)
        )

        def step(j, held, more):
            q1, q2, states = held
            q0 = strided(q_ref, j, PITCH)
            product = product_ref[j]
            states = tuple(a * h + product for a, h in zip(factors, states))
            gate = taps[0] * q0 + taps[1] * q1 + taps[2] * q2
            put(j, gate, skip * product, [w * h for w, h in zip(spread, states)], more)
            return q0, q1, states

        over_steps(step, (*before, states), more_gains, 6)

    ones = jnp.ones((LANES, LANES), BF16)
    lane = lax.broadcasted_iota(jnp.int32, (CHUNKS, LANES), 1)
    power = jnp.zeros((CHUNKS, LANES), F32)
    tiles = run // CHUNKS
    for s in range(CHUNKS):
        gated = gated_ref[s * SPAN : s * SPAN + run, :]
        square = gated * gated
        high = square.astype(BF16)
        low = (square - high.astype(F32)).astype(BF16)
        sums = jnp.dot(high, ones, preferred_element_type=F32) + jnp.dot(low, ones, preferred_element_type=F32)
        for i in range(tiles):
            power = jnp.where(lane == s * tiles + i, sums[i * CHUNKS : (i + 1) * CHUNKS, :], power)
    power_ref[...] = jnp.broadcast_to(power[None], power_ref.shape)


def finish_kernel(channels, axis, power_ref, upper_ref, lower_ref, gain_ref, mixed_ref):
    run = mixed_ref.shape[0] // CHUNKS
    tiles = run // CHUNKS
    inverse = lax.rsqrt(jnp.sum(power_ref[...], 0) / channels + 1e-05)
    gain = over_sublanes(gain_ref[...])

    def scale(gated_ref):
        for s in range(CHUNKS):
            for i in range(0, tiles, 2):
                halves = []
                for h in (i, i + 1):
                    gated = gated_ref[s * SPAN + h * CHUNKS : s * SPAN + (h + 1) * CHUNKS, :]
                    halves.append(gated * gain * inverse[:, s * tiles + h : s * tiles + h + 1])
                rows = slice(s * run + i * CHUNKS, s * run + (i + 2) * CHUNKS)
                mixed_ref[rows, :] = jnp.concatenate(halves, 0).astype(BF16)

    for half, ref in enumerate((lower_ref, upper_ref)):
        pl.when(lax.rem(lax.axis_index(axis), PAIR) == half)(functools.partial(scale, ref))


def per_device(projections, short_filter, residues, decays, skip, gain):
    positions, _, width = projections.shape
    modes = decays.shape[0]
    ctx_count = lax.axis_size("ctx")
    tp_count = lax.axis_size("tp")
    pairs = ctx_count // PAIR
    run = positions // CHUNKS
    x = jnp.swapaxes(projections, 0, 1)

    def shape(*extent, kind=F32):
        return jax.ShapeDtypeStruct(extent, kind)

    def call(kernel, name, out_shape, in_specs, scratch, *operands):
        return pl.pallas_call(
            kernel,
            out_shape=out_shape,
            in_specs=in_specs,
            out_specs=jax.tree.map(lambda _: VMEM, out_shape),
            scratch_shapes=scratch,
            compiler_params=pltpu.CompilerParams(vmem_limit_bytes=VMEM_LIMIT),
            name=name,
        )(*operands)

    block = shape(run, CHUNKS, width)
    table = shape(modes, CHUNKS, width)
    sources = (x, short_filter, decays, residues, skip[None, :], gain[None, :])
    rows, product, state, q, short_filter, decays, residues, skip, gain = call(
        functools.partial(states_kernel, modes),
        "states",
        (shape(modes + EXTRA, width), block, table, shape(positions, width, kind=BF16))
        + tuple(shape(*s.shape) for s in sources[1:]),
        [ANY] * 6,
        [
            pltpu.VMEM((positions, width), BF16),
            pltpu.VMEM((positions, width), BF16),
            pltpu.VMEM((PITCH * (CHUNKS + 1), width), F32),
            pltpu.VMEM((PITCH * (CHUNKS + 1), width), F32),
            pltpu.VMEM((3, modes, width), F32),
            pltpu.SemaphoreType.DMA((8,)),
        ],
        *[pltpu.with_memory_space_constraint(s, pltpu.HBM) for s in sources],
    )
    partners = [(i, i + 1 - 2 * (i % PAIR)) for i in range(ctx_count)]
    other = lax.ppermute(rows, "ctx", partners)
    params = (short_filter, decays, residues, skip)
    pitched = pltpu.VMEM((PITCH * (CHUNKS + 1), width), F32)
    sent, joined, *early_locals = call(
        functools.partial(join_kernel, modes, "ctx"),
        "join",
        (shape(pairs, modes + EXTRA, width, kind=BF16), shape(PAIR, modes + EXTRA, width), block, block, table, table),
        [VMEM] * 9,
        [pitched],
        rows,
        other,
        q,
        product,
        state,
        *params,
    )
    received = lax.all_to_all(
        sent, ("ctx", "tp"), split_axis=0, concat_axis=0, tiled=True, axis_index_groups=ctx_groups(pairs, tp_count)
    )
    enter_shape = shape(modes + EDGE, width)
    local_shapes = (block, block, table, table)
    enter, *locals_ = call(
        functools.partial(enter_kernel, modes, "ctx"),
        "enter",
        (enter_shape, *local_shapes),
        [VMEM] * 9,
        [
            pltpu.VMEM(((pairs + 2) * (modes + EXTRA), width), F32),
            pltpu.VMEM((pairs, width), F32),
            pltpu.VMEM((pairs, width), F32),
            pitched,
        ],
        received,
        q,
        product,
        state,
        joined,
        *params,
    )
    entered = lax.ppermute(enter, "ctx", partners)
    carry_shapes = (shape(tp_count, CHUNKS, run), shape(SPAN * (CHUNKS + 1), width))
    power, upper_gated = call(
        functools.partial(carry_kernel, modes, "ctx", 1),
        "upper",
        carry_shapes,
        [VMEM] * 13,
        [pitched],
        enter,
        *early_locals,
        q,
        product,
        state,
        joined,
        *params,
    )
    power, lower_gated = call(
        functools.partial(carry_kernel, modes, "ctx", 0),
        "lower",
        carry_shapes,
        [VMEM] * 14,
        [],
        entered,
        *early_locals,
        *locals_,
        *params,
        power,
    )
    powers = lax.all_to_all(
        power, "tp", split_axis=0, concat_axis=0, tiled=True, axis_index_groups=[slice_order(tp_count)]
    )
    return call(
        functools.partial(finish_kernel, width * tp_count, "ctx"),
        "finish",
        shape(positions, width, kind=BF16),
        [VMEM] * 4,
        [],
        powers,
        upper_gated,
        lower_gated,
        gain,
    )


def solution(mesh):
    in_specs = (
        P("ctx", None, "tp"),
        P(None, None, "tp"),
        P(None, "tp"),
        P(None, "tp"),
        P("tp"),
        P("tp"),
    )
    return jax.shard_map(per_device, mesh=mesh, in_specs=in_specs, out_specs=P("ctx", "tp"), check_vma=False)
```

```python
import functools

import jax
import jax.numpy as jnp
from jax import lax
from jax.experimental import pallas as pl
from jax.experimental.pallas import tpu as pltpu
from jax.sharding import PartitionSpec as P

F32 = jnp.float32
BF16 = jnp.bfloat16
CHUNKS = 8
LANES = 128
PAIR = 2
VMEM_LIMIT = 40 * 1024 * 1024
VMEM = pl.BlockSpec(memory_space=pltpu.VMEM)
ANY = pl.BlockSpec(memory_space=pl.ANY)

FIRST_PAIR = 10
FIRST_SLICE = 5
GRID = 4
PITCH = 137
SPAN = 136

K_LAST, V_LAST, Q_LAST, K_FIRST, V_FIRST = 0, 2, 4, 6, 8
EXTRA = 16
EDGE = 8


def first_then(first, members, distance):
    return [first] + sorted((i for i in range(members) if i != first), key=lambda i: -distance(i, first))


def around(a, b, size):
    return min((a - b) % size, (b - a) % size)


def pair_order(pairs):
    def distance(a, b):
        return around(a // GRID, b // GRID, max(pairs // GRID, 1)) + 2 * around(a % GRID, b % GRID, GRID)

    return first_then(FIRST_PAIR % pairs, pairs, distance)


def ctx_groups(pairs, slices):
    def index(pair, half, piece):
        return (pair * PAIR + half) * slices + piece

    groups = [[index(p, PAIR - 1, piece) for p in pair_order(pairs)] for piece in range(slices)]
    rest = [(p % GRID, p // GRID // 2, -index(p, 0, piece)) for p in range(pairs) for piece in range(slices)]
    rest = [-i for *_, i in sorted(rest)]
    return groups + [rest[i : i + pairs] for i in range(0, len(rest), pairs)]


def slice_order(slices):
    return first_then(FIRST_SLICE % slices, slices, lambda a, b: 0)


def over_sublanes(row):
    return jnp.broadcast_to(row, (CHUNKS, LANES))


def sublane_index():
    return lax.broadcasted_iota(jnp.int32, (CHUNKS, LANES), 0)


def next_chunk(block, distance=1):
    rolled = pltpu.roll(block, distance, 0)
    return jnp.where(sublane_index() >= distance, rolled, 0.0)


def strided(ref, step, run):
    return ref[pl.ds(step, CHUNKS, stride=run), :]


def added(terms):
    while len(terms) > 1:
        pairs = [terms[i] + terms[i + 1] for i in range(0, len(terms) - 1, 2)]
        terms = pairs + terms[2 * len(pairs) :]
    return terms[0]


def boundary(taps_ref, last, first):
    products = []
    for j in (1, 2):
        tap = [taps_ref[j, i : i + 1, :] for i in range(3)]
        (far, near), (zero, one) = last[j - 1], first[j - 1]
        own = (tap[0] * zero, tap[0] * one + tap[1] * zero)
        gained = (tap[1] * near + tap[2] * far, tap[2] * near)
        products.append((own, gained))
    (k_own, k_gained), (v_own, v_gained) = products
    return [k_own[i] * v_gained[i] + k_gained[i] * (v_own[i] + v_gained[i]) for i in range(2)]


def two_rows(ref, row):
    return ref[row : row + 1, :], ref[row + 1 : row + 2, :]


def pair_boundary(modes, taps_ref, lower_ref, upper_ref):
    last = [two_rows(lower_ref, modes + row) for row in (K_LAST, V_LAST)]
    first = [two_rows(upper_ref, modes + row) for row in (K_FIRST, V_FIRST)]
    return boundary(taps_ref, last, first)


def states_kernel(modes, *refs):
    sources, refs = refs[:6], refs[6:]
    x_hbm = sources[0]
    (rows_ref, product_ref, state_ref, q_ref), refs = refs[:4], refs[4:]
    params, refs = refs[:5], refs[5:]
    taps_ref, decays_ref = params[0], params[1]
    k_half, v_half, k_ref, v_ref, jump_ref, semaphores = refs
    copies = [pltpu.make_async_copy(s, d, semaphores.at[i]) for i, (s, d) in enumerate(zip(sources[1:], params))]
    streams = [
        pltpu.make_async_copy(x_hbm.at[j], d, semaphores.at[5 + j]) for j, d in enumerate((q_ref, k_half, v_half))
    ]
    for copy in (streams[1], streams[2], copies[1], copies[0], streams[0], copies[2], copies[3], copies[4]):
        copy.start()
    positions = q_ref.shape[0]
    run = positions // CHUNKS
    copies[1].wait()
    copies[0].wait()
    k_taps = [over_sublanes(taps_ref[1, i : i + 1, :]) for i in range(3)]
    v_taps = [over_sublanes(taps_ref[2, i : i + 1, :]) for i in range(3)]
    rates = decays_ref[...]
    factor = jnp.exp(-rates)
    factors = [over_sublanes(factor[m : m + 1, :]) for m in range(modes)]
    for i in range(3):
        jump_ref[i] = jnp.exp(-float(run << i) * rates)
    streams[1].wait()
    for s in range(CHUNKS):
        k_ref[s * PITCH : s * PITCH + run, :] = k_half[s * run : (s + 1) * run, :].astype(F32)
    streams[2].wait()
    for s in range(CHUNKS):
        v_ref[s * PITCH : s * PITCH + run, :] = v_half[s * run : (s + 1) * run, :].astype(F32)

    def step(j, carry):
        k1, k2, v1, v2, states = carry
        k0 = strided(k_ref, j, PITCH)
        v0 = strided(v_ref, j, PITCH)
        k = k_taps[0] * k0 + k_taps[1] * k1 + k_taps[2] * k2
        v = v_taps[0] * v0 + v_taps[1] * v1 + v_taps[2] * v2
        product = k * v
        product_ref[j] = product
        states = tuple(a * h + product for a, h in zip(factors, states))
        return k0, k1, v0, v1, states

    start = (
        next_chunk(strided(k_ref, run - 1, PITCH)),
        next_chunk(strided(k_ref, run - 2, PITCH)),
        next_chunk(strided(v_ref, run - 1, PITCH)),
        next_chunk(strided(v_ref, run - 2, PITCH)),
        tuple(jnp.zeros((CHUNKS, LANES), F32) for _ in range(modes)),
    )
    states = lax.fori_loop(0, run, step, start, unroll=16)[4]
    for m in range(modes):
        total = states[m]
        for i in range(3):
            total = total + over_sublanes(jump_ref[i, m : m + 1, :]) * next_chunk(total, 1 << i)
        state_ref[m] = next_chunk(total)
        rows_ref[m : m + 1, :] = total[CHUNKS - 1 : CHUNKS, :]
    streams[0].wait()
    rows_ref[modes + K_LAST : modes + K_LAST + 2, :] = k_ref[7 * PITCH + run - 2 : 7 * PITCH + run, :]
    rows_ref[modes + V_LAST : modes + V_LAST + 2, :] = v_ref[7 * PITCH + run - 2 : 7 * PITCH + run, :]
    rows_ref[modes + Q_LAST : modes + Q_LAST + 2, :] = q_ref[positions - 16 : positions, :].astype(F32)[14:16]
    rows_ref[modes + K_FIRST : modes + K_FIRST + 2, :] = k_ref[0:2, :]
    rows_ref[modes + V_FIRST : modes + V_FIRST + 2, :] = v_ref[0:2, :]
    rows_ref[modes + V_FIRST + 2 :, :] = jnp.zeros((EXTRA - V_FIRST - 2, LANES), F32)
    for i in (2, 3, 4):
        copies[i].wait()


def starts_early(axis):
    pair = lax.axis_index(axis) // PAIR
    y, z = pair // GRID, lax.rem(pair, GRID)
    return jnp.logical_or(z < 1, jnp.logical_and(z < 2, y < 2))


def mode_weights(decays_ref, residues_ref):
    return residues_ref[...] * jnp.sqrt(2.0 * decays_ref[...])


def edge_gains(taps_ref, skip_ref, rates, weights, first, second, far, near):
    early = jnp.sum(weights * jnp.exp(rates), 0, keepdims=True) * second
    skip = skip_ref[...]
    gate = (taps_ref[0, 1:2, :] * near + taps_ref[0, 2:3, :] * far, taps_ref[0, 2:3, :] * near)
    return gate, (skip * first - early, skip * second)


def from_lower(modes, axis, pair_ref, taps_ref, decays_ref, residues_ref, skip_ref):
    inside = lax.rem(lax.axis_index(axis), PAIR).astype(F32)
    rates = decays_ref[...]
    first, second = (inside * p for p in pair_boundary(modes, taps_ref, pair_ref.at[0], pair_ref.at[1]))
    state = inside * pair_ref[0, :modes, :] + jnp.exp(rates) * first + jnp.exp(2.0 * rates) * second
    far, near = (inside * row for row in two_rows(pair_ref.at[0], modes + Q_LAST))
    weights = mode_weights(decays_ref, residues_ref)
    return state, *edge_gains(taps_ref, skip_ref, rates, weights, first, second, far, near)


def at_top(block, row):
    return block + jnp.where(sublane_index() == 0, over_sublanes(row), 0.0)


def fades(decays_ref, run, m):
    return jnp.exp(over_sublanes(decays_ref[m : m + 1, :]) * (sublane_index().astype(F32) * -float(run)))


def load_gate(q_ref, q_half, taps_ref):
    run = q_half.shape[0] // CHUNKS
    for s in range(CHUNKS):
        q_ref[s * PITCH : s * PITCH + run, :] = q_half[s * run : (s + 1) * run, :].astype(F32)
    taps = [over_sublanes(taps_ref[0, i : i + 1, :]) for i in range(3)]
    return taps, [next_chunk(strided(q_ref, run - 1 - i, PITCH)) for i in range(2)]


def split(table):
    return [over_sublanes(table[m : m + 1, :]) for m in range(table.shape[0])]


def local_work(
    modes, axis, q_half, product_ref, state_ref, pair_ref, taps_ref, decays_ref, residues_ref, skip_ref,
    gate_ref, base_ref, begin_ref, reach_ref, q_ref,
):
    run = product_ref.shape[0]
    positions = run * CHUNKS
    inside = lax.rem(lax.axis_index(axis), PAIR).astype(F32)
    rates = decays_ref[...]
    spread = split(mode_weights(decays_ref, residues_ref))
    factors = split(jnp.exp(-rates))
    skip = over_sublanes(skip_ref[...])
    taps, before = load_gate(q_ref, q_half, taps_ref)

    def step(j, carry):
        q1, q2, states = carry
        q0 = strided(q_ref, j, PITCH)
        gate_ref[j] = taps[0] * q0 + taps[1] * q1 + taps[2] * q2
        product = product_ref[j]
        states = tuple(a * h + product for a, h in zip(factors, states))
        base_ref[j] = added([skip * product] + [w * h for w, h in zip(spread, states)])
        return q0, q1, states

    start = (*before, tuple(jnp.zeros((CHUNKS, LANES), F32) for _ in range(modes)))
    lax.fori_loop(0, run, step, start, unroll=4)

    arrived, gate_gain, base_gain = from_lower(modes, axis, pair_ref, taps_ref, decays_ref, residues_ref, skip_ref)
    for j in range(2):
        gate_ref[j] = at_top(gate_ref[j], gate_gain[j])
        base_ref[j] = at_top(base_ref[j], base_gain[j])
    across = jnp.exp(-rates * (inside * float(positions)))
    for m in range(modes):
        fade = fades(decays_ref, run, m)
        begin_ref[m] = spread[m] * (state_ref[m] + fade * over_sublanes(arrived[m : m + 1, :]))
        reach_ref[m] = spread[m] * fade * over_sublanes(across[m : m + 1, :])


def join_kernel(
    modes, axis, own_ref, other_ref, q_half, product_ref, state_ref, taps_ref, decays_ref, residues_ref, skip_ref,
    sent_ref, pair_ref, *refs,
):
    positions = q_half.shape[0]
    below, above = other_ref[...], own_ref[...]
    pair_ref[0] = below
    pair_ref[1] = above
    first, second = pair_boundary(modes, taps_ref, pair_ref.at[0], pair_ref.at[1])
    rates = decays_ref[...]
    state = jnp.exp(-float(positions) * rates) * below[:modes] + above[:modes]
    state = state + jnp.exp(-float(positions - 1) * rates) * first + jnp.exp(-float(positions - 2) * rates) * second
    row = lax.broadcasted_iota(jnp.int32, (EXTRA, LANES), 0)
    beside = jnp.where(row < K_FIRST, above[modes:], below[modes:])
    rows = jnp.concatenate([state, beside], 0).astype(BF16)
    sent_ref[...] = jnp.broadcast_to(rows[None], sent_ref.shape)

    @pl.when(starts_early(axis))
    def _():
        params = (taps_ref, decays_ref, residues_ref, skip_ref)
        local_work(modes, axis, q_half, product_ref, state_ref, pair_ref, *params, *refs)


def enter_kernel(
    modes, axis, received_ref, q_half, product_ref, state_ref, pair_ref, taps_ref, decays_ref, residues_ref, skip_ref, *refs
):
    enter_ref, local_refs, (rows_ref, first_ref, second_ref, q_ref) = refs[0], refs[1:5], refs[5:]
    positions = q_half.shape[0]
    device = lax.axis_index(axis)
    pair = device // PAIR
    upper = lax.rem(device, PAIR) == 1

    @pl.when(jnp.logical_not(jnp.logical_or(upper, starts_early(axis))))
    def _():
        params = (taps_ref, decays_ref, residues_ref, skip_ref)
        local_work(modes, axis, q_half, product_ref, state_ref, pair_ref, *params, *local_refs, q_ref)

    enter_ref[...] = jnp.zeros_like(enter_ref)

    @pl.when(upper)
    def _():
        pairs = received_ref.shape[0]
        pitch = modes + EXTRA
        rows_ref[0:pitch, :] = jnp.zeros((pitch, LANES), F32)
        for slot, e in enumerate(pair_order(pairs)):
            rows_ref[pitch * (e + 1) : pitch * (e + 2), :] = received_ref[slot].astype(F32)

        def of_all(row, block):
            return tuple(rows_ref[pl.ds(pitch * block + modes + row + i, pairs, stride=pitch), :] for i in range(2))

        last = [of_all(row, 0) for row in (K_LAST, V_LAST)]
        begun = [of_all(row, 1) for row in (K_FIRST, V_FIRST)]
        first_ref[...], second_ref[...] = boundary(taps_ref, last, begun)

        rates = decays_ref[...]
        length = PAIR * positions
        across = jnp.exp(-float(length) * rates)
        late_first = jnp.exp(-float(length - 1) * rates)
        late_second = jnp.exp(-float(length - 2) * rates)
        state = jnp.zeros((modes, LANES), F32)
        for e in range(pairs - 1):
            sent = rows_ref[pitch * (e + 1) : pitch * (e + 1) + modes, :]
            sent = sent + late_first * first_ref[e : e + 1, :] + late_second * second_ref[e : e + 1, :]
            state = jnp.where(e < pair, across * state + sent, state)
        first, second = first_ref[pl.ds(pair, 1), :], second_ref[pl.ds(pair, 1), :]
        enter_ref[:modes, :] = state + jnp.exp(rates) * first + jnp.exp(2.0 * rates) * second
        enter_ref[modes : modes + 1, :] = first
        enter_ref[modes + 1 : modes + 2, :] = second
        for i in range(2):
            enter_ref[modes + 2 + i : modes + 3 + i, :] = rows_ref[pl.ds(pair * pitch + modes + Q_LAST + i, 1), :]
        enter_ref[modes + 4 :, :] = jnp.zeros((EDGE - 4, LANES), F32)


def carry_kernel(modes, axis, half, *refs):
    mine = lax.rem(lax.axis_index(axis), PAIR) == half
    if half == 0:
        *refs, power_in_ref, power_ref, gated_ref = refs

        @pl.when(jnp.logical_not(mine))
        def _():
            power_ref[...] = power_in_ref[...]

        refs = (*refs, power_ref, gated_ref)

    @pl.when(mine)
    def _():
        carry_work(modes, axis, half, *refs)


def carry_work(modes, axis, half, enter_ref, *refs):
    early_locals, refs = refs[:4], refs[4:]
    if half:
        (q_half, product_ref, state_ref, pair_ref), refs = refs[:4], refs[4:]
        taps_ref, decays_ref, residues_ref, skip_ref, power_ref, gated_ref, q_ref = refs
    else:
        locals_, refs = refs[:4], refs[4:]
        taps_ref, decays_ref, residues_ref, skip_ref, power_ref, gated_ref = refs
    run = early_locals[0].shape[0]
    positions = run * CHUNKS
    rates = decays_ref[...]
    state = enter_ref[:modes, :]
    weights = mode_weights(decays_ref, residues_ref)
    if half:
        edges = from_lower(modes, axis, pair_ref, taps_ref, decays_ref, residues_ref, skip_ref)
    else:
        edge = (enter_ref[modes + i : modes + i + 1, :] for i in range(4))
        gains = edge_gains(taps_ref, skip_ref, rates, weights, *edge)
    factors = split(jnp.exp(-rates))

    def put(j, gate, base, terms, more):
        if more is not None:
            gate, base = at_top(gate, more[0]), at_top(base, more[1])
        gated_ref[pl.ds(j, CHUNKS, stride=SPAN), :] = gate * added([base] + terms)

    def over_steps(step, held, gains, unroll):
        for j in range(2):
            held = step(j, held, gains and (gains[0][j], gains[1][j]))
        lax.fori_loop(2, run, lambda j, held: step(j, held, None), held, unroll=unroll)

    early = starts_early(axis)

    def from_local(gate_ref, base_ref, begin_ref, reach_ref):
        def step(j, carried, more):
            carried = tuple(a * g for a, g in zip(factors, carried))
            put(j, gate_ref[j], base_ref[j], list(carried), more)
            return carried

        carried = tuple(begin_ref[m] + reach_ref[m] * over_sublanes(state[m : m + 1, :]) for m in range(modes))
        over_steps(step, carried, None if half else gains, 42)

    @pl.when(early)
    def _():
        from_local(*early_locals)

    @pl.when(jnp.logical_not(early))
    def _():
        if not half:
            from_local(*locals_)
            return
        taps, before = load_gate(q_ref, q_half, taps_ref)
        skip = over_sublanes(skip_ref[...])
        spread = split(weights)
        arrived, *more_gains = edges
        arrived = arrived + jnp.exp(-rates * float(positions)) * state
        states = tuple(
            state_ref[m] + fades(decays_ref, run, m) * over_sublanes(arrived[m : m + 1, :]) for m in range(modes)
        )

        def step(j, held, more):
            q1, q2, states = held
            q0 = strided(q_ref, j, PITCH)
            product = product_ref[j]
            states = tuple(a * h + product for a, h in zip(factors, states))
            gate = taps[0] * q0 + taps[1] * q1 + taps[2] * q2
            put(j, gate, skip * product, [w * h for w, h in zip(spread, states)], more)
            return q0, q1, states

        over_steps(step, (*before, states), more_gains, 6)

    ones = jnp.ones((LANES, LANES), BF16)
    lane = lax.broadcasted_iota(jnp.int32, (CHUNKS, LANES), 1)
    power = jnp.zeros((CHUNKS, LANES), F32)
    tiles = run // CHUNKS
    for s in range(CHUNKS):
        gated = gated_ref[s * SPAN : s * SPAN + run, :]
        square = gated * gated
        sums = jnp.dot(square.astype(BF16), ones, preferred_element_type=F32)
        for i in range(tiles):
            power = jnp.where(lane == s * tiles + i, sums[i * CHUNKS : (i + 1) * CHUNKS, :], power)
    power_ref[...] = jnp.broadcast_to(power[None], power_ref.shape)


def finish_kernel(channels, axis, power_ref, upper_ref, lower_ref, gain_ref, mixed_ref):
    run = mixed_ref.shape[0] // CHUNKS
    tiles = run // CHUNKS
    inverse = lax.rsqrt(jnp.sum(power_ref[...], 0) / channels + 1e-05)
    gain = over_sublanes(gain_ref[...])

    def scale(gated_ref):
        for s in range(CHUNKS):
            for i in range(0, tiles, 2):
                halves = []
                for h in (i, i + 1):
                    gated = gated_ref[s * SPAN + h * CHUNKS : s * SPAN + (h + 1) * CHUNKS, :]
                    halves.append(gated * gain * inverse[:, s * tiles + h : s * tiles + h + 1])
                rows = slice(s * run + i * CHUNKS, s * run + (i + 2) * CHUNKS)
                mixed_ref[rows, :] = jnp.concatenate(halves, 0).astype(BF16)

    for half, ref in enumerate((lower_ref, upper_ref)):
        pl.when(lax.rem(lax.axis_index(axis), PAIR) == half)(functools.partial(scale, ref))


def per_device(projections, short_filter, residues, decays, skip, gain):
    positions, _, width = projections.shape
    modes = decays.shape[0]
    ctx_count = lax.axis_size("ctx")
    tp_count = lax.axis_size("tp")
    pairs = ctx_count // PAIR
    run = positions // CHUNKS
    x = jnp.swapaxes(projections, 0, 1)

    def shape(*extent, kind=F32):
        return jax.ShapeDtypeStruct(extent, kind)

    def call(kernel, name, out_shape, in_specs, scratch, *operands):
        return pl.pallas_call(
            kernel,
            out_shape=out_shape,
            in_specs=in_specs,
            out_specs=jax.tree.map(lambda _: VMEM, out_shape),
            scratch_shapes=scratch,
            compiler_params=pltpu.CompilerParams(vmem_limit_bytes=VMEM_LIMIT),
            name=name,
        )(*operands)

    block = shape(run, CHUNKS, width)
    table = shape(modes, CHUNKS, width)
    sources = (x, short_filter, decays, residues, skip[None, :], gain[None, :])
    rows, product, state, q, short_filter, decays, residues, skip, gain = call(
        functools.partial(states_kernel, modes),
        "states",
        (shape(modes + EXTRA, width), block, table, shape(positions, width, kind=BF16))
        + tuple(shape(*s.shape) for s in sources[1:]),
        [ANY] * 6,
        [
            pltpu.VMEM((positions, width), BF16),
            pltpu.VMEM((positions, width), BF16),
            pltpu.VMEM((PITCH * (CHUNKS + 1), width), F32),
            pltpu.VMEM((PITCH * (CHUNKS + 1), width), F32),
            pltpu.VMEM((3, modes, width), F32),
            pltpu.SemaphoreType.DMA((8,)),
        ],
        *[pltpu.with_memory_space_constraint(s, pltpu.HBM) for s in sources],
    )
    partners = [(i, i + 1 - 2 * (i % PAIR)) for i in range(ctx_count)]
    other = lax.ppermute(rows, "ctx", partners)
    params = (short_filter, decays, residues, skip)
    pitched = pltpu.VMEM((PITCH * (CHUNKS + 1), width), F32)
    sent, joined, *early_locals = call(
        functools.partial(join_kernel, modes, "ctx"),
        "join",
        (shape(pairs, modes + EXTRA, width, kind=BF16), shape(PAIR, modes + EXTRA, width), block, block, table, table),
        [VMEM] * 9,
        [pitched],
        rows,
        other,
        q,
        product,
        state,
        *params,
    )
    received = lax.all_to_all(
        sent, ("ctx", "tp"), split_axis=0, concat_axis=0, tiled=True, axis_index_groups=ctx_groups(pairs, tp_count)
    )
    enter_shape = shape(modes + EDGE, width)
    local_shapes = (block, block, table, table)
    enter, *locals_ = call(
        functools.partial(enter_kernel, modes, "ctx"),
        "enter",
        (enter_shape, *local_shapes),
        [VMEM] * 9,
        [
            pltpu.VMEM(((pairs + 2) * (modes + EXTRA), width), F32),
            pltpu.VMEM((pairs, width), F32),
            pltpu.VMEM((pairs, width), F32),
            pitched,
        ],
        received,
        q,
        product,
        state,
        joined,
        *params,
    )
    entered = lax.ppermute(enter, "ctx", partners)
    carry_shapes = (shape(tp_count, CHUNKS, run), shape(SPAN * (CHUNKS + 1), width))
    power, upper_gated = call(
        functools.partial(carry_kernel, modes, "ctx", 1),
        "upper",
        carry_shapes,
        [VMEM] * 13,
        [pitched],
        enter,
        *early_locals,
        q,
        product,
        state,
        joined,
        *params,
    )
    power, lower_gated = call(
        functools.partial(carry_kernel, modes, "ctx", 0),
        "lower",
        carry_shapes,
        [VMEM] * 14,
        [],
        entered,
        *early_locals,
        *locals_,
        *params,
        power,
    )
    powers = lax.all_to_all(
        power, "tp", split_axis=0, concat_axis=0, tiled=True, axis_index_groups=[slice_order(tp_count)]
    )
    return call(
        functools.partial(finish_kernel, width * tp_count, "ctx"),
        "finish",
        shape(positions, width, kind=BF16),
        [VMEM] * 4,
        [],
        powers,
        upper_gated,
        lower_gated,
        gain,
    )


def solution(mesh):
    in_specs = (
        P("ctx", None, "tp"),
        P(None, None, "tp"),
        P(None, "tp"),
        P(None, "tp"),
        P("tp"),
        P("tp"),
    )
    return jax.shard_map(per_device, mesh=mesh, in_specs=in_specs, out_specs=P("ctx", "tp"), check_vma=False)
```

```python
import functools

import jax
import jax.numpy as jnp
from jax import lax
from jax.experimental import pallas as pl
from jax.experimental.pallas import tpu as pltpu
from jax.sharding import PartitionSpec as P

F32 = jnp.float32
BF16 = jnp.bfloat16
CHUNKS = 8
LANES = 128
PAIR = 2
VMEM_LIMIT = 40 * 1024 * 1024
VMEM = pl.BlockSpec(memory_space=pltpu.VMEM)
ANY = pl.BlockSpec(memory_space=pl.ANY)

FIRST_PAIR = 10
FIRST_SLICE = 5
GRID = 4
PITCH = 137
SPAN = 136

K_LAST, V_LAST, Q_LAST, K_FIRST, V_FIRST = 0, 2, 4, 6, 8
EXTRA = 16
EDGE = 8


def first_then(first, members, distance):
    return [first] + sorted((i for i in range(members) if i != first), key=lambda i: -distance(i, first))


def around(a, b, size):
    return min((a - b) % size, (b - a) % size)


def pair_order(pairs):
    def distance(a, b):
        return around(a // GRID, b // GRID, max(pairs // GRID, 1)) + 2 * around(a % GRID, b % GRID, GRID)

    return first_then(FIRST_PAIR % pairs, pairs, distance)


def ctx_groups(pairs, slices):
    def index(pair, half, piece):
        return (pair * PAIR + half) * slices + piece

    groups = [[index(p, PAIR - 1, piece) for p in pair_order(pairs)] for piece in range(slices)]
    rest = [(p % GRID, p // GRID // 2, -index(p, 0, piece)) for p in range(pairs) for piece in range(slices)]
    rest = [-i for *_, i in sorted(rest)]
    return groups + [rest[i : i + pairs] for i in range(0, len(rest), pairs)]


def slice_order(slices):
    return first_then(FIRST_SLICE % slices, slices, lambda a, b: 0)


def over_sublanes(row):
    return jnp.broadcast_to(row, (CHUNKS, LANES))


def sublane_index():
    return lax.broadcasted_iota(jnp.int32, (CHUNKS, LANES), 0)


def next_chunk(block, distance=1):
    rolled = pltpu.roll(block, distance, 0)
    return jnp.where(sublane_index() >= distance, rolled, 0.0)


def strided(ref, step, run):
    return ref[pl.ds(step, CHUNKS, stride=run), :]


def added(terms):
    while len(terms) > 1:
        pairs = [terms[i] + terms[i + 1] for i in range(0, len(terms) - 1, 2)]
        terms = pairs + terms[2 * len(pairs) :]
    return terms[0]


def boundary(taps_ref, last, first):
    products = []
    for j in (1, 2):
        tap = [taps_ref[j, i : i + 1, :] for i in range(3)]
        (far, near), (zero, one) = last[j - 1], first[j - 1]
        own = (tap[0] * zero, tap[0] * one + tap[1] * zero)
        gained = (tap[1] * near + tap[2] * far, tap[2] * near)
        products.append((own, gained))
    (k_own, k_gained), (v_own, v_gained) = products
    return [k_own[i] * v_gained[i] + k_gained[i] * (v_own[i] + v_gained[i]) for i in range(2)]


def two_rows(ref, row):
    return ref[row : row + 1, :], ref[row + 1 : row + 2, :]


def pair_boundary(modes, taps_ref, lower_ref, upper_ref):
    last = [two_rows(lower_ref, modes + row) for row in (K_LAST, V_LAST)]
    first = [two_rows(upper_ref, modes + row) for row in (K_FIRST, V_FIRST)]
    return boundary(taps_ref, last, first)


def states_kernel(modes, *refs):
    sources, refs = refs[:6], refs[6:]
    x_hbm = sources[0]
    (rows_ref, product_ref, state_ref, q_ref), refs = refs[:4], refs[4:]
    params, refs = refs[:5], refs[5:]
    taps_ref, decays_ref = params[0], params[1]
    k_half, v_half, k_ref, v_ref, jump_ref, semaphores = refs
    copies = [pltpu.make_async_copy(s, d, semaphores.at[i]) for i, (s, d) in enumerate(zip(sources[1:], params))]
    streams = [
        pltpu.make_async_copy(x_hbm.at[j], d, semaphores.at[5 + j]) for j, d in enumerate((q_ref, k_half, v_half))
    ]
    for copy in (streams[1], streams[2], copies[1], copies[0], streams[0], copies[2], copies[3], copies[4]):
        copy.start()
    positions = q_ref.shape[0]
    run = positions // CHUNKS
    copies[1].wait()
    copies[0].wait()
    k_taps = [over_sublanes(taps_ref[1, i : i + 1, :]) for i in range(3)]
    v_taps = [over_sublanes(taps_ref[2, i : i + 1, :]) for i in range(3)]
    rates = decays_ref[...]
    factor = jnp.exp(-rates)
    factors = [over_sublanes(factor[m : m + 1, :]) for m in range(modes)]
    for i in range(3):
        jump_ref[i] = jnp.exp(-float(run << i) * rates)
    streams[1].wait()
    for s in range(CHUNKS):
        k_ref[s * PITCH : s * PITCH + run, :] = k_half[s * run : (s + 1) * run, :].astype(F32)
    streams[2].wait()
    for s in range(CHUNKS):
        v_ref[s * PITCH : s * PITCH + run, :] = v_half[s * run : (s + 1) * run, :].astype(F32)

    def step(j, carry):
        k1, k2, v1, v2, states = carry
        k0 = strided(k_ref, j, PITCH)
        v0 = strided(v_ref, j, PITCH)
        k = k_taps[0] * k0 + k_taps[1] * k1 + k_taps[2] * k2
        v = v_taps[0] * v0 + v_taps[1] * v1 + v_taps[2] * v2
        product = k * v
        product_ref[j] = product
        states = tuple(a * h + product for a, h in zip(factors, states))
        return k0, k1, v0, v1, states

    start = (
        next_chunk(strided(k_ref, run - 1, PITCH)),
        next_chunk(strided(k_ref, run - 2, PITCH)),
        next_chunk(strided(v_ref, run - 1, PITCH)),
        next_chunk(strided(v_ref, run - 2, PITCH)),
        tuple(jnp.zeros((CHUNKS, LANES), F32) for _ in range(modes)),
    )
    states = lax.fori_loop(0, run, step, start, unroll=16)[4]
    for m in range(modes):
        total = states[m]
        for i in range(3):
            total = total + over_sublanes(jump_ref[i, m : m + 1, :]) * next_chunk(total, 1 << i)
        state_ref[m] = next_chunk(total)
        rows_ref[m : m + 1, :] = total[CHUNKS - 1 : CHUNKS, :]
    streams[0].wait()
    rows_ref[modes + K_LAST : modes + K_LAST + 2, :] = k_ref[7 * PITCH + run - 2 : 7 * PITCH + run, :]
    rows_ref[modes + V_LAST : modes + V_LAST + 2, :] = v_ref[7 * PITCH + run - 2 : 7 * PITCH + run, :]
    rows_ref[modes + Q_LAST : modes + Q_LAST + 2, :] = q_ref[positions - 16 : positions, :].astype(F32)[14:16]
    rows_ref[modes + K_FIRST : modes + K_FIRST + 2, :] = k_ref[0:2, :]
    rows_ref[modes + V_FIRST : modes + V_FIRST + 2, :] = v_ref[0:2, :]
    rows_ref[modes + V_FIRST + 2 :, :] = jnp.zeros((EXTRA - V_FIRST - 2, LANES), F32)
    for i in (2, 3, 4):
        copies[i].wait()


def starts_early(axis):
    pair = lax.axis_index(axis) // PAIR
    y, z = pair // GRID, lax.rem(pair, GRID)
    return jnp.logical_or(z < 1, jnp.logical_and(z < 2, y < 2))


def mode_weights(decays_ref, residues_ref):
    return residues_ref[...] * jnp.sqrt(2.0 * decays_ref[...])


def early_weight(decays_ref, residues_ref):
    return jnp.sum(mode_weights(decays_ref, residues_ref) * jnp.exp(decays_ref[...]), 0, keepdims=True)


def edge_gains(taps_ref, skip_ref, weight, first, second, far, near):
    early = weight * second
    skip = skip_ref[...]
    gate = (taps_ref[0, 1:2, :] * near + taps_ref[0, 2:3, :] * far, taps_ref[0, 2:3, :] * near)
    return gate, (skip * first - early, skip * second)


def from_lower(modes, axis, pair_ref, taps_ref, decays_ref, residues_ref, skip_ref):
    inside = lax.rem(lax.axis_index(axis), PAIR).astype(F32)
    rates = decays_ref[...]
    first, second = (inside * p for p in pair_boundary(modes, taps_ref, pair_ref.at[0], pair_ref.at[1]))
    state = inside * pair_ref[0, :modes, :] + jnp.exp(rates) * first + jnp.exp(2.0 * rates) * second
    far, near = (inside * row for row in two_rows(pair_ref.at[0], modes + Q_LAST))
    weight = early_weight(decays_ref, residues_ref)
    return state, *edge_gains(taps_ref, skip_ref, weight, first, second, far, near)


def at_top(block, row):
    return block + jnp.where(sublane_index() == 0, over_sublanes(row), 0.0)


def fades(decays_ref, run, m):
    return jnp.exp(over_sublanes(decays_ref[m : m + 1, :]) * (sublane_index().astype(F32) * -float(run)))


def load_gate(q_ref, q_half, taps_ref):
    run = q_half.shape[0] // CHUNKS
    for s in range(CHUNKS):
        q_ref[s * PITCH : s * PITCH + run, :] = q_half[s * run : (s + 1) * run, :].astype(F32)
    taps = [over_sublanes(taps_ref[0, i : i + 1, :]) for i in range(3)]
    return taps, [next_chunk(strided(q_ref, run - 1 - i, PITCH)) for i in range(2)]


def split(table):
    return [over_sublanes(table[m : m + 1, :]) for m in range(table.shape[0])]


def local_work(
    modes, axis, q_half, product_ref, state_ref, pair_ref, taps_ref, decays_ref, residues_ref, skip_ref,
    gate_ref, base_ref, begin_ref, reach_ref, q_ref,
):
    run = product_ref.shape[0]
    positions = run * CHUNKS
    inside = lax.rem(lax.axis_index(axis), PAIR).astype(F32)
    rates = decays_ref[...]
    spread = split(mode_weights(decays_ref, residues_ref))
    factors = split(jnp.exp(-rates))
    skip = over_sublanes(skip_ref[...])
    taps, before = load_gate(q_ref, q_half, taps_ref)

    def step(j, carry):
        q1, q2, states = carry
        q0 = strided(q_ref, j, PITCH)
        gate_ref[j] = taps[0] * q0 + taps[1] * q1 + taps[2] * q2
        product = product_ref[j]
        states = tuple(a * h + product for a, h in zip(factors, states))
        base_ref[j] = added([skip * product] + [w * h for w, h in zip(spread, states)])
        return q0, q1, states

    start = (*before, tuple(jnp.zeros((CHUNKS, LANES), F32) for _ in range(modes)))
    lax.fori_loop(0, run, step, start, unroll=4)

    arrived, gate_gain, base_gain = from_lower(modes, axis, pair_ref, taps_ref, decays_ref, residues_ref, skip_ref)
    for j in range(2):
        gate_ref[j] = at_top(gate_ref[j], gate_gain[j])
        base_ref[j] = at_top(base_ref[j], base_gain[j])
    across = jnp.exp(-rates * (inside * float(positions)))
    for m in range(modes):
        fade = fades(decays_ref, run, m)
        begin_ref[m] = spread[m] * (state_ref[m] + fade * over_sublanes(arrived[m : m + 1, :]))
        reach_ref[m] = spread[m] * fade * over_sublanes(across[m : m + 1, :])


def join_kernel(
    modes, axis, own_ref, other_ref, q_half, product_ref, state_ref, taps_ref, decays_ref, residues_ref, skip_ref,
    sent_ref, pair_ref, *refs,
):
    positions = q_half.shape[0]
    below, above = other_ref[...], own_ref[...]
    pair_ref[0] = below
    pair_ref[1] = above
    first, second = pair_boundary(modes, taps_ref, pair_ref.at[0], pair_ref.at[1])
    rates = decays_ref[...]
    state = jnp.exp(-float(positions) * rates) * below[:modes] + above[:modes]
    state = state + jnp.exp(-float(positions - 1) * rates) * first + jnp.exp(-float(positions - 2) * rates) * second
    row = lax.broadcasted_iota(jnp.int32, (EXTRA, LANES), 0)
    beside = jnp.where(row < K_FIRST, above[modes:], below[modes:])
    rows = jnp.concatenate([state, beside], 0).astype(BF16)
    sent_ref[...] = jnp.broadcast_to(rows[None], sent_ref.shape)

    @pl.when(starts_early(axis))
    def _():
        params = (taps_ref, decays_ref, residues_ref, skip_ref)
        local_work(modes, axis, q_half, product_ref, state_ref, pair_ref, *params, *refs)


def enter_kernel(
    modes, axis, received_ref, q_half, product_ref, state_ref, pair_ref, taps_ref, decays_ref, residues_ref, skip_ref, *refs
):
    enter_ref, local_refs, (rows_ref, first_ref, second_ref, q_ref) = refs[0], refs[1:5], refs[5:]
    positions = q_half.shape[0]
    device = lax.axis_index(axis)
    pair = device // PAIR
    upper = lax.rem(device, PAIR) == 1

    @pl.when(jnp.logical_not(jnp.logical_or(upper, starts_early(axis))))
    def _():
        params = (taps_ref, decays_ref, residues_ref, skip_ref)
        local_work(modes, axis, q_half, product_ref, state_ref, pair_ref, *params, *local_refs, q_ref)

    enter_ref[...] = jnp.zeros_like(enter_ref)

    @pl.when(jnp.logical_not(upper))
    def _():
        enter_ref[:modes, :] = jnp.exp(-decays_ref[...])
        enter_ref[modes : modes + 1, :] = early_weight(decays_ref, residues_ref)

    @pl.when(upper)
    def _():
        pairs = received_ref.shape[0]
        pitch = modes + EXTRA
        rows_ref[0:pitch, :] = jnp.zeros((pitch, LANES), F32)
        for slot, e in enumerate(pair_order(pairs)):
            rows_ref[pitch * (e + 1) : pitch * (e + 2), :] = received_ref[slot].astype(F32)

        def of_all(row, block):
            return tuple(rows_ref[pl.ds(pitch * block + modes + row + i, pairs, stride=pitch), :] for i in range(2))

        last = [of_all(row, 0) for row in (K_LAST, V_LAST)]
        begun = [of_all(row, 1) for row in (K_FIRST, V_FIRST)]
        first_ref[...], second_ref[...] = boundary(taps_ref, last, begun)

        rates = decays_ref[...]
        length = PAIR * positions
        across = jnp.exp(-float(length) * rates)
        late_first = jnp.exp(-float(length - 1) * rates)
        late_second = jnp.exp(-float(length - 2) * rates)
        state = jnp.zeros((modes, LANES), F32)
        for e in range(pairs - 1):
            sent = rows_ref[pitch * (e + 1) : pitch * (e + 1) + modes, :]
            sent = sent + late_first * first_ref[e : e + 1, :] + late_second * second_ref[e : e + 1, :]
            state = jnp.where(e < pair, across * state + sent, state)
        first, second = first_ref[pl.ds(pair, 1), :], second_ref[pl.ds(pair, 1), :]
        enter_ref[:modes, :] = state + jnp.exp(rates) * first + jnp.exp(2.0 * rates) * second
        enter_ref[modes : modes + 1, :] = first
        enter_ref[modes + 1 : modes + 2, :] = second
        for i in range(2):
            enter_ref[modes + 2 + i : modes + 3 + i, :] = rows_ref[pl.ds(pair * pitch + modes + Q_LAST + i, 1), :]
        enter_ref[modes + 4 :, :] = jnp.zeros((EDGE - 4, LANES), F32)


def carry_kernel(modes, axis, half, *refs):
    mine = lax.rem(lax.axis_index(axis), PAIR) == half
    if half == 0:
        *refs, power_in_ref, power_ref, gated_ref = refs

        @pl.when(jnp.logical_not(mine))
        def _():
            power_ref[...] = power_in_ref[...]

        refs = (*refs, power_ref, gated_ref)

    @pl.when(mine)
    def _():
        carry_work(modes, axis, half, *refs)


def carry_work(modes, axis, half, enter_ref, *refs):
    early_locals, refs = refs[:4], refs[4:]
    if half:
        (q_half, product_ref, state_ref, pair_ref), refs = refs[:4], refs[4:]
        taps_ref, decays_ref, residues_ref, skip_ref, power_ref, gated_ref, q_ref = refs
    else:
        (table_ref, *locals_), refs = refs[:5], refs[5:]
        taps_ref, decays_ref, residues_ref, skip_ref, power_ref, gated_ref = refs
    run = early_locals[0].shape[0]
    positions = run * CHUNKS
    rates = decays_ref[...]
    state = enter_ref[:modes, :]
    if half:
        weights = mode_weights(decays_ref, residues_ref)
        edges = from_lower(modes, axis, pair_ref, taps_ref, decays_ref, residues_ref, skip_ref)
        factors = split(jnp.exp(-rates))
    else:
        edge = (enter_ref[modes + i : modes + i + 1, :] for i in range(4))
        gains = edge_gains(taps_ref, skip_ref, table_ref[modes : modes + 1, :], *edge)
        factors = split(table_ref[:modes, :])

    def put(j, gate, base, terms, more):
        if more is not None:
            gate, base = at_top(gate, more[0]), at_top(base, more[1])
        gated_ref[pl.ds(j, CHUNKS, stride=SPAN), :] = gate * added([base] + terms)

    def over_steps(step, held, gains, unroll):
        for j in range(2):
            held = step(j, held, gains and (gains[0][j], gains[1][j]))
        lax.fori_loop(2, run, lambda j, held: step(j, held, None), held, unroll=unroll)

    early = starts_early(axis)

    def from_local(gate_ref, base_ref, begin_ref, reach_ref):
        def step(j, carried, more):
            carried = tuple(a * g for a, g in zip(factors, carried))
            put(j, gate_ref[j], base_ref[j], list(carried), more)
            return carried

        carried = tuple(begin_ref[m] + reach_ref[m] * over_sublanes(state[m : m + 1, :]) for m in range(modes))
        over_steps(step, carried, None if half else gains, 42)

    @pl.when(early)
    def _():
        from_local(*early_locals)

    @pl.when(jnp.logical_not(early))
    def _():
        if not half:
            from_local(*locals_)
            return
        taps, before = load_gate(q_ref, q_half, taps_ref)
        skip = over_sublanes(skip_ref[...])
        spread = split(weights)
        arrived, *more_gains = edges
        arrived = arrived + jnp.exp(-rates * float(positions)) * state
        states = tuple(
            state_ref[m] + fades(decays_ref, run, m) * over_sublanes(arrived[m : m + 1, :]) for m in range(modes)
        )

        def step(j, held, more):
            q1, q2, states = held
            q0 = strided(q_ref, j, PITCH)
            product = product_ref[j]
            states = tuple(a * h + product for a, h in zip(factors, states))
            gate = taps[0] * q0 + taps[1] * q1 + taps[2] * q2
            put(j, gate, skip * product, [w * h for w, h in zip(spread, states)], more)
            return q0, q1, states

        over_steps(step, (*before, states), more_gains, 6)

    ones = jnp.ones((LANES, LANES), BF16)
    lane = lax.broadcasted_iota(jnp.int32, (CHUNKS, LANES), 1)
    power = jnp.zeros((CHUNKS, LANES), F32)
    tiles = run // CHUNKS
    for s in range(CHUNKS):
        gated = gated_ref[s * SPAN : s * SPAN + run, :]
        square = gated * gated
        sums = jnp.dot(square.astype(BF16), ones, preferred_element_type=F32)
        for i in range(tiles):
            power = jnp.where(lane == s * tiles + i, sums[i * CHUNKS : (i + 1) * CHUNKS, :], power)
    power_ref[...] = jnp.broadcast_to(power[None], power_ref.shape)


def finish_kernel(channels, axis, power_ref, upper_ref, lower_ref, gain_ref, mixed_ref):
    run = mixed_ref.shape[0] // CHUNKS
    tiles = run // CHUNKS
    inverse = lax.rsqrt(jnp.sum(power_ref[...], 0) / channels + 1e-05)
    gain = over_sublanes(gain_ref[...])

    def scale(gated_ref):
        for s in range(CHUNKS):
            for i in range(0, tiles, 2):
                halves = []
                for h in (i, i + 1):
                    gated = gated_ref[s * SPAN + h * CHUNKS : s * SPAN + (h + 1) * CHUNKS, :]
                    halves.append(gated * gain * inverse[:, s * tiles + h : s * tiles + h + 1])
                rows = slice(s * run + i * CHUNKS, s * run + (i + 2) * CHUNKS)
                mixed_ref[rows, :] = jnp.concatenate(halves, 0).astype(BF16)

    for half, ref in enumerate((lower_ref, upper_ref)):
        pl.when(lax.rem(lax.axis_index(axis), PAIR) == half)(functools.partial(scale, ref))


def per_device(projections, short_filter, residues, decays, skip, gain):
    positions, _, width = projections.shape
    modes = decays.shape[0]
    ctx_count = lax.axis_size("ctx")
    tp_count = lax.axis_size("tp")
    pairs = ctx_count // PAIR
    run = positions // CHUNKS
    x = jnp.swapaxes(projections, 0, 1)

    def shape(*extent, kind=F32):
        return jax.ShapeDtypeStruct(extent, kind)

    def call(kernel, name, out_shape, in_specs, scratch, *operands):
        return pl.pallas_call(
            kernel,
            out_shape=out_shape,
            in_specs=in_specs,
            out_specs=jax.tree.map(lambda _: VMEM, out_shape),
            scratch_shapes=scratch,
            compiler_params=pltpu.CompilerParams(vmem_limit_bytes=VMEM_LIMIT),
            name=name,
        )(*operands)

    block = shape(run, CHUNKS, width)
    table = shape(modes, CHUNKS, width)
    sources = (x, short_filter, decays, residues, skip[None, :], gain[None, :])
    rows, product, state, q, short_filter, decays, residues, skip, gain = call(
        functools.partial(states_kernel, modes),
        "states",
        (shape(modes + EXTRA, width), block, table, shape(positions, width, kind=BF16))
        + tuple(shape(*s.shape) for s in sources[1:]),
        [ANY] * 6,
        [
            pltpu.VMEM((positions, width), BF16),
            pltpu.VMEM((positions, width), BF16),
            pltpu.VMEM((PITCH * (CHUNKS + 1), width), F32),
            pltpu.VMEM((PITCH * (CHUNKS + 1), width), F32),
            pltpu.VMEM((3, modes, width), F32),
            pltpu.SemaphoreType.DMA((8,)),
        ],
        *[pltpu.with_memory_space_constraint(s, pltpu.HBM) for s in sources],
    )
    partners = [(i, i + 1 - 2 * (i % PAIR)) for i in range(ctx_count)]
    other = lax.ppermute(rows, "ctx", partners)
    params = (short_filter, decays, residues, skip)
    pitched = pltpu.VMEM((PITCH * (CHUNKS + 1), width), F32)
    sent, joined, *early_locals = call(
        functools.partial(join_kernel, modes, "ctx"),
        "join",
        (shape(pairs, modes + EXTRA, width, kind=BF16), shape(PAIR, modes + EXTRA, width), block, block, table, table),
        [VMEM] * 9,
        [pitched],
        rows,
        other,
        q,
        product,
        state,
        *params,
    )
    received = lax.all_to_all(
        sent, ("ctx", "tp"), split_axis=0, concat_axis=0, tiled=True, axis_index_groups=ctx_groups(pairs, tp_count)
    )
    enter_shape = shape(modes + EDGE, width)
    local_shapes = (block, block, table, table)
    enter, *locals_ = call(
        functools.partial(enter_kernel, modes, "ctx"),
        "enter",
        (enter_shape, *local_shapes),
        [VMEM] * 9,
        [
            pltpu.VMEM(((pairs + 2) * (modes + EXTRA), width), F32),
            pltpu.VMEM((pairs, width), F32),
            pltpu.VMEM((pairs, width), F32),
            pitched,
        ],
        received,
        q,
        product,
        state,
        joined,
        *params,
    )
    entered = lax.ppermute(enter, "ctx", partners)
    carry_shapes = (shape(tp_count, CHUNKS, run), shape(SPAN * (CHUNKS + 1), width))
    power, upper_gated = call(
        functools.partial(carry_kernel, modes, "ctx", 1),
        "upper",
        carry_shapes,
        [VMEM] * 13,
        [pitched],
        enter,
        *early_locals,
        q,
        product,
        state,
        joined,
        *params,
    )
    power, lower_gated = call(
        functools.partial(carry_kernel, modes, "ctx", 0),
        "lower",
        carry_shapes,
        [VMEM] * 15,
        [],
        entered,
        *early_locals,
        enter,
        *locals_,
        *params,
        power,
    )
    powers = lax.all_to_all(
        power, "tp", split_axis=0, concat_axis=0, tiled=True, axis_index_groups=[slice_order(tp_count)]
    )
    return call(
        functools.partial(finish_kernel, width * tp_count, "ctx"),
        "finish",
        shape(positions, width, kind=BF16),
        [VMEM] * 4,
        [],
        powers,
        upper_gated,
        lower_gated,
        gain,
    )


def solution(mesh):
    in_specs = (
        P("ctx", None, "tp"),
        P(None, None, "tp"),
        P(None, "tp"),
        P(None, "tp"),
        P("tp"),
        P("tp"),
    )
    return jax.shard_map(per_device, mesh=mesh, in_specs=in_specs, out_specs=P("ctx", "tp"), check_vma=False)
```

```python
import functools

import jax
import jax.numpy as jnp
from jax import lax
from jax.experimental import pallas as pl
from jax.experimental.pallas import tpu as pltpu
from jax.sharding import PartitionSpec as P

F32 = jnp.float32
BF16 = jnp.bfloat16
CHUNKS = 8
LANES = 128
PAIR = 2
VMEM_LIMIT = 40 * 1024 * 1024
VMEM = pl.BlockSpec(memory_space=pltpu.VMEM)
ANY = pl.BlockSpec(memory_space=pl.ANY)

FIRST_PAIR = 10
FIRST_SLICE = 5
GRID = 4
PITCH = 137
SPAN = 136

K_LAST, V_LAST, Q_LAST, K_FIRST, V_FIRST = 0, 2, 4, 6, 8
EXTRA = 16
EDGE = 8


def first_then(first, members, distance):
    return [first] + sorted((i for i in range(members) if i != first), key=lambda i: -distance(i, first))


def around(a, b, size):
    return min((a - b) % size, (b - a) % size)


def pair_order(pairs):
    def distance(a, b):
        return around(a // GRID, b // GRID, max(pairs // GRID, 1)) + 2 * around(a % GRID, b % GRID, GRID)

    return first_then(FIRST_PAIR % pairs, pairs, distance)


def ctx_groups(pairs, slices):
    def index(pair, half, piece):
        return (pair * PAIR + half) * slices + piece

    groups = [[index(p, PAIR - 1, piece) for p in pair_order(pairs)] for piece in range(slices)]
    rest = [(p % GRID, p // GRID // 2, -index(p, 0, piece)) for p in range(pairs) for piece in range(slices)]
    rest = [-i for *_, i in sorted(rest)]
    return groups + [rest[i : i + pairs] for i in range(0, len(rest), pairs)]


def slice_order(slices):
    return first_then(FIRST_SLICE % slices, slices, lambda a, b: 0)


def over_sublanes(row):
    return jnp.broadcast_to(row, (CHUNKS, LANES))


def sublane_index():
    return lax.broadcasted_iota(jnp.int32, (CHUNKS, LANES), 0)


def next_chunk(block, distance=1):
    rolled = pltpu.roll(block, distance, 0)
    return jnp.where(sublane_index() >= distance, rolled, 0.0)


def strided(ref, step, run):
    return ref[pl.ds(step, CHUNKS, stride=run), :]


def added(terms):
    while len(terms) > 1:
        pairs = [terms[i] + terms[i + 1] for i in range(0, len(terms) - 1, 2)]
        terms = pairs + terms[2 * len(pairs) :]
    return terms[0]


def boundary(taps_ref, last, first):
    products = []
    for j in (1, 2):
        tap = [taps_ref[j, i : i + 1, :] for i in range(3)]
        (far, near), (zero, one) = last[j - 1], first[j - 1]
        own = (tap[0] * zero, tap[0] * one + tap[1] * zero)
        gained = (tap[1] * near + tap[2] * far, tap[2] * near)
        products.append((own, gained))
    (k_own, k_gained), (v_own, v_gained) = products
    return [k_own[i] * v_gained[i] + k_gained[i] * (v_own[i] + v_gained[i]) for i in range(2)]


def two_rows(ref, row):
    return ref[row : row + 1, :], ref[row + 1 : row + 2, :]


def pair_boundary(modes, taps_ref, lower_ref, upper_ref):
    last = [two_rows(lower_ref, modes + row) for row in (K_LAST, V_LAST)]
    first = [two_rows(upper_ref, modes + row) for row in (K_FIRST, V_FIRST)]
    return boundary(taps_ref, last, first)


def states_kernel(modes, *refs):
    sources, refs = refs[:6], refs[6:]
    x_hbm = sources[0]
    (rows_ref, product_ref, state_ref, q_ref), refs = refs[:4], refs[4:]
    params, refs = refs[:5], refs[5:]
    taps_ref, decays_ref = params[0], params[1]
    k_half, v_half, k_ref, v_ref, jump_ref, semaphores = refs
    copies = [pltpu.make_async_copy(s, d, semaphores.at[i]) for i, (s, d) in enumerate(zip(sources[1:], params))]
    streams = [
        pltpu.make_async_copy(x_hbm.at[j], d, semaphores.at[5 + j]) for j, d in enumerate((q_ref, k_half, v_half))
    ]
    for copy in (streams[1], streams[2], copies[1], copies[0], streams[0], copies[2], copies[3], copies[4]):
        copy.start()
    positions = q_ref.shape[0]
    run = positions // CHUNKS
    copies[1].wait()
    copies[0].wait()
    k_taps = [over_sublanes(taps_ref[1, i : i + 1, :]) for i in range(3)]
    v_taps = [over_sublanes(taps_ref[2, i : i + 1, :]) for i in range(3)]
    rates = decays_ref[...]
    factor = jnp.exp(-rates)
    factors = [over_sublanes(factor[m : m + 1, :]) for m in range(modes)]
    for i in range(3):
        jump_ref[i] = jnp.exp(-float(run << i) * rates)
    streams[1].wait()
    for s in range(CHUNKS):
        k_ref[s * PITCH : s * PITCH + run, :] = k_half[s * run : (s + 1) * run, :].astype(F32)
    streams[2].wait()
    for s in range(CHUNKS):
        v_ref[s * PITCH : s * PITCH + run, :] = v_half[s * run : (s + 1) * run, :].astype(F32)

    def step(j, carry):
        k1, k2, v1, v2, states = carry
        k0 = strided(k_ref, j, PITCH)
        v0 = strided(v_ref, j, PITCH)
        k = k_taps[0] * k0 + k_taps[1] * k1 + k_taps[2] * k2
        v = v_taps[0] * v0 + v_taps[1] * v1 + v_taps[2] * v2
        product = k * v
        product_ref[j] = product
        states = tuple(a * h + product for a, h in zip(factors, states))
        return k0, k1, v0, v1, states

    start = (
        next_chunk(strided(k_ref, run - 1, PITCH)),
        next_chunk(strided(k_ref, run - 2, PITCH)),
        next_chunk(strided(v_ref, run - 1, PITCH)),
        next_chunk(strided(v_ref, run - 2, PITCH)),
        tuple(jnp.zeros((CHUNKS, LANES), F32) for _ in range(modes)),
    )
    states = lax.fori_loop(0, run, step, start, unroll=16)[4]
    for m in range(modes):
        total = states[m]
        for i in range(3):
            total = total + over_sublanes(jump_ref[i, m : m + 1, :]) * next_chunk(total, 1 << i)
        state_ref[m] = next_chunk(total)
        rows_ref[m : m + 1, :] = total[CHUNKS - 1 : CHUNKS, :]
    streams[0].wait()
    rows_ref[modes + K_LAST : modes + K_LAST + 2, :] = k_ref[7 * PITCH + run - 2 : 7 * PITCH + run, :]
    rows_ref[modes + V_LAST : modes + V_LAST + 2, :] = v_ref[7 * PITCH + run - 2 : 7 * PITCH + run, :]
    rows_ref[modes + Q_LAST : modes + Q_LAST + 2, :] = q_ref[positions - 16 : positions, :].astype(F32)[14:16]
    rows_ref[modes + K_FIRST : modes + K_FIRST + 2, :] = k_ref[0:2, :]
    rows_ref[modes + V_FIRST : modes + V_FIRST + 2, :] = v_ref[0:2, :]
    rows_ref[modes + V_FIRST + 2 :, :] = jnp.zeros((EXTRA - V_FIRST - 2, LANES), F32)
    for i in (2, 3, 4):
        copies[i].wait()


def starts_early(axis):
    pair = lax.axis_index(axis) // PAIR
    y, z = pair // GRID, lax.rem(pair, GRID)
    return jnp.logical_or(z < 1, jnp.logical_and(z < 2, y < 2))


def mode_weights(decays_ref, residues_ref):
    return residues_ref[...] * jnp.sqrt(2.0 * decays_ref[...])


def edge_gains(taps_ref, skip_ref, rates, weights, first, second, far, near):
    early = jnp.sum(weights * jnp.exp(rates), 0, keepdims=True) * second
    skip = skip_ref[...]
    gate = (taps_ref[0, 1:2, :] * near + taps_ref[0, 2:3, :] * far, taps_ref[0, 2:3, :] * near)
    return gate, (skip * first - early, skip * second)


def from_lower(modes, axis, pair_ref, taps_ref, decays_ref, residues_ref, skip_ref):
    inside = lax.rem(lax.axis_index(axis), PAIR).astype(F32)
    rates = decays_ref[...]
    first, second = (inside * p for p in pair_boundary(modes, taps_ref, pair_ref.at[0], pair_ref.at[1]))
    state = inside * pair_ref[0, :modes, :] + jnp.exp(rates) * first + jnp.exp(2.0 * rates) * second
    far, near = (inside * row for row in two_rows(pair_ref.at[0], modes + Q_LAST))
    weights = mode_weights(decays_ref, residues_ref)
    return state, *edge_gains(taps_ref, skip_ref, rates, weights, first, second, far, near)


def at_top(block, row):
    return block + jnp.where(sublane_index() == 0, over_sublanes(row), 0.0)


def fades(decays_ref, run, m):
    return jnp.exp(over_sublanes(decays_ref[m : m + 1, :]) * (sublane_index().astype(F32) * -float(run)))


def load_gate(q_ref, q_half, taps_ref):
    run = q_half.shape[0] // CHUNKS
    for s in range(CHUNKS):
        q_ref[s * PITCH : s * PITCH + run, :] = q_half[s * run : (s + 1) * run, :].astype(F32)
    taps = [over_sublanes(taps_ref[0, i : i + 1, :]) for i in range(3)]
    return taps, [next_chunk(strided(q_ref, run - 1 - i, PITCH)) for i in range(2)]


def split(table):
    return [over_sublanes(table[m : m + 1, :]) for m in range(table.shape[0])]


def local_work(
    modes, axis, q_half, product_ref, state_ref, pair_ref, taps_ref, decays_ref, residues_ref, skip_ref,
    gate_ref, base_ref, begin_ref, reach_ref, q_ref,
):
    run = product_ref.shape[0]
    positions = run * CHUNKS
    inside = lax.rem(lax.axis_index(axis), PAIR).astype(F32)
    rates = decays_ref[...]
    spread = split(mode_weights(decays_ref, residues_ref))
    factors = split(jnp.exp(-rates))
    skip = over_sublanes(skip_ref[...])
    taps, before = load_gate(q_ref, q_half, taps_ref)

    def step(j, carry):
        q1, q2, states = carry
        q0 = strided(q_ref, j, PITCH)
        gate_ref[j] = taps[0] * q0 + taps[1] * q1 + taps[2] * q2
        product = product_ref[j]
        states = tuple(a * h + product for a, h in zip(factors, states))
        base_ref[j] = added([skip * product] + [w * h for w, h in zip(spread, states)])
        return q0, q1, states

    start = (*before, tuple(jnp.zeros((CHUNKS, LANES), F32) for _ in range(modes)))
    lax.fori_loop(0, run, step, start, unroll=4)

    arrived, gate_gain, base_gain = from_lower(modes, axis, pair_ref, taps_ref, decays_ref, residues_ref, skip_ref)
    for j in range(2):
        gate_ref[j] = at_top(gate_ref[j], gate_gain[j])
        base_ref[j] = at_top(base_ref[j], base_gain[j])
    across = jnp.exp(-rates * (inside * float(positions)))
    for m in range(modes):
        fade = fades(decays_ref, run, m)
        begin_ref[m] = spread[m] * (state_ref[m] + fade * over_sublanes(arrived[m : m + 1, :]))
        reach_ref[m] = spread[m] * fade * over_sublanes(across[m : m + 1, :])


def join_kernel(
    modes, axis, own_ref, other_ref, q_half, product_ref, state_ref, taps_ref, decays_ref, residues_ref, skip_ref,
    sent_ref, pair_ref, *refs,
):
    positions = q_half.shape[0]
    below, above = other_ref[...], own_ref[...]
    pair_ref[0] = below
    pair_ref[1] = above
    first, second = pair_boundary(modes, taps_ref, pair_ref.at[0], pair_ref.at[1])
    rates = decays_ref[...]
    state = jnp.exp(-float(positions) * rates) * below[:modes] + above[:modes]
    state = state + jnp.exp(-float(positions - 1) * rates) * first + jnp.exp(-float(positions - 2) * rates) * second
    row = lax.broadcasted_iota(jnp.int32, (EXTRA, LANES), 0)
    beside = jnp.where(row < K_FIRST, above[modes:], below[modes:])
    rows = jnp.concatenate([state, beside], 0).astype(BF16)
    sent_ref[...] = jnp.broadcast_to(rows[None], sent_ref.shape)

    @pl.when(starts_early(axis))
    def _():
        params = (taps_ref, decays_ref, residues_ref, skip_ref)
        local_work(modes, axis, q_half, product_ref, state_ref, pair_ref, *params, *refs)


def enter_kernel(
    modes, axis, received_ref, q_half, product_ref, state_ref, pair_ref, taps_ref, decays_ref, residues_ref, skip_ref, *refs
):
    enter_ref, local_refs, (rows_ref, first_ref, second_ref, q_ref) = refs[0], refs[1:5], refs[5:]
    positions = q_half.shape[0]
    device = lax.axis_index(axis)
    pair = device // PAIR
    upper = lax.rem(device, PAIR) == 1

    @pl.when(jnp.logical_not(jnp.logical_or(upper, starts_early(axis))))
    def _():
        params = (taps_ref, decays_ref, residues_ref, skip_ref)
        local_work(modes, axis, q_half, product_ref, state_ref, pair_ref, *params, *local_refs, q_ref)

    enter_ref[...] = jnp.zeros_like(enter_ref)

    @pl.when(upper)
    def _():
        pairs = received_ref.shape[0]
        pitch = modes + EXTRA
        rows_ref[0:pitch, :] = jnp.zeros((pitch, LANES), F32)
        for slot, e in enumerate(pair_order(pairs)):
            rows_ref[pitch * (e + 1) : pitch * (e + 2), :] = received_ref[slot].astype(F32)

        def of_all(row, block):
            return tuple(rows_ref[pl.ds(pitch * block + modes + row + i, pairs, stride=pitch), :] for i in range(2))

        last = [of_all(row, 0) for row in (K_LAST, V_LAST)]
        begun = [of_all(row, 1) for row in (K_FIRST, V_FIRST)]
        first_ref[...], second_ref[...] = boundary(taps_ref, last, begun)

        rates = decays_ref[...]
        length = PAIR * positions
        across = jnp.exp(-float(length) * rates)
        late_first = jnp.exp(-float(length - 1) * rates)
        late_second = jnp.exp(-float(length - 2) * rates)
        state = jnp.zeros((modes, LANES), F32)
        for e in range(pairs - 1):
            sent = rows_ref[pitch * (e + 1) : pitch * (e + 1) + modes, :]
            sent = sent + late_first * first_ref[e : e + 1, :] + late_second * second_ref[e : e + 1, :]
            state = jnp.where(e < pair, across * state + sent, state)
        first, second = first_ref[pl.ds(pair, 1), :], second_ref[pl.ds(pair, 1), :]
        enter_ref[:modes, :] = state + jnp.exp(rates) * first + jnp.exp(2.0 * rates) * second
        enter_ref[modes : modes + 1, :] = first
        enter_ref[modes + 1 : modes + 2, :] = second
        for i in range(2):
            enter_ref[modes + 2 + i : modes + 3 + i, :] = rows_ref[pl.ds(pair * pitch + modes + Q_LAST + i, 1), :]
        enter_ref[modes + 4 :, :] = jnp.zeros((EDGE - 4, LANES), F32)


def carry_kernel(modes, axis, half, *refs):
    mine = lax.rem(lax.axis_index(axis), PAIR) == half
    if half == 0:
        *refs, power_in_ref, power_ref, gated_ref = refs

        @pl.when(jnp.logical_not(mine))
        def _():
            power_ref[...] = power_in_ref[...]

        refs = (*refs, power_ref, gated_ref)

    @pl.when(mine)
    def _():
        carry_work(modes, axis, half, *refs)


def carry_work(modes, axis, half, enter_ref, *refs):
    early_locals, refs = refs[:4], refs[4:]
    if half:
        (q_half, product_ref, state_ref, pair_ref), refs = refs[:4], refs[4:]
        taps_ref, decays_ref, residues_ref, skip_ref, power_ref, gated_ref, q_ref = refs
    else:
        locals_, refs = refs[:4], refs[4:]
        taps_ref, decays_ref, residues_ref, skip_ref, power_ref, gated_ref = refs
    run = early_locals[0].shape[0]
    positions = run * CHUNKS
    rates = decays_ref[...]
    state = enter_ref[:modes, :]
    weights = mode_weights(decays_ref, residues_ref)
    if half:
        edges = from_lower(modes, axis, pair_ref, taps_ref, decays_ref, residues_ref, skip_ref)
    else:
        edge = (enter_ref[modes + i : modes + i + 1, :] for i in range(4))
        gains = edge_gains(taps_ref, skip_ref, rates, weights, *edge)
    factors = split(jnp.exp(-rates))

    def put(j, gate, base, terms, more):
        if more is not None:
            gate, base = at_top(gate, more[0]), at_top(base, more[1])
        gated_ref[pl.ds(j, CHUNKS, stride=SPAN), :] = gate * added([base] + terms)

    def over_steps(step, held, gains, unroll):
        for j in range(2):
            held = step(j, held, gains and (gains[0][j], gains[1][j]))
        lax.fori_loop(2, run, lambda j, held: step(j, held, None), held, unroll=unroll)

    early = starts_early(axis)

    def from_local(gate_ref, base_ref, begin_ref, reach_ref):
        def step(j, carried, more):
            carried = tuple(a * g for a, g in zip(factors, carried))
            put(j, gate_ref[j], base_ref[j], list(carried), more)
            return carried

        carried = tuple(begin_ref[m] + reach_ref[m] * over_sublanes(state[m : m + 1, :]) for m in range(modes))
        over_steps(step, carried, None if half else gains, 42)

    @pl.when(early)
    def _():
        from_local(*early_locals)

    @pl.when(jnp.logical_not(early))
    def _():
        if not half:
            from_local(*locals_)
            return
        taps, before = load_gate(q_ref, q_half, taps_ref)
        skip = over_sublanes(skip_ref[...])
        spread = split(weights)
        arrived, *more_gains = edges
        arrived = arrived + jnp.exp(-rates * float(positions)) * state
        states = tuple(
            state_ref[m] + fades(decays_ref, run, m) * over_sublanes(arrived[m : m + 1, :]) for m in range(modes)
        )

        def step(j, held, more):
            q1, q2, states = held
            q0 = strided(q_ref, j, PITCH)
            product = product_ref[j]
            states = tuple(a * h + product for a, h in zip(factors, states))
            gate = taps[0] * q0 + taps[1] * q1 + taps[2] * q2
            put(j, gate, skip * product, [w * h for w, h in zip(spread, states)], more)
            return q0, q1, states

        over_steps(step, (*before, states), more_gains, 6)

    ones = jnp.ones((LANES, LANES), BF16)
    lane = lax.broadcasted_iota(jnp.int32, (CHUNKS, LANES), 1)
    power = jnp.zeros((CHUNKS, LANES), F32)
    tiles = run // CHUNKS
    for s in range(CHUNKS):
        gated = gated_ref[s * SPAN : s * SPAN + run, :]
        square = gated * gated
        sums = jnp.dot(square.astype(BF16), ones, preferred_element_type=F32)
        for i in range(tiles):
            power = jnp.where(lane == s * tiles + i, sums[i * CHUNKS : (i + 1) * CHUNKS, :], power)
    power_ref[...] = jnp.broadcast_to(power[None], power_ref.shape)


def finish_kernel(channels, axis, power_ref, upper_ref, lower_ref, gain_ref, mixed_hbm, mixed_ref, semaphores):
    run = mixed_ref.shape[0] // CHUNKS
    tiles = run // CHUNKS
    inverse = lax.rsqrt(jnp.sum(power_ref[...], 0) / channels + 1e-05)
    gain = over_sublanes(gain_ref[...])

    def scale(gated_ref):
        copies = []
        for s in range(CHUNKS):
            for i in range(0, tiles, 2):
                halves = []
                for h in (i, i + 1):
                    gated = gated_ref[s * SPAN + h * CHUNKS : s * SPAN + (h + 1) * CHUNKS, :]
                    halves.append(gated * gain * inverse[:, s * tiles + h : s * tiles + h + 1])
                rows = slice(s * run + i * CHUNKS, s * run + (i + 2) * CHUNKS)
                mixed_ref[rows, :] = jnp.concatenate(halves, 0).astype(BF16)
            if s % 2:
                part = pl.ds((s - 1) * run, 2 * run)
                copies.append(pltpu.make_async_copy(mixed_ref.at[part], mixed_hbm.at[part], semaphores.at[s // 2]))
                copies[-1].start()
        for copy in copies:
            copy.wait()

    for half, ref in enumerate((lower_ref, upper_ref)):
        pl.when(lax.rem(lax.axis_index(axis), PAIR) == half)(functools.partial(scale, ref))


def per_device(projections, short_filter, residues, decays, skip, gain):
    positions, _, width = projections.shape
    modes = decays.shape[0]
    ctx_count = lax.axis_size("ctx")
    tp_count = lax.axis_size("tp")
    pairs = ctx_count // PAIR
    run = positions // CHUNKS
    x = jnp.swapaxes(projections, 0, 1)

    def shape(*extent, kind=F32):
        return jax.ShapeDtypeStruct(extent, kind)

    def call(kernel, name, out_shape, in_specs, scratch, *operands, out_specs=None):
        return pl.pallas_call(
            kernel,
            out_shape=out_shape,
            in_specs=in_specs,
            out_specs=out_specs or jax.tree.map(lambda _: VMEM, out_shape),
            scratch_shapes=scratch,
            compiler_params=pltpu.CompilerParams(vmem_limit_bytes=VMEM_LIMIT),
            name=name,
        )(*operands)

    block = shape(run, CHUNKS, width)
    table = shape(modes, CHUNKS, width)
    sources = (x, short_filter, decays, residues, skip[None, :], gain[None, :])
    rows, product, state, q, short_filter, decays, residues, skip, gain = call(
        functools.partial(states_kernel, modes),
        "states",
        (shape(modes + EXTRA, width), block, table, shape(positions, width, kind=BF16))
        + tuple(shape(*s.shape) for s in sources[1:]),
        [ANY] * 6,
        [
            pltpu.VMEM((positions, width), BF16),
            pltpu.VMEM((positions, width), BF16),
            pltpu.VMEM((PITCH * (CHUNKS + 1), width), F32),
            pltpu.VMEM((PITCH * (CHUNKS + 1), width), F32),
            pltpu.VMEM((3, modes, width), F32),
            pltpu.SemaphoreType.DMA((8,)),
        ],
        *[pltpu.with_memory_space_constraint(s, pltpu.HBM) for s in sources],
    )
    partners = [(i, i + 1 - 2 * (i % PAIR)) for i in range(ctx_count)]
    other = lax.ppermute(rows, "ctx", partners)
    params = (short_filter, decays, residues, skip)
    pitched = pltpu.VMEM((PITCH * (CHUNKS + 1), width), F32)
    sent, joined, *early_locals = call(
        functools.partial(join_kernel, modes, "ctx"),
        "join",
        (shape(pairs, modes + EXTRA, width, kind=BF16), shape(PAIR, modes + EXTRA, width), block, block, table, table),
        [VMEM] * 9,
        [pitched],
        rows,
        other,
        q,
        product,
        state,
        *params,
    )
    received = lax.all_to_all(
        sent, ("ctx", "tp"), split_axis=0, concat_axis=0, tiled=True, axis_index_groups=ctx_groups(pairs, tp_count)
    )
    enter_shape = shape(modes + EDGE, width)
    local_shapes = (block, block, table, table)
    enter, *locals_ = call(
        functools.partial(enter_kernel, modes, "ctx"),
        "enter",
        (enter_shape, *local_shapes),
        [VMEM] * 9,
        [
            pltpu.VMEM(((pairs + 2) * (modes + EXTRA), width), F32),
            pltpu.VMEM((pairs, width), F32),
            pltpu.VMEM((pairs, width), F32),
            pitched,
        ],
        received,
        q,
        product,
        state,
        joined,
        *params,
    )
    entered = lax.ppermute(enter, "ctx", partners)
    carry_shapes = (shape(tp_count, CHUNKS, run), shape(SPAN * (CHUNKS + 1), width))
    power, upper_gated = call(
        functools.partial(carry_kernel, modes, "ctx", 1),
        "upper",
        carry_shapes,
        [VMEM] * 13,
        [pitched],
        enter,
        *early_locals,
        q,
        product,
        state,
        joined,
        *params,
    )
    power, lower_gated = call(
        functools.partial(carry_kernel, modes, "ctx", 0),
        "lower",
        carry_shapes,
        [VMEM] * 14,
        [],
        entered,
        *early_locals,
        *locals_,
        *params,
        power,
    )
    powers = lax.all_to_all(
        power, "tp", split_axis=0, concat_axis=0, tiled=True, axis_index_groups=[slice_order(tp_count)]
    )
    return call(
        functools.partial(finish_kernel, width * tp_count, "ctx"),
        "finish",
        shape(positions, width, kind=BF16),
        [VMEM] * 4,
        [pltpu.VMEM((positions, width), BF16), pltpu.SemaphoreType.DMA((CHUNKS // 2,))],
        powers,
        upper_gated,
        lower_gated,
        gain,
        out_specs=ANY,
    )


def solution(mesh):
    in_specs = (
        P("ctx", None, "tp"),
        P(None, None, "tp"),
        P(None, "tp"),
        P(None, "tp"),
        P("tp"),
        P("tp"),
    )
    return jax.shard_map(per_device, mesh=mesh, in_specs=in_specs, out_specs=P("ctx", "tp"), check_vma=False)
```
